32 devices in a mesh: row: 8 (over z, y), col: 4 (over x, core).
Axes of the slice: x: 2, y: 2, z: 4, core: 2. Of those that a mesh axis runs over, the one named last changes fastest.
Arguments:
- tile_values: float32 [4096, 128, 128], P(('row', 'col')), may hold values from -0.15625 to 0.15625
- tile_owner: int32 [4096, 1], P(('row', 'col')), may hold values from 0 to 31; in each aligned block of 128 rows (0 to 127, 128 to 255, ...) at most 8 rows name the same one
- tile_row: int32 [4096], P(('row', 'col')), may hold values from 0 to 23
- tile_col: int32 [4096], P(('row', 'col')), may hold values from 0 to 47
- tile_count: int32 [32], P(('row', 'col')), may hold values from 96 to 128, as said below
- relaxation: float32 [24576], P(('row', 'col')), may hold values from 0.3 to 1
- driving: float32 [24576, 64], P(('row', 'col')), may hold values from 0.2 to 2
- heat_weight: float32 [24576], P(('row', 'col')), may hold values from 0.1 to 3
Outputs:
- mode_flux: float32 [24576, 64], P(('row', 'col'))
- conductivity: float32 [64], replicated
The draws below stay inside these ranges and needn't reach their ends.
Inputs may be any that keep to these rules, and one draw needn't show every extreme that they name: `tile_owner`: owner d stands for row index d // 4 and column index d % 4. Among the 128 slots of one device no owner appears more than 8 times; in some device some owner appears exactly 8 times; every owner appears somewhere. Device d's slots below tile_count[d] are used, the rest are ignored; some device uses all 128.
All inputs are finite; a program needn't handle non-finite values.
Results may differ from the reference program's by a relative error of at most 0.0001.
Values sent between devices are 32-bit elements; how exact they have to be, the bound alone decides.
No kernel may reach another device: no remote copies, remote signals or barrier semaphores. Data moves between devices by JAX's collectives and lax.ppermute only.
A program may use at most 128 MiB of HBM per device.

```python
import math
import jax
import jax.numpy as jnp
import numpy as np
from jax import lax

TILE = 128
TEMPS = 64
ITERS = 3
ROWT_DEV = 24
TILES_DEV = 128
MODES = 24576
COLT_DEV = 48
CAP = 8
N_ROW = 8
N_COL = 4
DEVICES = 32


def draw_tile_count(key, part):
    counts = jax.random.randint(jax.random.fold_in(key, 11), (N_ROW * N_COL,), max(1, 3 * TILES_DEV // 4), TILES_DEV + 1)
    chosen = jax.random.randint(jax.random.fold_in(key, 12), (), 0, N_ROW * N_COL)
    return counts.at[chosen].set(TILES_DEV).astype(jnp.int32)


def touch_ends(result, key, low, high):
    longest = result.shape.index(max(result.shape))
    spots = []
    for shift in (0, 1):
        where = [jax.random.randint(jax.random.fold_in(key, axis), (), 0, length) for axis, length in enumerate(result.shape)]
        where[longest] = (where[longest] + shift) % result.shape[longest]
        spots.append(tuple(where))
    return result.at[spots[0]].set(low).at[spots[1]].set(high)


def block_scale(own_key, extent, pieces, smallest, top_value):
    level, own = 1.0, jax.random.fold_in(own_key, 6)
    for dim, blocks in pieces:
        steps = jnp.exp(jax.random.uniform(jax.random.fold_in(own, dim), (blocks,), jnp.float32, smallest / len(pieces), top_value / len(pieces)))
        level = level * jnp.repeat(steps, extent[dim] // blocks).reshape([-1 if axis == dim else 1 for axis in range(len(extent))])
    return level


def assign_block(rng, own, number, rows, number_of, top, reach, skew):
    order = jax.random.permutation(rng, number_of)
    packed, ordinary = shares(number_of, rows * top, reach, skew, True), shares(number_of, rows * top, reach, skew, False)
    places = jnp.arange(number_of)

    def named(sizes, rotation):
        used = int((sizes > 0).sum())
        fixed = max(1, used // 4)
        shifted = fixed + (places - fixed + rotation * (used - fixed)) % max(1, number_of - fixed)
        return jnp.zeros((number_of,), jnp.int32).at[order[jnp.where(places < fixed, places, shifted)]].set(jnp.asarray(sizes, jnp.int32))

    sizes = jnp.where(number % 4 == 0, named(packed, number // 4), named(ordinary, number - number // 4 - 1))
    mixed = jax.random.permutation(jax.random.fold_in(own, 3), number_of)
    giver, sink = mixed[0:number_of // 2 * 2:2], mixed[1:number_of // 2 * 2:2]
    room = jnp.minimum(sizes[giver] - 1, reach - sizes[sink]) // 2
    room = jnp.where((giver == order[0]) | (sink == order[0]) | (sizes[sink] == 0), 0, jnp.maximum(room, 0))
    shifted = jax.random.randint(jax.random.fold_in(own, 4), (number_of // 2,), 0, 1 << 20) % (room + 1)
    sizes = sizes.at[giver].add(-shifted).at[sink].add(shifted)
    items = jnp.searchsorted(jnp.cumsum(sizes), jnp.arange(rows * top), side="right").astype(jnp.int32)
    listing = items.reshape(top, rows).T
    listing = listing[jax.random.permutation(jax.random.fold_in(own, 1), rows)]
    rotation = jax.random.randint(jax.random.fold_in(own, 2), (rows, 1), 0, top)
    return jnp.take_along_axis(listing, (jnp.arange(top)[None, :] + rotation) % top, axis=1)


def shares(amount, total, most, lean, full):
    loads = [(1 << 20) // math.isqrt(standing ** lean) + 1 for standing in range(1, amount + 1)]
    largest = most if full else min(most, max(-(-total // amount), total * loads[0] // sum(loads)))
    least = 1 if total - largest >= amount - 1 else 0
    holding, spare = [largest] + [least] * (amount - 1), total - largest - least * (amount - 1)
    while spare > 0:
        candidates = [i for i in range(1, amount) if holding[i] < largest] or [i for i in range(1, amount) if holding[i] < most]
        pool, budget = sum([loads[i] for i in candidates]), spare
        for i in candidates:
            extra = min(most - holding[i], max(1, budget * loads[i] // pool), spare)
            holding[i] = holding[i] + extra
            spare = spare - extra
    return np.array(holding)


def centred(key, extent, width, limit, split=(), held_as=jnp.bfloat16):
    array = width * jax.random.normal(key, extent, jnp.float32)
    if split:
        array = array * block_scale(key, extent, split, -0.22, 0.18)
    return jnp.clip(array, -limit, limit).astype(held_as)


def setup_inputs(seed: int = 0) -> dict:
    key_list = jax.random.split(jax.random.key(seed), 9)
    tile_values = centred(key_list[0], (DEVICES * TILES_DEV, TILE, TILE), (0.6 / (TILE * DEVICES * TILES_DEV // (ROWT_DEV * N_ROW)) ** 0.5), 0.15625, ((0, 32),), jnp.float32)
    tile_owner_keys = jax.random.split(jax.random.fold_in(key_list[1], 1), (DEVICES * TILES_DEV) // TILES_DEV)
    tile_owner_turns = jax.random.permutation(jax.random.fold_in(key_list[1], 3), (DEVICES * TILES_DEV) // TILES_DEV)
    tile_owner = jax.vmap(lambda own, number: assign_block(jax.random.fold_in(key_list[1], 2), own, number, TILES_DEV, DEVICES, 1, CAP, 2))(tile_owner_keys, tile_owner_turns).reshape((DEVICES * TILES_DEV, 1))
    tile_row = touch_ends(jax.random.randint(key_list[2], (DEVICES * TILES_DEV,), 0, ROWT_DEV), jax.random.fold_in(key_list[2], 1), 0, ROWT_DEV - 1).astype(jnp.int32)
    tile_col = touch_ends(jax.random.randint(key_list[3], (DEVICES * TILES_DEV,), 0, COLT_DEV), jax.random.fold_in(key_list[3], 1), 0, COLT_DEV - 1).astype(jnp.int32)
    tile_count = draw_tile_count(jax.random.fold_in(key_list[8], 71), 0)
    relaxation = jnp.clip(jnp.exp(math.log(1.0) - 1.2039728 * jax.random.uniform(key_list[5], (MODES,), jnp.float32) ** block_scale(key_list[5], (MODES,), ((0, 32),), -0.2, 0.2)), 0.3, 1.0)
    driving = jnp.clip(0.2 + 1.8 * jax.random.uniform(key_list[6], (MODES, TEMPS), jnp.float32) ** block_scale(key_list[6], (MODES, TEMPS), ((0, 32),), -0.2, 0.2), 0.2, 2.0)
    heat_weight = jnp.clip(jnp.exp(math.log(3.0) - 3.4011974 * jax.random.uniform(key_list[7], (MODES,), jnp.float32) ** block_scale(key_list[7], (MODES,), ((0, 32),), -0.2, 0.2)), 0.1, 3.0)
    return dict(tile_values=tile_values, tile_owner=tile_owner, tile_row=tile_row, tile_col=tile_col, tile_count=tile_count, relaxation=relaxation, driving=driving, heat_weight=heat_weight)


def reference(tile_values, tile_owner, tile_row, tile_col, tile_count, relaxation, driving, heat_weight):
    devices = N_ROW * N_COL
    per_device = TILES_DEV
    per_group = ROWT_DEV // N_COL
    owners = tile_owner[:, 0]
    slots = jnp.arange(devices * per_device, dtype=jnp.int32)
    is_used = (slots % per_device) < tile_count[slots // per_device]
    grow = (owners // N_COL) * ROWT_DEV + tile_row
    gcol = ((tile_col // per_group) * N_COL + owners % N_COL) * per_group + tile_col % per_group
    weights = jnp.where(is_used[:, None, None], tile_values, jnp.zeros_like(tile_values)).astype(jnp.float32)
    num_tiles = MODES // TILE

    def apply_matrix(flux_now):
        tiled = flux_now.reshape(num_tiles, TILE, TEMPS)

        def step_one(accum, item):
            weight_block, rows_idx, cols_idx = item
            product = jnp.einsum("sij,sjk->sik", weight_block, tiled[cols_idx], precision=lax.Precision.HIGHEST)
            return accum.at[rows_idx].add(product), None

        start_acc = jnp.zeros((num_tiles, TILE, TEMPS), jnp.float32)
        accum, _ = lax.scan(step_one, start_acc, (weights.reshape(devices, per_device, TILE, TILE), grow.reshape(devices, per_device), gcol.reshape(devices, per_device)))
        return accum.reshape(MODES, TEMPS)

    mode_flux = relaxation[:, None] * driving
    for sweep in range(ITERS):
        mode_flux = relaxation[:, None] * (driving + apply_matrix(mode_flux))
    conductivity = jnp.sum(heat_weight[:, None] * mode_flux, axis=0) / jnp.sum(heat_weight)
    return mode_flux, conductivity
```

```python
import functools

import jax
import jax.numpy as jnp
from jax import lax
from jax.experimental import pallas as pl
from jax.experimental.pallas import tpu as pltpu
from jax.sharding import Mesh
from jax.sharding import PartitionSpec as P

ITERS = 3
CORES = 2
STEP = 16
UNROLL = 8
CHIPS = ("row", "x")
ALL = ("row", "x", "core")
DIMS = (((1,), (1,)), ((), ()))


def apply_kernel(length, row_ref, col_ref, used_ref, flux_ref, own_ref, other_ref, out_ref):
    step = pl.program_id(0)

    @pl.when(step == 0)
    def _():
        out_ref[...] = jnp.zeros_like(out_ref)

    def add_tile(tile, slot):
        flux = flux_ref[col_ref[slot]] * used_ref[slot]
        tile_high = tile.astype(jnp.bfloat16)
        tile_low = (tile - tile_high.astype(jnp.float32)).astype(jnp.bfloat16)
        flux_high = flux.astype(jnp.bfloat16)
        flux_low = (flux - flux_high.astype(jnp.float32)).astype(jnp.bfloat16)
        both = lax.dot_general(
            jnp.concatenate([flux_high, flux_low], axis=0),
            tile_high,
            DIMS,
            preferred_element_type=jnp.float32,
        )
        low = lax.dot_general(flux_high, tile_low, DIMS, preferred_element_type=jnp.float32)
        temps = flux.shape[0]
        out_ref[row_ref[slot]] += both[:temps] + (both[temps:] + low)

    for part, ref in enumerate((own_ref, other_ref)):
        base = part * length + step * STEP

        @pl.loop(0, STEP // UNROLL)
        def _(group):
            for k in range(UNROLL):
                add_tile(ref[group * UNROLL + k], base + group * UNROLL + k)


def apply_tiles(row, col, used, flux, own, other):
    length, size, _ = own.shape
    num, temps, _ = flux.shape
    whole = pl.BlockSpec((num, temps, size), lambda i, *_: (0, 0, 0))
    some = pl.BlockSpec((STEP, size, size), lambda i, *_: (i, 0, 0))
    return pl.pallas_call(
        functools.partial(apply_kernel, length),
        out_shape=jax.ShapeDtypeStruct(flux.shape, jnp.float32),
        grid_spec=pltpu.PrefetchScalarGridSpec(
            num_scalar_prefetch=3,
            grid=(length // STEP,),
            in_specs=[whole, some, some],
            out_specs=whole,
        ),
        compiler_params=pltpu.CompilerParams(vmem_limit_bytes=40 * 1024 * 1024),
        cost_estimate=pl.CostEstimate(
            flops=2 * 2 * length * size * size * temps * 3,
            bytes_accessed=4 * (2 * length * size * size + 2 * num * temps * size),
            transcendentals=0,
        ),
    )(row, col, used, flux, own, other)


def shards(
    tile_values, tile_owner, tile_row, tile_col, tile_count, relaxation, driving, heat_weight
):
    n_cols = lax.axis_size("x") * CORES
    n_rows = lax.axis_size("row")
    length, size, _ = tile_values.shape
    modes, columns = driving.shape
    per = modes // size
    num = n_rows * n_cols * per
    half = columns // CORES
    core = lax.axis_index("core")
    swap = [(0, 1), (1, 0)]

    other_values = lax.ppermute(tile_values, "core", swap)
    owners = tile_owner[:, 0]
    row = (owners // n_cols) * (n_cols * per) + tile_row
    col = ((tile_col // per) * n_cols + owners % n_cols) * per + tile_col % per
    used = jnp.arange(length, dtype=jnp.int32) < tile_count[0]
    places = jnp.where(used, row * num + col, -1)
    places = jnp.concatenate([places, lax.ppermute(places, "core", swap)])
    is_used = places >= 0
    places = jnp.where(is_used, places, 0)
    row, col, used = places // num, places % num, is_used.astype(jnp.float32)

    def by_core(own, other):
        return jnp.concatenate(
            [jnp.where(core == 0, own, other), jnp.where(core == 0, other, own)], axis=0
        )

    drive = jnp.transpose(driving.reshape(per, size, columns), (0, 2, 1))
    relax = relaxation.reshape(per, 1, size)
    low, high = drive[:, :half], drive[:, half:]
    mine = jnp.where(core == 0, low, high)
    theirs = jnp.where(core == 0, high, low)
    packed = jnp.concatenate([theirs, jnp.broadcast_to(relax, (per, 8, size))], axis=1)
    got = lax.ppermute(packed, "core", swap)
    drive_half = by_core(mine, got[:, :half])
    relax_both = by_core(relax, got[:, half : half + 1])

    flux = relax_both * drive_half
    for sweep in range(ITERS):
        panel = lax.all_gather(flux, CHIPS, axis=0, tiled=True)
        partial_sum = apply_tiles(row, col, used, panel, tile_values, other_values)
        summed = lax.psum_scatter(partial_sum, CHIPS, scatter_dimension=0, tiled=True)
        flux = relax_both * (drive_half + summed)
    first, second = flux[:per], flux[per:]
    mine = jnp.where(core == 0, first, second)
    got = lax.ppermute(jnp.where(core == 0, second, first), "core", swap)
    both = jnp.concatenate(
        [jnp.where(core == 0, mine, got), jnp.where(core == 0, got, mine)], axis=1
    )
    mode_flux = jnp.transpose(both, (0, 2, 1)).reshape(modes, columns)
    weighted_local = jnp.sum(heat_weight[:, None] * mode_flux, axis=0)
    weighted, weight_sum = lax.psum((weighted_local, jnp.sum(heat_weight)), ALL)
    return (mode_flux, weighted / weight_sum)


def solution(mesh):
    n_rows, n_cols = mesh.shape["row"], mesh.shape["col"]
    chips = Mesh(mesh.devices.reshape(n_rows, n_cols // CORES, CORES), ALL)
    placed = (
        P(ALL, None, None),
        P(ALL, None),
        P(ALL),
        P(ALL),
        P(ALL),
        P(ALL),
        P(ALL, None),
        P(ALL),
    )
    return jax.shard_map(
        shards,
        mesh=chips,
        in_specs=placed,
        out_specs=(P(ALL, None), P()),
        check_vma=False,
    )
```

```python
import functools

import jax
import jax.numpy as jnp
from jax import lax
from jax.experimental import pallas as pl
from jax.experimental.pallas import tpu as pltpu
from jax.sharding import Mesh
from jax.sharding import PartitionSpec as P

ITERS = 3
CORES = 2
STEP = 16
UNROLL = 8
CHIPS = ("row", "x")
ALL = ("row", "x", "core")
DIMS = (((1,), (1,)), ((), ()))
ORDERS = (("z", "x", "y"), ("z", "y", "x"), ("x", "y", "z"))


def sizes_of(n_rows, n_x):
    y = max(n for n in range(1, n_rows + 1) if n_rows % n == 0 and n * n <= n_rows)
    return {"z": n_rows // y, "y": y, "x": n_x}


def chip_of(sizes, z, y, x):
    return (z * sizes["y"] + y) * sizes["x"] + x


def shift(sizes, array, axis, by):
    pairs = []
    for z in range(sizes["z"]):
        for y in range(sizes["y"]):
            for x in range(sizes["x"]):
                at = {"z": z, "y": y, "x": x}
                to = dict(at, **{axis: (at[axis] + by) % sizes[axis]})
                pairs.append((chip_of(sizes, **at), chip_of(sizes, **to)))
    return lax.ppermute(array, CHIPS, pairs)


def gather(sizes, block, order):
    for axis in order[:-1]:
        block = jnp.concatenate(
            [block] + [shift(sizes, block, axis, j) for j in range(1, sizes[axis])], axis=0
        )
    axis = order[-1]
    return [block] + [shift(sizes, block, axis, j) for j in range(1, sizes[axis])]


def reduce(sizes, pieces, order):
    for place in range(len(order) - 1, -1, -1):
        axis = order[place]
        got = [shift(sizes, pieces[j], axis, j) for j in range(1, sizes[axis])]
        if place == 0:
            return sum(got, pieces[0])
        count = sizes[order[place - 1]]
        length = pieces[0].shape[0] // count
        pieces = [
            sum([g[k * length : (k + 1) * length] for g in got], pieces[0][k * length : (k + 1) * length])
            for k in range(count)
        ]


def apply_kernel(length, counts, row_ref, col_ref, used_ref, own_ref, other_ref, *refs):
    step = pl.program_id(0)
    pieces = len(counts)
    given, outs = refs[:pieces], refs[pieces : 2 * pieces]
    flux_ref, sum_ref, sem = refs[2 * pieces :]
    starts = [sum(counts[:k]) for k in range(pieces)]

    @pl.when(step == 0)
    def _():
        copies = [
            pltpu.make_async_copy(given[k], flux_ref.at[pl.ds(starts[k], counts[k])], sem.at[k])
            for k in range(pieces)
        ]
        for copy in copies:
            copy.start()
        sum_ref[...] = jnp.zeros_like(sum_ref)
        for copy in copies:
            copy.wait()

    def add_tile(tile, slot):
        flux = flux_ref[col_ref[slot]] * used_ref[slot]
        tile_high = tile.astype(jnp.bfloat16)
        tile_low = (tile - tile_high.astype(jnp.float32)).astype(jnp.bfloat16)
        flux_high = flux.astype(jnp.bfloat16)
        flux_low = (flux - flux_high.astype(jnp.float32)).astype(jnp.bfloat16)
        both = lax.dot_general(
            jnp.concatenate([flux_high, flux_low], axis=0),
            tile_high,
            DIMS,
            preferred_element_type=jnp.float32,
        )
        low = lax.dot_general(flux_high, tile_low, DIMS, preferred_element_type=jnp.float32)
        temps = flux.shape[0]
        sum_ref[row_ref[slot]] += both[:temps] + (both[temps:] + low)

    for part, ref in enumerate((own_ref, other_ref)):
        base = part * length + step * STEP

        @pl.loop(0, STEP // UNROLL)
        def _(group):
            for k in range(UNROLL):
                add_tile(ref[group * UNROLL + k], base + group * UNROLL + k)

    @pl.when(step == pl.num_programs(0) - 1)
    def _():
        copies = [
            pltpu.make_async_copy(sum_ref.at[pl.ds(starts[k], counts[k])], outs[k], sem.at[k])
            for k in range(pieces)
        ]
        for copy in copies:
            copy.start()
        for copy in copies:
            copy.wait()


def apply_tiles(row, col, used, own, other, pieces):
    length, size, _ = own.shape
    counts = [piece.shape[0] for piece in pieces]
    temps = pieces[0].shape[1]
    num = sum(counts)
    some = pl.BlockSpec((STEP, size, size), lambda i, *_: (i, 0, 0))
    anywhere = pl.BlockSpec(memory_space=pl.ANY)
    return pl.pallas_call(
        functools.partial(apply_kernel, length, counts),
        out_shape=[jax.ShapeDtypeStruct(piece.shape, jnp.float32) for piece in pieces],
        grid_spec=pltpu.PrefetchScalarGridSpec(
            num_scalar_prefetch=3,
            grid=(length // STEP,),
            in_specs=[some, some] + [anywhere] * len(pieces),
            out_specs=[anywhere] * len(pieces),
            scratch_shapes=[
                pltpu.VMEM((num, temps, size), jnp.float32),
                pltpu.VMEM((num, temps, size), jnp.float32),
                pltpu.SemaphoreType.DMA((len(pieces),)),
            ],
        ),
        compiler_params=pltpu.CompilerParams(vmem_limit_bytes=40 * 1024 * 1024),
        cost_estimate=pl.CostEstimate(
            flops=2 * 2 * length * size * size * temps * 3,
            bytes_accessed=4 * (2 * length * size * size + 2 * num * temps * size),
            transcendentals=0,
        ),
    )(row, col, used, own, other, *pieces)


def shards(
    tile_values, tile_owner, tile_row, tile_col, tile_count, relaxation, driving, heat_weight
):
    n_cols = lax.axis_size("x") * CORES
    n_rows = lax.axis_size("row")
    sizes = sizes_of(n_rows, n_cols // CORES)
    length, size, _ = tile_values.shape
    modes, columns = driving.shape
    per = modes // size
    chip_tiles = CORES * per
    num = n_rows * n_cols * per
    half = columns // CORES
    core = lax.axis_index("core")
    row_at = lax.axis_index("row")
    here = {"z": row_at // sizes["y"], "y": row_at % sizes["y"], "x": lax.axis_index("x")}
    swap = [(0, 1), (1, 0)]

    last = chip_tiles // 4
    first = (chip_tiles - last) // 2
    bounds = (0, first, chip_tiles - last, chip_tiles)
    parts = [(bounds[k], bounds[k + 1]) for k in range(len(ORDERS))]

    def place(tile, sign):
        chip, inside = tile // chip_tiles, tile % chip_tiles
        at = {
            "z": chip // (sizes["y"] * sizes["x"]),
            "y": (chip // sizes["x"]) % sizes["y"],
            "x": chip % sizes["x"],
        }
        away = {a: (sign * (at[a] - here[a]) + sizes[a]) % sizes[a] for a in sizes}
        out = jnp.zeros_like(tile)
        chips = n_rows * n_cols // CORES
        for order, (low, high) in zip(ORDERS, parts):
            inner, middle, outer = order
            slot = (away[outer] * sizes[middle] + away[middle]) * sizes[inner] + away[inner]
            slot = chips * low + slot * (high - low) + inside - low
            out = jnp.where((inside >= low) & (inside < high), slot, out)
        return out

    other_values = lax.ppermute(tile_values, "core", swap)
    owners = tile_owner[:, 0]
    row = (owners // n_cols) * (n_cols * per) + tile_row
    col = ((tile_col // per) * n_cols + owners % n_cols) * per + tile_col % per
    used = jnp.arange(length, dtype=jnp.int32) < tile_count[0]
    places = jnp.where(used, place(row, 1) * num + place(col, -1), -1)
    places = jnp.concatenate([places, lax.ppermute(places, "core", swap)])
    is_used = places >= 0
    places = jnp.where(is_used, places, 0)
    row, col, used = places // num, places % num, is_used.astype(jnp.float32)

    def by_core(own, other):
        return jnp.concatenate(
            [jnp.where(core == 0, own, other), jnp.where(core == 0, other, own)], axis=0
        )

    drive = jnp.transpose(driving.reshape(per, size, columns), (0, 2, 1))
    relax = relaxation.reshape(per, 1, size)
    low, high = drive[:, :half], drive[:, half:]
    mine = jnp.where(core == 0, low, high)
    theirs = jnp.where(core == 0, high, low)
    packed = jnp.concatenate([theirs, jnp.broadcast_to(relax, (per, 8, size))], axis=1)
    got = lax.ppermute(packed, "core", swap)
    drive_half = by_core(mine, got[:, :half])
    relax_both = by_core(relax, got[:, half : half + 1])

    drives = [drive_half[a:b] for a, b in parts]
    relaxes = [relax_both[a:b] for a, b in parts]
    fluxes = [r * d for r, d in zip(relaxes, drives)]
    for sweep in range(ITERS):
        pieces = [gather(sizes, flux, order) for flux, order in zip(fluxes, ORDERS)]
        sums = apply_tiles(row, col, used, tile_values, other_values, sum(pieces, []))
        fluxes, done = [], 0
        for order, piece, d, r in zip(ORDERS, pieces, drives, relaxes):
            summed = reduce(sizes, sums[done : done + len(piece)], order)
            done += len(piece)
            fluxes.append(r * (d + summed))
    flux = jnp.concatenate(fluxes, axis=0)
    first, second = flux[:per], flux[per:]
    mine = jnp.where(core == 0, first, second)
    got = lax.ppermute(jnp.where(core == 0, second, first), "core", swap)
    both = jnp.concatenate(
        [jnp.where(core == 0, mine, got), jnp.where(core == 0, got, mine)], axis=1
    )
    mode_flux = jnp.transpose(both, (0, 2, 1)).reshape(modes, columns)
    weighted_local = jnp.sum(heat_weight[:, None] * mode_flux, axis=0)
    weighted, weight_sum = lax.psum((weighted_local, jnp.sum(heat_weight)), ALL)
    return (mode_flux, weighted / weight_sum)


def solution(mesh):
    n_rows, n_cols = mesh.shape["row"], mesh.shape["col"]
    chips = Mesh(mesh.devices.reshape(n_rows, n_cols // CORES, CORES), ALL)
    placed = (
        P(ALL, None, None),
        P(ALL, None),
        P(ALL),
        P(ALL),
        P(ALL),
        P(ALL),
        P(ALL, None),
        P(ALL),
    )
    return jax.shard_map(
        shards,
        mesh=chips,
        in_specs=placed,
        out_specs=(P(ALL, None), P()),
        check_vma=False,
    )
```

```python
import functools

import jax
import jax.numpy as jnp
from jax import lax
from jax.experimental import pallas as pl
from jax.experimental.pallas import tpu as pltpu
from jax.sharding import Mesh
from jax.sharding import PartitionSpec as P

ITERS = 3
CORES = 2
STEP = 16
UNROLL = 8
CHIPS = ("row", "x")
ALL = ("row", "x", "core")
DIMS = (((1,), (1,)), ((), ()))
ORDERS = (("z", "x", "y"), ("z", "y", "x"), ("x", "y", "z"))


def sizes_of(n_rows, n_x):
    y = max(n for n in range(1, n_rows + 1) if n_rows % n == 0 and n * n <= n_rows)
    return {"z": n_rows // y, "y": y, "x": n_x}


def chip_of(sizes, z, y, x):
    return (z * sizes["y"] + y) * sizes["x"] + x


def shift(sizes, array, axis, by):
    pairs = []
    for z in range(sizes["z"]):
        for y in range(sizes["y"]):
            for x in range(sizes["x"]):
                at = {"z": z, "y": y, "x": x}
                to = dict(at, **{axis: (at[axis] + by) % sizes[axis]})
                pairs.append((chip_of(sizes, **at), chip_of(sizes, **to)))
    return lax.ppermute(array, CHIPS, pairs)


def shifts(sizes, block, axis):
    return [block] + [shift(sizes, block, axis, j) for j in range(1, sizes[axis])]


def gather(sizes, flux, bounds):
    first, second, last = bounds
    blocks = shifts(sizes, flux[:second], "z")
    pieces = []
    for (low, high), (_, middle, outer) in zip(((0, first), (first, second)), ORDERS):
        block = jnp.concatenate([b[low:high] for b in blocks], axis=0)
        block = jnp.concatenate(shifts(sizes, block, middle), axis=0)
        pieces.append(shifts(sizes, block, outer))
    block = flux[second:last]
    for axis in ORDERS[2][:2]:
        block = jnp.concatenate(shifts(sizes, block, axis), axis=0)
    pieces.append(shifts(sizes, block, ORDERS[2][2]))
    return pieces


def fold(sizes, pieces, axis, count):
    got = [shift(sizes, pieces[j], axis, j) for j in range(1, sizes[axis])]
    length = pieces[0].shape[0] // count
    return [
        sum([g[k * length : (k + 1) * length] for g in got], pieces[0][k * length : (k + 1) * length])
        for k in range(count)
    ]


def reduce(sizes, pieces):
    inner, middle, outer = ORDERS[2]
    blocks = fold(sizes, pieces[2], outer, sizes[middle])
    blocks = fold(sizes, blocks, middle, sizes[inner])
    tail = fold(sizes, blocks, inner, 1)[0]
    halves = []
    for piece, (inner, middle, outer) in zip(pieces, ORDERS[:2]):
        blocks = fold(sizes, piece, outer, sizes[middle])
        halves.append(fold(sizes, blocks, middle, sizes[inner]))
    head = fold(sizes, [jnp.concatenate(pair, axis=0) for pair in zip(*halves)], "z", 1)[0]
    return jnp.concatenate([head, tail], axis=0)


def split_kernel(tile_ref, pair_ref):
    size = tile_ref.shape[1]

    @pl.loop(0, STEP // UNROLL)
    def _(group):
        for k in range(UNROLL):
            tile = jnp.transpose(tile_ref[group * UNROLL + k])
            high = tile.astype(jnp.bfloat16)
            low = (tile - high.astype(jnp.float32)).astype(jnp.bfloat16)
            pair_ref[group * UNROLL + k, :size] = high
            pair_ref[group * UNROLL + k, size:] = low


def split_tiles(tiles):
    length, size, _ = tiles.shape
    return pl.pallas_call(
        split_kernel,
        out_shape=jax.ShapeDtypeStruct((length, 2 * size, size), jnp.bfloat16),
        grid=(length // STEP,),
        in_specs=[pl.BlockSpec((STEP, size, size), lambda i: (i, 0, 0))],
        out_specs=pl.BlockSpec((STEP, 2 * size, size), lambda i: (i, 0, 0)),
        compiler_params=pltpu.CompilerParams(vmem_limit_bytes=40 * 1024 * 1024),
        cost_estimate=pl.CostEstimate(
            flops=3 * length * size * size, bytes_accessed=8 * length * size * size, transcendentals=0
        ),
    )(tiles)


def apply_kernel(length, counts, weighs, row_ref, col_ref, used_ref, own_ref, other_ref, *refs):
    step = pl.program_id(0)
    pieces = len(counts)
    weight_ref, refs = (refs[0], refs[1:]) if weighs else (None, refs)
    given, outs, refs = refs[:pieces], refs[pieces : 2 * pieces], refs[2 * pieces :]
    weighted_ref, refs = (refs[0], refs[1:]) if weighs else (None, refs)
    flux_ref, sum_ref, sem = refs
    starts = [sum(counts[:k]) for k in range(pieces)]

    @pl.when(step == 0)
    def _():
        copies = [
            pltpu.make_async_copy(given[k], flux_ref.at[pl.ds(starts[k], counts[k])], sem.at[k])
            for k in range(pieces)
        ]
        for copy in copies:
            copy.start()
        sum_ref[...] = jnp.zeros_like(sum_ref)
        for copy in copies:
            copy.wait()

    def add_tile(pair, slot):
        flux = flux_ref[col_ref[slot]] * used_ref[slot]
        high = flux.astype(jnp.bfloat16)
        low = (flux - high.astype(jnp.float32)).astype(jnp.bfloat16)
        left = jnp.concatenate([high, low], axis=0)
        both = jnp.dot(
            jnp.concatenate([left, left], axis=1), pair, preferred_element_type=jnp.float32
        )
        temps = flux.shape[0]
        sum_ref[row_ref[slot]] += both[:temps] + both[temps:]

    for part, ref in enumerate((own_ref, other_ref)):
        base = part * length + step * STEP

        @pl.loop(0, STEP // UNROLL)
        def _(group):
            for k in range(UNROLL):
                add_tile(ref[group * UNROLL + k], base + group * UNROLL + k)

    @pl.when(step == pl.num_programs(0) - 1)
    def _():
        copies = [
            pltpu.make_async_copy(sum_ref.at[pl.ds(starts[k], counts[k])], outs[k], sem.at[k])
            for k in range(pieces)
        ]
        for copy in copies:
            copy.start()
        if weighs:

            def weigh(k, total):
                return total + sum_ref[k] * weight_ref[k]

            weighted_ref[...] = lax.fori_loop(
                0, sum(counts), weigh, jnp.zeros(weighted_ref.shape, jnp.float32)
            )
        for copy in copies:
            copy.wait()


def apply_tiles(row, col, used, own, other, pieces, weights=None):
    length, _, size = own.shape
    counts = [piece.shape[0] for piece in pieces]
    temps = pieces[0].shape[1]
    num = sum(counts)
    some = pl.BlockSpec((STEP, 2 * size, size), lambda i, *_: (i, 0, 0))
    anywhere = pl.BlockSpec(memory_space=pl.ANY)
    weighs = weights is not None
    out_shape = [jax.ShapeDtypeStruct(piece.shape, jnp.float32) for piece in pieces]
    in_specs, out_specs, given = [some, some], [anywhere] * len(pieces), []
    if weighs:
        in_specs.append(pl.BlockSpec((num, 1, size), lambda i, *_: (0, 0, 0)))
        out_specs.append(pl.BlockSpec((temps, size), lambda i, *_: (0, 0)))
        out_shape.append(jax.ShapeDtypeStruct((temps, size), jnp.float32))
        given.append(weights)
    return pl.pallas_call(
        functools.partial(apply_kernel, length, counts, weighs),
        out_shape=out_shape,
        grid_spec=pltpu.PrefetchScalarGridSpec(
            num_scalar_prefetch=3,
            grid=(length // STEP,),
            in_specs=in_specs + [anywhere] * len(pieces),
            out_specs=out_specs,
            scratch_shapes=[
                pltpu.VMEM((num, temps, size), jnp.float32),
                pltpu.VMEM((num, temps, size), jnp.float32),
                pltpu.SemaphoreType.DMA((len(pieces),)),
            ],
        ),
        compiler_params=pltpu.CompilerParams(vmem_limit_bytes=40 * 1024 * 1024),
        cost_estimate=pl.CostEstimate(
            flops=2 * 2 * length * size * size * temps * 4,
            bytes_accessed=4 * (2 * length * size * size + 2 * num * temps * size),
            transcendentals=0,
        ),
    )(row, col, used, own, other, *given, *pieces)


def shards(
    tile_values, tile_owner, tile_row, tile_col, tile_count, relaxation, driving, heat_weight
):
    n_cols = lax.axis_size("x") * CORES
    n_rows = lax.axis_size("row")
    sizes = sizes_of(n_rows, n_cols // CORES)
    length, size, _ = tile_values.shape
    modes, columns = driving.shape
    per = modes // size
    chip_tiles = CORES * per
    num = n_rows * n_cols * per
    half = columns // CORES
    core = lax.axis_index("core")
    row_at = lax.axis_index("row")
    here = {"z": row_at // sizes["y"], "y": row_at % sizes["y"], "x": lax.axis_index("x")}
    swap = [(0, 1), (1, 0)]

    chips = n_rows * n_cols // CORES

    second = chip_tiles - max(1, chip_tiles // 6)
    bounds = (second // 2, second, chip_tiles)
    parts = ((0, second // 2), (second // 2, second), (second, chip_tiles))

    def place(tile, sign):
        chip, inside = tile // chip_tiles, tile % chip_tiles
        at = {
            "z": chip // (sizes["y"] * sizes["x"]),
            "y": (chip // sizes["x"]) % sizes["y"],
            "x": chip % sizes["x"],
        }
        away = {a: (sign * (at[a] - here[a]) + sizes[a]) % sizes[a] for a in sizes}
        out = jnp.zeros_like(tile)
        for order, (low, high) in zip(ORDERS, parts):
            inner, middle, outer = order
            slot = (away[outer] * sizes[middle] + away[middle]) * sizes[inner] + away[inner]
            slot = chips * low + slot * (high - low) + inside - low
            out = jnp.where((inside >= low) & (inside < high), slot, out)
        return out

    def placed_tiles():
        out = []
        for order, (low, high) in zip(ORDERS, parts):
            inner, middle, outer = order
            at = {}
            for axis, across in ((outer, 0), (middle, 1), (inner, 2)):
                steps = jnp.arange(sizes[axis], dtype=jnp.int32).reshape(
                    [-1 if k == across else 1 for k in range(4)]
                )
                at[axis] = (here[axis] + steps) % sizes[axis]
            tiles = chip_of(sizes, **at) * chip_tiles + jnp.arange(low, high, dtype=jnp.int32)
            out.append(tiles.reshape(-1))
        return jnp.concatenate(out)

    other_values = lax.ppermute(tile_values, "core", swap)
    owners = tile_owner[:, 0]
    row = (owners // n_cols) * (n_cols * per) + tile_row
    col = ((tile_col // per) * n_cols + owners % n_cols) * per + tile_col % per
    used = jnp.arange(length, dtype=jnp.int32) < tile_count[0]
    places = jnp.where(used, place(row, 1) * num + place(col, -1), -1)
    places = jnp.concatenate([places, lax.ppermute(places, "core", swap)])
    is_used = places >= 0
    places = jnp.where(is_used, places, 0)
    row, col, used = places // num, places % num, is_used.astype(jnp.float32)

    def by_core(own, other):
        return jnp.concatenate(
            [jnp.where(core == 0, own, other), jnp.where(core == 0, other, own)], axis=0
        )

    drive = jnp.transpose(driving.reshape(per, size, columns), (0, 2, 1))
    relax = relaxation.reshape(per, 1, size)
    heat = heat_weight.reshape(per, 1, size)
    low, high = drive[:, :half], drive[:, half:]
    mine = jnp.where(core == 0, low, high)
    theirs = jnp.where(core == 0, high, low)
    packed = [theirs, jnp.broadcast_to(relax, (per, 8, size)), jnp.broadcast_to(heat, (per, 8, size))]
    got = lax.ppermute(jnp.concatenate(packed, axis=1), "core", swap)
    drive_half = by_core(mine, got[:, :half])
    relax_both = by_core(relax, got[:, half : half + 1])
    heat_both = by_core(heat, got[:, half + 8 : half + 9])

    own = split_tiles(tile_values)
    other = split_tiles(other_values)
    flux = relax_both * drive_half
    weighted_own = jnp.sum(heat_both * flux, axis=(0, 2))
    heats = lax.all_gather(jnp.concatenate([heat, heat * relax], axis=1), ALL, axis=0, tiled=True)
    weight_sum = jnp.sum(heats[:, 0])
    weights = heats[:, 1:][placed_tiles()]
    for sweep in range(ITERS):
        pieces = gather(sizes, flux, bounds)
        counts = [len(piece) for piece in pieces]
        last = sweep == ITERS - 1
        sums = apply_tiles(row, col, used, own, other, sum(pieces, []), weights if last else None)
        if last:
            *sums, weighted = sums
            weighted = weighted_own + jnp.sum(weighted, axis=1)
            weighted = jnp.pad(weighted[None], ((0, 0), (0, size - half)))
            weighted = lax.all_gather(weighted, ALL, axis=0, tiled=True)
            weighted = jnp.sum(weighted.reshape(chips, CORES, size), axis=0)[:, :half]
        sums = [sums[sum(counts[:k]) : sum(counts[: k + 1])] for k in range(len(counts))]
        flux = relax_both * (drive_half + reduce(sizes, sums))
    first, second = flux[:per], flux[per:]
    mine = jnp.where(core == 0, first, second)
    got = lax.ppermute(jnp.where(core == 0, second, first), "core", swap)
    both = jnp.concatenate(
        [jnp.where(core == 0, mine, got), jnp.where(core == 0, got, mine)], axis=1
    )
    mode_flux = jnp.transpose(both, (0, 2, 1)).reshape(modes, columns)
    return (mode_flux, weighted.reshape(columns) / weight_sum)


def solution(mesh):
    n_rows, n_cols = mesh.shape["row"], mesh.shape["col"]
    chips = Mesh(mesh.devices.reshape(n_rows, n_cols // CORES, CORES), ALL)
    placed = (
        P(ALL, None, None),
        P(ALL, None),
        P(ALL),
        P(ALL),
        P(ALL),
        P(ALL),
        P(ALL, None),
        P(ALL),
    )
    return jax.shard_map(
        shards,
        mesh=chips,
        in_specs=placed,
        out_specs=(P(ALL, None), P()),
        check_vma=False,
    )
```

```python
import functools

import jax
import jax.numpy as jnp
from jax import lax
from jax.experimental import pallas as pl
from jax.experimental.pallas import tpu as pltpu
from jax.sharding import Mesh
from jax.sharding import PartitionSpec as P

ITERS = 3
CORES = 2
STEP = 16
UNROLL = 8
VMEM = 60 * 1024 * 1024
PLANE = ("y", "x")
CHIPS = ("z", "y", "x")
ALL = ("z", "y", "x", "core")


def depth_of(n_rows):
    return min(n for n in range(1, n_rows + 1) if n_rows % n == 0 and n * n >= n_rows)


def exchange(blocks, axes):
    return lax.all_to_all(blocks, axes, split_axis=0, concat_axis=0, tiled=True)


def spread(block, axes):
    return exchange(jnp.concatenate([block] * lax.axis_size(axes), axis=0), axes)


def fold(blocks, axes):
    got = exchange(blocks, axes)
    return jnp.sum(got.reshape((lax.axis_size(axes), -1) + got.shape[1:]), axis=0)


def after(value, *others):
    return lax.optimization_barrier((value,) + others)[0]


def split_kernel(tile_ref, pair_ref):
    size = tile_ref.shape[1]

    @pl.loop(0, STEP // UNROLL)
    def _(group):
        for k in range(UNROLL):
            tile = jnp.transpose(tile_ref[group * UNROLL + k])
            high = tile.astype(jnp.bfloat16)
            low = (tile - high.astype(jnp.float32)).astype(jnp.bfloat16)
            pair_ref[group * UNROLL + k, :size] = high
            pair_ref[group * UNROLL + k, size:] = low


def split_tiles(tiles):
    length, size, _ = tiles.shape
    return pl.pallas_call(
        split_kernel,
        out_shape=jax.ShapeDtypeStruct((length, 2 * size, size), jnp.bfloat16),
        grid=(length // STEP,),
        in_specs=[pl.BlockSpec((STEP, size, size), lambda i: (i, 0, 0))],
        out_specs=pl.BlockSpec((STEP, 2 * size, size), lambda i: (i, 0, 0)),
        compiler_params=pltpu.CompilerParams(vmem_limit_bytes=VMEM),
        cost_estimate=pl.CostEstimate(
            flops=3 * length * size * size, bytes_accessed=8 * length * size * size, transcendentals=0
        ),
    )(tiles)


def apply_kernel(length, counts, row_ref, col_ref, used_ref, own_ref, other_ref, *refs):
    step = pl.program_id(0)
    pieces = len(counts)
    given, outs = refs[:pieces], refs[pieces : 2 * pieces]
    flux_ref, sum_ref, sem = refs[2 * pieces :]
    starts = [sum(counts[:k]) for k in range(pieces)]

    @pl.when(step == 0)
    def _():
        copies = [
            pltpu.make_async_copy(given[k], flux_ref.at[pl.ds(starts[k], counts[k])], sem.at[k])
            for k in range(pieces)
        ]
        for copy in copies:
            copy.start()
        sum_ref[...] = jnp.zeros_like(sum_ref)
        for copy in copies:
            copy.wait()

    def add_tile(pair, slot):
        flux = flux_ref[col_ref[slot]] * used_ref[slot]
        high = flux.astype(jnp.bfloat16)
        low = (flux - high.astype(jnp.float32)).astype(jnp.bfloat16)
        left = jnp.concatenate([high, low], axis=0)
        both = jnp.dot(
            jnp.concatenate([left, left], axis=1), pair, preferred_element_type=jnp.float32
        )
        temps = flux.shape[0]
        sum_ref[row_ref[slot]] += both[:temps] + both[temps:]

    for part, ref in enumerate((own_ref, other_ref)):
        base = part * length + step * STEP

        @pl.loop(0, STEP // UNROLL)
        def _(group):
            for k in range(UNROLL):
                add_tile(ref[group * UNROLL + k], base + group * UNROLL + k)

    @pl.when(step == pl.num_programs(0) - 1)
    def _():
        copies = [
            pltpu.make_async_copy(sum_ref.at[pl.ds(starts[k], counts[k])], outs[k], sem.at[k])
            for k in range(pieces)
        ]
        for copy in copies:
            copy.start()
        for copy in copies:
            copy.wait()


def apply_tiles(row, col, used, own, other, pieces):
    length, _, size = own.shape
    counts = [piece.shape[0] for piece in pieces]
    temps = pieces[0].shape[1]
    num = sum(counts)
    some = pl.BlockSpec((STEP, 2 * size, size), lambda i, *_: (i, 0, 0))
    anywhere = pl.BlockSpec(memory_space=pl.ANY)
    return pl.pallas_call(
        functools.partial(apply_kernel, length, counts),
        out_shape=[jax.ShapeDtypeStruct(piece.shape, jnp.float32) for piece in pieces],
        grid_spec=pltpu.PrefetchScalarGridSpec(
            num_scalar_prefetch=3,
            grid=(length // STEP,),
            in_specs=[some, some] + [anywhere] * len(pieces),
            out_specs=[anywhere] * len(pieces),
            scratch_shapes=[
                pltpu.VMEM((num, temps, size), jnp.float32),
                pltpu.VMEM((num, temps, size), jnp.float32),
                pltpu.SemaphoreType.DMA((len(pieces),)),
            ],
        ),
        compiler_params=pltpu.CompilerParams(vmem_limit_bytes=VMEM),
        cost_estimate=pl.CostEstimate(
            flops=2 * 2 * length * size * size * temps * 4,
            bytes_accessed=4 * (2 * length * size * size + 2 * num * temps * size),
            transcendentals=0,
        ),
    )(row, col, used, own, other, *pieces)


def shards(
    tile_values, tile_owner, tile_row, tile_col, tile_count, relaxation, driving, heat_weight
):
    n_cols = lax.axis_size("x") * CORES
    planes, plane = lax.axis_size("z"), lax.axis_size(PLANE)
    chips = planes * plane
    length, size, _ = tile_values.shape
    modes, columns = driving.shape
    per = modes // size
    chip_tiles = CORES * per
    num = chips * chip_tiles
    half = columns // CORES
    core = lax.axis_index("core")
    swap = [(0, 1), (1, 0)]

    second = chip_tiles - max(1, chip_tiles // 6)
    bounds = (0, second // 2, second, chip_tiles)
    parts = list(zip(bounds[:-1], bounds[1:]))

    def place(tile):
        chip, inside = tile // chip_tiles, tile % chip_tiles
        z, at = chip // plane, chip % plane
        out = jnp.zeros_like(tile)
        for k, (low, high) in enumerate(parts):
            slot = z * plane + at if k == 2 else at * planes + z
            slot = chips * low + slot * (high - low) + inside - low
            out = jnp.where((inside >= low) & (inside < high), slot, out)
        return out

    other_values = lax.ppermute(tile_values, "core", swap)
    owners = tile_owner[:, 0]
    row = (owners // n_cols) * (n_cols * per) + tile_row
    col = ((tile_col // per) * n_cols + owners % n_cols) * per + tile_col % per
    used = jnp.arange(length, dtype=jnp.int32) < tile_count[0]
    places = jnp.where(used, place(row) * num + place(col), -1)
    places = jnp.concatenate([places, lax.ppermute(places, "core", swap)])
    is_used = places >= 0
    places = jnp.where(is_used, places, 0)
    row, col, used = places // num, places % num, is_used.astype(jnp.float32)

    def by_core(own, other):
        return jnp.concatenate(
            [jnp.where(core == 0, own, other), jnp.where(core == 0, other, own)], axis=0
        )

    drive = jnp.transpose(driving.reshape(per, size, columns), (0, 2, 1))
    relax = relaxation.reshape(per, 1, size)
    heat = heat_weight.reshape(per, 1, size)
    low, high = drive[:, :half], drive[:, half:]
    mine = jnp.where(core == 0, low, high)
    theirs = jnp.where(core == 0, high, low)
    packed = [theirs, jnp.broadcast_to(relax, (per, 8, size)), jnp.broadcast_to(heat, (per, 8, size))]
    got = lax.ppermute(jnp.concatenate(packed, axis=1), "core", swap)
    drive_half = by_core(mine, got[:, :half])
    relax_both = by_core(relax, got[:, half : half + 1])
    heat_both = by_core(heat, got[:, half + 8 : half + 9])

    own = split_tiles(tile_values)
    other = split_tiles(other_values)
    drives = [drive_half[low:high] for low, high in parts]
    relaxes = [relax_both[low:high] for low, high in parts]
    fluxes = [r * d for r, d in zip(relaxes, drives)]
    for sweep in range(ITERS):
        by_z = [spread(flux, "z") for flux in fluxes[:2]]
        by_plane = spread(fluxes[2], PLANE)
        first = spread(by_z[0], PLANE)
        third = spread(after(by_plane, by_z[1]), "z")
        second = spread(after(by_z[1], first), PLANE)
        sums = apply_tiles(row, col, used, own, other, [first, second, third])
        third = fold(sums[2], "z")
        first = fold(sums[0], PLANE)
        second = fold(after(sums[1], first), PLANE)
        summed = [fold(first, "z"), fold(second, "z"), fold(third, PLANE)]
        fluxes = [r * (d + s) for r, d, s in zip(relaxes, drives, summed)]
    flux = jnp.concatenate(fluxes, axis=0)
    weighted = jnp.sum(heat_both * flux, axis=(0, 2))
    totals = jnp.concatenate([weighted, jnp.sum(heat).reshape(1)])
    totals = spread(jnp.pad(totals[None], ((0, 0), (0, size - half - 1))), ALL)
    totals = jnp.sum(totals.reshape(chips, CORES, size), axis=0)
    conductivity = totals[:, :half].reshape(columns) / jnp.sum(totals[:, half])
    first, second = flux[:per], flux[per:]
    mine = jnp.where(core == 0, first, second)
    got = lax.ppermute(jnp.where(core == 0, second, first), "core", swap)
    both = jnp.concatenate(
        [jnp.where(core == 0, mine, got), jnp.where(core == 0, got, mine)], axis=1
    )
    mode_flux = jnp.transpose(both, (0, 2, 1)).reshape(modes, columns)
    return (mode_flux, conductivity)


def solution(mesh):
    n_rows, n_cols = mesh.shape["row"], mesh.shape["col"]
    planes = depth_of(n_rows)
    chips = Mesh(mesh.devices.reshape(planes, n_rows // planes, n_cols // CORES, CORES), ALL)
    placed = (
        P(ALL, None, None),
        P(ALL, None),
        P(ALL),
        P(ALL),
        P(ALL),
        P(ALL),
        P(ALL, None),
        P(ALL),
    )
    return jax.shard_map(
        shards,
        mesh=chips,
        in_specs=placed,
        out_specs=(P(ALL, None), P()),
        check_vma=False,
    )
```

```python
import functools

import jax
import jax.numpy as jnp
from jax import lax
from jax.experimental import pallas as pl
from jax.experimental.pallas import tpu as pltpu
from jax.sharding import Mesh
from jax.sharding import PartitionSpec as P

ITERS = 3
CORES = 2
STEP = 16
UNROLL = 8
VMEM = 60 * 1024 * 1024
CHIPS = ("z", "y", "x")
ALL = ("z", "y", "x", "core")
NEAR = ("x", "y", "z")
GROUPS = 2


def depth_of(n_rows):
    return min(n for n in range(1, n_rows + 1) if n_rows % n == 0 and n * n >= n_rows)


def far_steps():
    return [(a, 1 << k) for a in NEAR for k in range(1, lax.axis_size(a).bit_length() - 1)]


def near_steps(part):
    turn = part % len(NEAR)
    return [(a, 1) for a in NEAR[turn:] + NEAR[:turn]]


def swap(array, step):
    axis, distance = step
    pairs = [(i, i ^ distance) for i in range(lax.axis_size(axis))]
    return lax.ppermute(array, axis, pairs)


def after(value, *others):
    return lax.optimization_barrier((value,) + others)[0]


def halves(array):
    middle = array.shape[0] // 2
    return array[:middle], array[middle:]


def gather(flux, bounds, part, held=None):
    blocks = [flux]
    for step in reversed(far_steps()):
        send = blocks[0] if len(blocks) == 1 else jnp.concatenate(blocks, axis=0)
        got = swap(send if held is None else after(send, held), step)
        held = got if held is None else held
        blocks = blocks + jnp.split(got, len(blocks))
    pieces = []
    for k, (low, high) in enumerate(bounds):
        block = jnp.concatenate([b[low:high] for b in blocks], axis=0)
        steps = near_steps(part + k)
        for step in reversed(steps[1:]):
            block = jnp.concatenate([block, swap(block, step)], axis=0)
        pieces.append((block, swap(block, steps[0])))
    return pieces, got


def reduce(pieces, part, held=None):
    ends, firsts = [], []
    for k, (keep, send) in enumerate(pieces):
        if held is not None:
            send = after(send, held[k])
        steps = near_steps(part + k)
        got = swap(send, steps[0])
        firsts.append(got)
        for step in steps[1:]:
            keep, send = [k + g for k, g in zip(halves(keep), halves(got))]
            got = swap(send, step)
        ends.append((keep, got))
    far = far_steps()
    blocks = [
        [k + g for k, g in zip(jnp.split(keep, 1 << len(far)), jnp.split(got, 1 << len(far)))]
        for keep, got in ends
    ]
    blocks = [jnp.concatenate(group, axis=0) for group in zip(*blocks)]
    for step in far:
        middle = len(blocks) // 2
        send = blocks[middle:]
        got = swap(jnp.concatenate(send, axis=0) if middle > 1 else send[0], step)
        blocks = [b + g for b, g in zip(blocks[:middle], jnp.split(got, middle))]
    return blocks[0], firsts


def split_kernel(tile_ref, pair_ref):
    size = tile_ref.shape[1]

    @pl.loop(0, STEP // UNROLL)
    def _(group):
        for k in range(UNROLL):
            tile = jnp.transpose(tile_ref[group * UNROLL + k])
            high = tile.astype(jnp.bfloat16)
            low = (tile - high.astype(jnp.float32)).astype(jnp.bfloat16)
            pair_ref[group * UNROLL + k, :size] = high
            pair_ref[group * UNROLL + k, size:] = low


def split_tiles(tiles):
    length, size, _ = tiles.shape
    return pl.pallas_call(
        split_kernel,
        out_shape=jax.ShapeDtypeStruct((length, 2 * size, size), jnp.bfloat16),
        grid=(length // STEP,),
        in_specs=[pl.BlockSpec((STEP, size, size), lambda i: (i, 0, 0))],
        out_specs=pl.BlockSpec((STEP, 2 * size, size), lambda i: (i, 0, 0)),
        compiler_params=pltpu.CompilerParams(vmem_limit_bytes=VMEM),
        cost_estimate=pl.CostEstimate(
            flops=3 * length * size * size, bytes_accessed=8 * length * size * size, transcendentals=0
        ),
    )(tiles)


def apply_kernel(length, counts, row_ref, col_ref, used_ref, own_ref, other_ref, *refs):
    step = pl.program_id(0)
    pieces = len(counts)
    given, outs = refs[:pieces], refs[pieces : 2 * pieces]
    flux_ref, sum_ref, sem = refs[2 * pieces :]
    starts = [sum(counts[:k]) for k in range(pieces)]

    @pl.when(step == 0)
    def _():
        copies = [
            pltpu.make_async_copy(given[k], flux_ref.at[pl.ds(starts[k], counts[k])], sem.at[k])
            for k in range(pieces)
        ]
        for copy in copies:
            copy.start()
        sum_ref[...] = jnp.zeros_like(sum_ref)
        for copy in copies:
            copy.wait()

    def add_tile(pair, slot):
        flux = flux_ref[col_ref[slot]] * used_ref[slot]
        high = flux.astype(jnp.bfloat16)
        low = (flux - high.astype(jnp.float32)).astype(jnp.bfloat16)
        left = jnp.concatenate([high, low], axis=0)
        both = jnp.dot(
            jnp.concatenate([left, left], axis=1), pair, preferred_element_type=jnp.float32
        )
        temps = flux.shape[0]
        sum_ref[row_ref[slot]] += both[:temps] + both[temps:]

    for part, ref in enumerate((own_ref, other_ref)):
        base = part * length + step * STEP

        @pl.loop(0, STEP // UNROLL)
        def _(group):
            for k in range(UNROLL):
                add_tile(ref[group * UNROLL + k], base + group * UNROLL + k)

    @pl.when(step == pl.num_programs(0) - 1)
    def _():
        copies = [
            pltpu.make_async_copy(sum_ref.at[pl.ds(starts[k], counts[k])], outs[k], sem.at[k])
            for k in range(pieces)
        ]
        for copy in copies:
            copy.start()
        for copy in copies:
            copy.wait()


def apply_tiles(row, col, used, own, other, pieces):
    length, _, size = own.shape
    counts = [piece.shape[0] for piece in pieces]
    temps = pieces[0].shape[1]
    num = sum(counts)
    some = pl.BlockSpec((STEP, 2 * size, size), lambda i, *_: (i, 0, 0))
    anywhere = pl.BlockSpec(memory_space=pl.ANY)
    return pl.pallas_call(
        functools.partial(apply_kernel, length, counts),
        out_shape=[jax.ShapeDtypeStruct(piece.shape, jnp.float32) for piece in pieces],
        grid_spec=pltpu.PrefetchScalarGridSpec(
            num_scalar_prefetch=3,
            grid=(length // STEP,),
            in_specs=[some, some] + [anywhere] * len(pieces),
            out_specs=[anywhere] * len(pieces),
            scratch_shapes=[
                pltpu.VMEM((num, temps, size), jnp.float32),
                pltpu.VMEM((num, temps, size), jnp.float32),
                pltpu.SemaphoreType.DMA((len(pieces),)),
            ],
        ),
        compiler_params=pltpu.CompilerParams(vmem_limit_bytes=VMEM),
        cost_estimate=pl.CostEstimate(
            flops=2 * 2 * length * size * size * temps * 4,
            bytes_accessed=4 * (2 * length * size * size + 2 * num * temps * size),
            transcendentals=0,
        ),
    )(row, col, used, own, other, *pieces)


def shards(
    tile_values, tile_owner, tile_row, tile_col, tile_count, relaxation, driving, heat_weight
):
    n_cols = lax.axis_size("x") * CORES
    chips = lax.axis_size(CHIPS)
    length, size, _ = tile_values.shape
    modes, columns = driving.shape
    per = modes // size
    chip_tiles = CORES * per
    num = chips * chip_tiles
    half = columns // CORES
    core = lax.axis_index("core")
    cores = ("core", 1)

    count = GROUPS * len(NEAR)
    edges = [chip_tiles * k // count for k in range(count + 1)]

    def place(tile):
        chip, inside = tile // chip_tiles, tile % chip_tiles
        away, width = {}, 1
        for axis in reversed(CHIPS):
            n = lax.axis_size(axis)
            away[axis] = ((chip // width) % n) ^ lax.axis_index(axis)
            width *= n
        out = jnp.zeros_like(tile)
        for part in range(count):
            slot = jnp.zeros_like(tile)
            for axis, distance in near_steps(part) + far_steps():
                slot = 2 * slot + (away[axis] // distance) % 2
            slot = chips * edges[part] + slot * (edges[part + 1] - edges[part]) + inside - edges[part]
            out = jnp.where(inside >= edges[part], slot, out)
        return out

    owners = tile_owner[:, 0]
    row = (owners // n_cols) * (n_cols * per) + tile_row
    col = ((tile_col // per) * n_cols + owners % n_cols) * per + tile_col % per
    used = jnp.arange(length, dtype=jnp.int32) < tile_count[0]
    places = jnp.where(used, place(row) * num + place(col), -1)
    places = jnp.concatenate([places, swap(places, cores)])
    is_used = places >= 0
    places = jnp.where(is_used, places, 0)
    row, col, used = places // num, places % num, is_used.astype(jnp.float32)

    def by_core(own, other):
        return jnp.concatenate(
            [jnp.where(core == 0, own, other), jnp.where(core == 0, other, own)], axis=0
        )

    drive = jnp.transpose(driving.reshape(per, size, columns), (0, 2, 1))
    relax = relaxation.reshape(per, 1, size)
    heat = heat_weight.reshape(per, 1, size)
    low, high = drive[:, :half], drive[:, half:]
    mine = jnp.where(core == 0, low, high)
    theirs = jnp.where(core == 0, high, low)
    packed = [theirs, jnp.broadcast_to(relax, (per, 8, size)), jnp.broadcast_to(heat, (per, 8, size))]
    got = swap(jnp.concatenate(packed, axis=1), cores)
    other_values = swap(after(tile_values, got), cores)
    drive_half = by_core(mine, got[:, :half])
    relax_both = by_core(relax, got[:, half : half + 1])
    heat_both = by_core(heat, got[:, half + 8 : half + 9])

    own = split_tiles(tile_values)
    other = split_tiles(other_values)
    groups = []
    for g in range(GROUPS):
        part = g * len(NEAR)
        low, high = edges[part], edges[part + len(NEAR)]
        bounds = [(edges[part + k] - low, edges[part + k + 1] - low) for k in range(len(NEAR))]
        groups.append((part, bounds, relax_both[low:high], drive_half[low:high]))
    fluxes = [relax * drive for _, _, relax, drive in groups]
    for sweep in range(ITERS):
        pieces, held = [], None
        for (part, bounds, _, _), flux in zip(groups, fluxes):
            gathered, held = gather(flux, bounds, part, held if sweep == 0 else None)
            pieces.extend(gathered)
        sums = apply_tiles(row, col, used, own, other, [p for pair in pieces for p in pair])
        pairs = list(zip(sums[0::2], sums[1::2]))
        fluxes, held = [], None
        for part, _, relax, drive in groups:
            summed, held = reduce(pairs[part : part + len(NEAR)], part, held)
            fluxes.append(relax * (drive + summed))
    flux = jnp.concatenate(fluxes, axis=0)
    weighted = jnp.sum(heat_both * flux, axis=(0, 2))
    totals = jnp.concatenate([weighted, jnp.sum(heat).reshape(1)])
    totals = jnp.pad(totals[None], ((0, 0), (0, size - half - 1)))
    totals = lax.all_to_all(
        jnp.broadcast_to(totals, (chips * CORES, size)), ALL, split_axis=0, concat_axis=0, tiled=True
    )
    totals = jnp.sum(totals.reshape(chips, CORES, size), axis=0)
    conductivity = totals[:, :half].reshape(columns) / jnp.sum(totals[:, half])
    first, second = flux[:per], flux[per:]
    mine = jnp.where(core == 0, first, second)
    got = swap(jnp.where(core == 0, second, first), cores)
    both = jnp.concatenate(
        [jnp.where(core == 0, mine, got), jnp.where(core == 0, got, mine)], axis=1
    )
    mode_flux = jnp.transpose(both, (0, 2, 1)).reshape(modes, columns)
    return (mode_flux, conductivity)


def solution(mesh):
    n_rows, n_cols = mesh.shape["row"], mesh.shape["col"]
    planes = depth_of(n_rows)
    chips = Mesh(mesh.devices.reshape(planes, n_rows // planes, n_cols // CORES, CORES), ALL)
    placed = (
        P(ALL, None, None),
        P(ALL, None),
        P(ALL),
        P(ALL),
        P(ALL),
        P(ALL),
        P(ALL, None),
        P(ALL),
    )
    return jax.shard_map(
        shards,
        mesh=chips,
        in_specs=placed,
        out_specs=(P(ALL, None), P()),
        check_vma=False,
    )
```

```python
import functools

import jax
import jax.numpy as jnp
from jax import lax
from jax.experimental import pallas as pl
from jax.experimental.pallas import tpu as pltpu
from jax.sharding import Mesh
from jax.sharding import PartitionSpec as P

ITERS = 3
CORES = 2
STEP = 16
UNROLL = 8
VMEM = 60 * 1024 * 1024
CHIPS = ("z", "y", "x")
ALL = ("z", "y", "x", "core")
NEAR = ("x", "y", "z")
GROUPS = 1


def depth_of(n_rows):
    return min(n for n in range(1, n_rows + 1) if n_rows % n == 0 and n * n >= n_rows)


def far_steps():
    return [(a, 1 << k) for a in NEAR for k in range(1, lax.axis_size(a).bit_length() - 1)]


def near_steps(part):
    turn = part % len(NEAR)
    return [(a, 1) for a in NEAR[turn:] + NEAR[:turn]]


def swap(array, step):
    axis, distance = step
    pairs = [(i, i ^ distance) for i in range(lax.axis_size(axis))]
    return lax.ppermute(array, axis, pairs)


def after(value, *others):
    return lax.optimization_barrier((value,) + others)[0]


def halves(array):
    middle = array.shape[0] // 2
    return array[:middle], array[middle:]


def gather(flux, bounds, part, held=None):
    blocks = [flux]
    for step in reversed(far_steps()):
        send = blocks[0] if len(blocks) == 1 else jnp.concatenate(blocks, axis=0)
        got = swap(send if held is None else after(send, held), step)
        held = got if held is None else held
        blocks = blocks + jnp.split(got, len(blocks))
    pieces = []
    for k, (low, high) in enumerate(bounds):
        block = jnp.concatenate([b[low:high] for b in blocks], axis=0)
        steps = near_steps(part + k)
        for step in reversed(steps[1:]):
            block = jnp.concatenate([block, swap(block, step)], axis=0)
        pieces.append((block, swap(block, steps[0])))
    return pieces, got


def reduce(pieces, part, held=None):
    ends, firsts = [], []
    for k, (keep, send) in enumerate(pieces):
        if held is not None:
            send = after(send, held[k])
        steps = near_steps(part + k)
        got = swap(send, steps[0])
        firsts.append(got)
        for step in steps[1:]:
            keep, send = [k + g for k, g in zip(halves(keep), halves(got))]
            got = swap(send, step)
        ends.append((keep, got))
    far = far_steps()
    blocks = [
        [k + g for k, g in zip(jnp.split(keep, 1 << len(far)), jnp.split(got, 1 << len(far)))]
        for keep, got in ends
    ]
    blocks = [jnp.concatenate(group, axis=0) for group in zip(*blocks)]
    for step in far:
        middle = len(blocks) // 2
        send = blocks[middle:]
        got = swap(jnp.concatenate(send, axis=0) if middle > 1 else send[0], step)
        blocks = [b + g for b, g in zip(blocks[:middle], jnp.split(got, middle))]
    return blocks[0], firsts


def split_kernel(tile_ref, pair_ref):
    size = tile_ref.shape[1]

    @pl.loop(0, STEP // UNROLL)
    def _(group):
        for k in range(UNROLL):
            tile = jnp.transpose(tile_ref[group * UNROLL + k])
            high = tile.astype(jnp.bfloat16)
            low = (tile - high.astype(jnp.float32)).astype(jnp.bfloat16)
            pair_ref[group * UNROLL + k, :size] = high
            pair_ref[group * UNROLL + k, size:] = low


def split_tiles(tiles):
    length, size, _ = tiles.shape
    return pl.pallas_call(
        split_kernel,
        out_shape=jax.ShapeDtypeStruct((length, 2 * size, size), jnp.bfloat16),
        grid=(length // STEP,),
        in_specs=[pl.BlockSpec((STEP, size, size), lambda i: (i, 0, 0))],
        out_specs=pl.BlockSpec((STEP, 2 * size, size), lambda i: (i, 0, 0)),
        compiler_params=pltpu.CompilerParams(vmem_limit_bytes=VMEM),
        cost_estimate=pl.CostEstimate(
            flops=3 * length * size * size, bytes_accessed=8 * length * size * size, transcendentals=0
        ),
    )(tiles)


def apply_kernel(length, counts, row_ref, col_ref, used_ref, own_ref, other_ref, *refs):
    step = pl.program_id(0)
    pieces = len(counts)
    given, outs = refs[:pieces], refs[pieces : 2 * pieces]
    flux_ref, sum_ref, sem = refs[2 * pieces :]
    starts = [sum(counts[:k]) for k in range(pieces)]

    @pl.when(step == 0)
    def _():
        copies = [
            pltpu.make_async_copy(given[k], flux_ref.at[pl.ds(starts[k], counts[k])], sem.at[k])
            for k in range(pieces)
        ]
        for copy in copies:
            copy.start()
        sum_ref[...] = jnp.zeros_like(sum_ref)
        for copy in copies:
            copy.wait()

    def add_tile(pair, slot):
        flux = flux_ref[col_ref[slot]] * used_ref[slot]
        high = flux.astype(jnp.bfloat16)
        low = (flux - high.astype(jnp.float32)).astype(jnp.bfloat16)
        left = jnp.concatenate([high, low], axis=0)
        both = jnp.dot(
            jnp.concatenate([left, left], axis=1), pair, preferred_element_type=jnp.float32
        )
        temps = flux.shape[0]
        sum_ref[row_ref[slot]] += both[:temps] + both[temps:]

    for part, ref in enumerate((own_ref, other_ref)):
        base = part * length + step * STEP

        @pl.loop(0, STEP // UNROLL)
        def _(group):
            for k in range(UNROLL):
                add_tile(ref[group * UNROLL + k], base + group * UNROLL + k)

    @pl.when(step == pl.num_programs(0) - 1)
    def _():
        copies = [
            pltpu.make_async_copy(sum_ref.at[pl.ds(starts[k], counts[k])], outs[k], sem.at[k])
            for k in range(pieces)
        ]
        for copy in copies:
            copy.start()
        for copy in copies:
            copy.wait()


def apply_tiles(row, col, used, own, other, pieces):
    length, _, size = own.shape
    counts = [piece.shape[0] for piece in pieces]
    temps = pieces[0].shape[1]
    num = sum(counts)
    some = pl.BlockSpec((STEP, 2 * size, size), lambda i, *_: (i, 0, 0))
    anywhere = pl.BlockSpec(memory_space=pl.ANY)
    return pl.pallas_call(
        functools.partial(apply_kernel, length, counts),
        out_shape=[jax.ShapeDtypeStruct(piece.shape, jnp.float32) for piece in pieces],
        grid_spec=pltpu.PrefetchScalarGridSpec(
            num_scalar_prefetch=3,
            grid=(length // STEP,),
            in_specs=[some, some] + [anywhere] * len(pieces),
            out_specs=[anywhere] * len(pieces),
            scratch_shapes=[
                pltpu.VMEM((num, temps, size), jnp.float32),
                pltpu.VMEM((num, temps, size), jnp.float32),
                pltpu.SemaphoreType.DMA((len(pieces),)),
            ],
        ),
        compiler_params=pltpu.CompilerParams(vmem_limit_bytes=VMEM),
        cost_estimate=pl.CostEstimate(
            flops=2 * 2 * length * size * size * temps * 4,
            bytes_accessed=4 * (2 * length * size * size + 2 * num * temps * size),
            transcendentals=0,
        ),
    )(row, col, used, own, other, *pieces)


def shards(
    tile_values, tile_owner, tile_row, tile_col, tile_count, relaxation, driving, heat_weight
):
    n_cols = lax.axis_size("x") * CORES
    chips = lax.axis_size(CHIPS)
    length, size, _ = tile_values.shape
    modes, columns = driving.shape
    per = modes // size
    chip_tiles = CORES * per
    num = chips * chip_tiles
    half = columns // CORES
    core = lax.axis_index("core")
    cores = ("core", 1)

    count = GROUPS * len(NEAR)
    edges = [chip_tiles * k // count for k in range(count + 1)]

    def place(tile):
        chip, inside = tile // chip_tiles, tile % chip_tiles
        away, width = {}, 1
        for axis in reversed(CHIPS):
            n = lax.axis_size(axis)
            away[axis] = ((chip // width) % n) ^ lax.axis_index(axis)
            width *= n
        out = jnp.zeros_like(tile)
        for part in range(count):
            slot = jnp.zeros_like(tile)
            for axis, distance in near_steps(part) + far_steps():
                slot = 2 * slot + (away[axis] // distance) % 2
            slot = chips * edges[part] + slot * (edges[part + 1] - edges[part]) + inside - edges[part]
            out = jnp.where(inside >= edges[part], slot, out)
        return out

    owners = tile_owner[:, 0]
    row = (owners // n_cols) * (n_cols * per) + tile_row
    col = ((tile_col // per) * n_cols + owners % n_cols) * per + tile_col % per
    used = jnp.arange(length, dtype=jnp.int32) < tile_count[0]
    places = jnp.where(used, place(row) * num + place(col), -1)
    places = jnp.concatenate([places, swap(places, cores)])
    is_used = places >= 0
    places = jnp.where(is_used, places, 0)
    row, col, used = places // num, places % num, is_used.astype(jnp.float32)

    def by_core(own, other):
        return jnp.concatenate(
            [jnp.where(core == 0, own, other), jnp.where(core == 0, other, own)], axis=0
        )

    drive = jnp.transpose(driving.reshape(per, size, columns), (0, 2, 1))
    relax = relaxation.reshape(per, 1, size)
    heat = heat_weight.reshape(per, 1, size)
    low, high = drive[:, :half], drive[:, half:]
    mine = jnp.where(core == 0, low, high)
    theirs = jnp.where(core == 0, high, low)
    packed = [theirs, jnp.broadcast_to(relax, (per, 8, size)), jnp.broadcast_to(heat, (per, 8, size))]
    got = swap(jnp.concatenate(packed, axis=1), cores)
    other_values = swap(after(tile_values, got), cores)
    drive_half = by_core(mine, got[:, :half])
    relax_both = by_core(relax, got[:, half : half + 1])
    heat_both = by_core(heat, got[:, half + 8 : half + 9])

    own = split_tiles(tile_values)
    other = split_tiles(other_values)
    groups = []
    for g in range(GROUPS):
        part = g * len(NEAR)
        low, high = edges[part], edges[part + len(NEAR)]
        bounds = [(edges[part + k] - low, edges[part + k + 1] - low) for k in range(len(NEAR))]
        groups.append((part, bounds, relax_both[low:high], drive_half[low:high]))
    fluxes = [relax * drive for _, _, relax, drive in groups]
    for sweep in range(ITERS):
        pieces, held = [], None
        for (part, bounds, _, _), flux in zip(groups, fluxes):
            gathered, held = gather(flux, bounds, part, held if sweep == 0 else None)
            pieces.extend(gathered)
        sums = apply_tiles(row, col, used, own, other, [p for pair in pieces for p in pair])
        pairs = list(zip(sums[0::2], sums[1::2]))
        fluxes, held = [], None
        for part, _, relax, drive in groups:
            summed, held = reduce(pairs[part : part + len(NEAR)], part, held)
            fluxes.append(relax * (drive + summed))
    flux = jnp.concatenate(fluxes, axis=0)
    weighted = jnp.sum(heat_both * flux, axis=(0, 2))
    totals = jnp.concatenate([weighted, jnp.sum(heat).reshape(1)])
    totals = jnp.pad(totals[None], ((0, 0), (0, size - half - 1)))
    totals = lax.all_to_all(
        jnp.broadcast_to(totals, (chips * CORES, size)), ALL, split_axis=0, concat_axis=0, tiled=True
    )
    totals = jnp.sum(totals.reshape(chips, CORES, size), axis=0)
    conductivity = totals[:, :half].reshape(columns) / jnp.sum(totals[:, half])
    first, second = flux[:per], flux[per:]
    mine = jnp.where(core == 0, first, second)
    got = swap(jnp.where(core == 0, second, first), cores)
    both = jnp.concatenate(
        [jnp.where(core == 0, mine, got), jnp.where(core == 0, got, mine)], axis=1
    )
    mode_flux = jnp.transpose(both, (0, 2, 1)).reshape(modes, columns)
    return (mode_flux, conductivity)


def solution(mesh):
    n_rows, n_cols = mesh.shape["row"], mesh.shape["col"]
    planes = depth_of(n_rows)
    chips = Mesh(mesh.devices.reshape(planes, n_rows // planes, n_cols // CORES, CORES), ALL)
    placed = (
        P(ALL, None, None),
        P(ALL, None),
        P(ALL),
        P(ALL),
        P(ALL),
        P(ALL),
        P(ALL, None),
        P(ALL),
    )
    return jax.shard_map(
        shards,
        mesh=chips,
        in_specs=placed,
        out_specs=(P(ALL, None), P()),
        check_vma=False,
    )
```

```python
import functools

import jax
import jax.numpy as jnp
from jax import lax
from jax.experimental import pallas as pl
from jax.experimental.pallas import tpu as pltpu
from jax.sharding import Mesh
from jax.sharding import PartitionSpec as P

ITERS = 3
CORES = 2
STEP = 16
UNROLL = 8
CHUNK = 8
SLOTS = 8
VMEM = 60 * 1024 * 1024
CHIPS = ("z", "y", "x")
ALL = ("z", "y", "x", "core")
NEAR = ("x", "y", "z")


def depth_of(n_rows):
    return min(n for n in range(1, n_rows + 1) if n_rows % n == 0 and n * n >= n_rows)


def far_steps():
    return [(a, 1 << k) for a in NEAR for k in range(1, lax.axis_size(a).bit_length() - 1)]


def near_steps(part):
    turn = part % len(NEAR)
    return [(a, 1) for a in NEAR[turn:] + NEAR[:turn]]


def swap(array, step):
    axis, distance = step
    pairs = [(i, i ^ distance) for i in range(lax.axis_size(axis))]
    return lax.ppermute(array, axis, pairs)


def after(value, *others):
    return lax.optimization_barrier((value,) + others)[0]


def halves(array):
    middle = array.shape[0] // 2
    return array[:middle], array[middle:]


def gather_far(block, beside=None):
    blocks = [block]
    for step in reversed(far_steps()):
        got = swap(blocks[0] if len(blocks) == 1 else jnp.concatenate(blocks, axis=0), step)
        if beside is not None:
            got, beside = after(got, beside), None
        blocks = blocks + jnp.split(got, len(blocks))
    return blocks


def gather(flux, edges, beside=None):
    blocks = gather_far(flux, beside)
    pieces = []
    for part in range(len(NEAR)):
        block = jnp.concatenate([b[edges[part] : edges[part + 1]] for b in blocks], axis=0)
        steps = near_steps(part)
        for step in reversed(steps[1:]):
            block = jnp.concatenate([block, swap(block, step)], axis=0)
        pieces.append((block, swap(block, steps[0])))
    return pieces


def reduce_near(keeps, sends):
    far = 1 << len(far_steps())
    parts = []
    for part, (keep, send) in enumerate(zip(keeps, sends)):
        steps = near_steps(part)
        got = swap(send, steps[0])
        for step in steps[1:]:
            keep, send = [k + g for k, g in zip(halves(keep), halves(got))]
            got = swap(send, step)
        parts.append([k + g for k, g in zip(jnp.split(keep, far), jnp.split(got, far))])
    return [jnp.concatenate(group, axis=0) for group in zip(*parts)]


def reduce_far(blocks):
    for step in far_steps():
        middle = len(blocks) // 2
        send = blocks[middle:]
        got = swap(jnp.concatenate(send, axis=0) if middle > 1 else send[0], step)
        blocks = [b + g for b, g in zip(blocks[:middle], jnp.split(got, middle))]
    return blocks[0]


def split_kernel(tile_ref, *refs):
    pair_ref = refs[-1]
    size = tile_ref.shape[1]

    @pl.loop(0, STEP // UNROLL)
    def _(group):
        for k in range(UNROLL):
            tile = jnp.transpose(tile_ref[group * UNROLL + k])
            high = tile.astype(jnp.bfloat16)
            low = (tile - high.astype(jnp.float32)).astype(jnp.bfloat16)
            pair_ref[group * UNROLL + k, :size] = high
            pair_ref[group * UNROLL + k, size:] = low


def split_tiles(tiles, place, pairs=None):
    length, size, _ = tiles.shape
    steps = length // STEP
    given = [] if pairs is None else [pairs]
    return pl.pallas_call(
        split_kernel,
        out_shape=jax.ShapeDtypeStruct((CORES * length, 2 * size, size), jnp.bfloat16),
        grid=(steps,),
        in_specs=[pl.BlockSpec((STEP, size, size), lambda i: (i, 0, 0))]
        + [pl.BlockSpec(memory_space=pl.ANY)] * len(given),
        out_specs=pl.BlockSpec((STEP, 2 * size, size), lambda i: (place * steps + i, 0, 0)),
        input_output_aliases={1: 0} if given else {},
        compiler_params=pltpu.CompilerParams(vmem_limit_bytes=VMEM),
        cost_estimate=pl.CostEstimate(
            flops=3 * length * size * size, bytes_accessed=8 * length * size * size, transcendentals=0
        ),
    )(tiles, *given)


def apply_kernel(span, skip, counts, has_base, ends_ref, order_ref, row_ref, col_ref, pairs_ref, *refs):
    ends, refs = refs[: len(counts)], refs[len(counts) :]
    base_ref, refs = (refs[0], refs[1:]) if has_base else (None, refs)
    *outs, flux_ref, sum_ref, held_ref, sem, held_sem = refs
    total = order_ref.shape[0]
    start, stop = ends_ref[span], ends_ref[span + 1]
    chunks = (stop - start + CHUNK - 1) // CHUNK

    def fetch(chunk):
        slot = lax.rem(chunk, SLOTS)
        for k in range(CHUNK):
            at = jnp.minimum(start + chunk * CHUNK + k, total - 1)
            pltpu.make_async_copy(
                pairs_ref.at[order_ref[at]], held_ref.at[slot, k], held_sem.at[slot]
            ).start()

    copies = [
        pltpu.make_async_copy(
            piece, flux_ref.at[pl.ds(sum(counts[:k]), counts[k])], sem.at[k]
        )
        for k, piece in enumerate(ends)
    ]
    if has_base:
        copies.append(pltpu.make_async_copy(base_ref, sum_ref, sem.at[len(counts)]))
    for copy in copies:
        copy.start()
    for chunk in range(SLOTS - 1):

        @pl.when(chunk < chunks)
        def _():
            fetch(jnp.int32(chunk))

    if not has_base:
        sum_ref[...] = jnp.zeros_like(sum_ref)
    for copy in copies:
        copy.wait()

    @pl.loop(0, chunks)
    def _(chunk):
        slot = lax.rem(chunk, SLOTS)
        pltpu.make_async_copy(
            pairs_ref.at[pl.ds(0, CHUNK)], held_ref.at[slot], held_sem.at[slot]
        ).wait()

        @pl.when(chunk + SLOTS - 1 < chunks)
        def _():
            fetch(chunk + SLOTS - 1)

        products, rows = [], []
        for k in range(CHUNK):
            at = start + chunk * CHUNK + k
            valid = jnp.where(at < stop, 1.0, 0.0)
            at = jnp.minimum(at, stop - 1)
            flux = flux_ref[col_ref[at]] * valid
            high = flux.astype(jnp.bfloat16)
            low = (flux - high.astype(jnp.float32)).astype(jnp.bfloat16)
            left = jnp.concatenate([high, low], axis=0)
            both = jnp.dot(
                jnp.concatenate([left, left], axis=1),
                held_ref[slot, k],
                preferred_element_type=jnp.float32,
            )
            temps = flux.shape[0]
            products.append(both[:temps] + both[temps:])
            rows.append(row_ref[at] - skip)
        for row, product in zip(rows, products):
            sum_ref[row] += product

    sizes = [out.shape[0] for out in outs]
    copies = [
        pltpu.make_async_copy(sum_ref.at[pl.ds(sum(sizes[:k]), sizes[k])], out, sem.at[k])
        for k, out in enumerate(outs)
    ]
    for copy in copies:
        copy.start()
    for copy in copies:
        copy.wait()


def apply_tiles(span, skip, places, pairs, flux, sizes, share, base=None):
    total, _, size = pairs.shape
    counts = [piece.shape[0] for piece in flux]
    temps = flux[0].shape[1]
    anywhere = pl.BlockSpec(memory_space=pl.ANY)
    given = [pairs, *flux] + ([] if base is None else [base])
    return pl.pallas_call(
        functools.partial(apply_kernel, span, skip, counts, base is not None),
        out_shape=[jax.ShapeDtypeStruct((n, temps, size), jnp.float32) for n in sizes],
        grid_spec=pltpu.PrefetchScalarGridSpec(
            num_scalar_prefetch=4,
            grid=(),
            in_specs=[anywhere] * len(given),
            out_specs=[anywhere] * len(sizes),
            scratch_shapes=[
                pltpu.VMEM((sum(counts), temps, size), jnp.float32),
                pltpu.VMEM((sum(sizes), temps, size), jnp.float32),
                pltpu.VMEM((SLOTS, CHUNK) + pairs.shape[1:], jnp.bfloat16),
                pltpu.SemaphoreType.DMA((len(counts) + 1,)),
                pltpu.SemaphoreType.DMA((SLOTS,)),
            ],
        ),
        compiler_params=pltpu.CompilerParams(vmem_limit_bytes=VMEM),
        cost_estimate=pl.CostEstimate(
            flops=int(share * total * size * size * temps * 8),
            bytes_accessed=int(share * total * size * size * 4) + 8 * sum(sizes) * temps * size,
            transcendentals=0,
        ),
    )(*places, *given)


def shards(
    tile_values, tile_owner, tile_row, tile_col, tile_count, relaxation, driving, heat_weight
):
    n_cols = lax.axis_size("x") * CORES
    chips = lax.axis_size(CHIPS)
    length, size, _ = tile_values.shape
    modes, columns = driving.shape
    per = modes // size
    chip_tiles = CORES * per
    num = chips * chip_tiles
    half = columns // CORES
    core = lax.axis_index("core")
    cores = ("core", 1)

    edges = [chip_tiles * k // len(NEAR) for k in range(len(NEAR) + 1)]

    def place(tile):
        chip, inside = tile // chip_tiles, tile % chip_tiles
        away, width = {}, 1
        for axis in reversed(CHIPS):
            n = lax.axis_size(axis)
            away[axis] = ((chip // width) % n) ^ lax.axis_index(axis)
            width *= n
        side, out = jnp.zeros_like(tile), jnp.zeros_like(tile)
        for part in range(len(NEAR)):
            low, high = edges[part], edges[part + 1]
            (first, _), *steps = near_steps(part)
            slot = jnp.zeros_like(tile)
            for axis, distance in steps + far_steps():
                slot = 2 * slot + (away[axis] // distance) % 2
            slot = chips // 2 * low + slot * (high - low) + inside - low
            out = jnp.where(inside >= low, slot, out)
            side = jnp.where(inside >= low, away[first] % 2, side)
        return side, out

    owners = tile_owner[:, 0]
    row_side, row = place((owners // n_cols) * (n_cols * per) + tile_row)
    col_side, col = place(((tile_col // per) * n_cols + owners % n_cols) * per + tile_col % per)
    used = jnp.arange(length, dtype=jnp.int32) < tile_count[0]
    kind = jnp.where(used, jnp.where(col_side == 0, 0, 2 - row_side), 3)
    row = jnp.where(row_side == 1, row, row + num // 2)
    code = (kind * num + row) * num + col
    code = jnp.concatenate([code, swap(code, cores)])
    kind = code // (num * num)
    slots = jnp.arange(CORES * length, dtype=jnp.int32)
    key = kind * (CORES * length) + slots
    rank = jnp.sum((key[None, :] < key[:, None]).astype(jnp.int32), axis=1)
    ends = jnp.sum((kind[None, :] < jnp.arange(4, dtype=jnp.int32)[:, None]).astype(jnp.int32), axis=1)
    sorts = rank[None, :] == slots[:, None]
    order = jnp.sum(jnp.where(sorts, slots[None, :], 0), axis=1)
    code = jnp.sum(jnp.where(sorts, code[None, :] % (num * num), 0), axis=1)
    places = (ends, order, code // num, code % num)

    def by_core(own, other):
        return jnp.concatenate(
            [jnp.where(core == 0, own, other), jnp.where(core == 0, other, own)], axis=0
        )

    drive = jnp.transpose(driving.reshape(per, size, columns), (0, 2, 1))
    relax = relaxation.reshape(per, 1, size)
    heat = heat_weight.reshape(per, 1, size)
    low, high = drive[:, :half], drive[:, half:]
    mine = jnp.where(core == 0, low, high)
    theirs = jnp.where(core == 0, high, low)
    packed = [theirs, jnp.broadcast_to(relax, (per, 8, size)), jnp.broadcast_to(heat, (per, 8, size))]
    got = swap(jnp.concatenate(packed, axis=1), cores)
    other_values = swap(after(tile_values, got), cores)
    drive_half = by_core(mine, got[:, :half])
    relax_both = by_core(relax, got[:, half : half + 1])
    heat_both = by_core(heat, got[:, half + 8 : half + 9])

    pairs = split_tiles(tile_values, 0)
    beside = pairs
    heats = gather_far(heat_both * relax_both)
    flux = relax_both * drive_half
    sizes = [chips // 2 * (high - low) for low, high in zip(edges[:-1], edges[1:])]
    for sweep in range(ITERS):
        pieces = gather(flux, edges, beside)
        if sweep == 0:
            pairs, beside = split_tiles(other_values, 1, pairs), None
        near, far = [p for p, _ in pieces], [p for _, p in pieces]
        base = apply_tiles(0, 0, places, pairs, near, [num // 2, num // 2], 0.5)
        sends = apply_tiles(1, 0, places, pairs, far, sizes, 0.25, base[0])
        keeps = apply_tiles(2, num // 2, places, pairs, far, sizes, 0.25, base[1])
        blocks = reduce_near(keeps, sends)
        if sweep == ITERS - 1:
            weighted = sum(
                [jnp.sum(w * b, axis=(0, 2)) for w, b in zip(heats, blocks)],
                jnp.sum(heats[0] * drive_half, axis=(0, 2)),
            )
            totals = jnp.concatenate([weighted, jnp.sum(heat).reshape(1)])
            totals = jnp.pad(totals[None], ((0, 0), (0, size - half - 1)))
            totals = lax.all_to_all(
                jnp.broadcast_to(totals, (chips * CORES, size)), ALL, split_axis=0, concat_axis=0, tiled=True
            )
            totals = jnp.sum(totals.reshape(chips, CORES, size), axis=0)
            conductivity = totals[:, :half].reshape(columns) / jnp.sum(totals[:, half])
        flux = relax_both * (drive_half + reduce_far(blocks))
    first, second = flux[:per], flux[per:]
    mine = jnp.where(core == 0, first, second)
    got = swap(jnp.where(core == 0, second, first), cores)
    both = jnp.concatenate(
        [jnp.where(core == 0, mine, got), jnp.where(core == 0, got, mine)], axis=1
    )
    mode_flux = jnp.transpose(both, (0, 2, 1)).reshape(modes, columns)
    return (mode_flux, conductivity)


def solution(mesh):
    n_rows, n_cols = mesh.shape["row"], mesh.shape["col"]
    planes = depth_of(n_rows)
    chips = Mesh(mesh.devices.reshape(planes, n_rows // planes, n_cols // CORES, CORES), ALL)
    placed = (
        P(ALL, None, None),
        P(ALL, None),
        P(ALL),
        P(ALL),
        P(ALL),
        P(ALL),
        P(ALL, None),
        P(ALL),
    )
    return jax.shard_map(
        shards,
        mesh=chips,
        in_specs=placed,
        out_specs=(P(ALL, None), P()),
        check_vma=False,
    )
```

```python
import functools

import jax
import jax.numpy as jnp
from jax import lax
from jax.experimental import pallas as pl
from jax.experimental.pallas import tpu as pltpu
from jax.sharding import Mesh
from jax.sharding import PartitionSpec as P

ITERS = 3
CORES = 2
STEP = 16
UNROLL = 8
CHUNK = 8
SLOTS = 8
VMEM = 16 * 1024 * 1024
CHIPS = ("z", "y", "x")
ALL = ("z", "y", "x", "core")
NEAR = ("x", "y", "z")


def depth_of(n_rows):
    return min(n for n in range(1, n_rows + 1) if n_rows % n == 0 and n * n >= n_rows)


def far_steps():
    return [(a, 1 << k) for a in NEAR for k in range(1, lax.axis_size(a).bit_length() - 1)]


def near_steps(part):
    turn = part % len(NEAR)
    return [(a, 1) for a in NEAR[turn:] + NEAR[:turn]]


def swap(array, step):
    axis, distance = step
    pairs = [(i, i ^ distance) for i in range(lax.axis_size(axis))]
    return lax.ppermute(array, axis, pairs)


def after(value, *others):
    return lax.optimization_barrier((value,) + others)[0]


def halves(array):
    middle = array.shape[0] // 2
    return array[:middle], array[middle:]


def gather_far(block, beside=None):
    blocks = [block]
    for step in reversed(far_steps()):
        got = swap(blocks[0] if len(blocks) == 1 else jnp.concatenate(blocks, axis=0), step)
        if beside is not None:
            got, beside = after(got, *beside), None
        blocks = blocks + jnp.split(got, len(blocks))
    return blocks


def gather(flux, edges, beside=None):
    blocks = gather_far(flux, beside)
    starts = [
        jnp.concatenate([b[low:high] for b in blocks], axis=0) for low, high in zip(edges[:-1], edges[1:])
    ]
    pieces = []
    for part, block in enumerate(lax.optimization_barrier(starts)):
        steps = near_steps(part)
        for step in reversed(steps[1:]):
            block = jnp.concatenate([block, swap(block, step)], axis=0)
        pieces.append((block, swap(block, steps[0])))
    return pieces


def reduce_near(keeps, sends):
    far = 1 << len(far_steps())
    parts = []
    for part, (keep, send) in enumerate(zip(keeps, sends)):
        steps = near_steps(part)
        got = swap(send, steps[0])
        for step in steps[1:]:
            keep, send = [k + g for k, g in zip(halves(keep), halves(got))]
            got = swap(send, step)
        parts.append([k + g for k, g in zip(jnp.split(keep, far), jnp.split(got, far))])
    return [jnp.concatenate(group, axis=0) for group in zip(*parts)]


def reduce_far(blocks):
    for step in far_steps():
        middle = len(blocks) // 2
        send = blocks[middle:]
        got = swap(jnp.concatenate(send, axis=0) if middle > 1 else send[0], step)
        blocks = [b + g for b, g in zip(blocks[:middle], jnp.split(got, middle))]
    return blocks[0]


def split_kernel(tile_ref, *refs):
    pair_ref = refs[-1]
    size = tile_ref.shape[1]

    @pl.loop(0, STEP // UNROLL)
    def _(group):
        for k in range(UNROLL):
            tile = jnp.transpose(tile_ref[group * UNROLL + k])
            high = tile.astype(jnp.bfloat16)
            low = (tile - high.astype(jnp.float32)).astype(jnp.bfloat16)
            pair_ref[group * UNROLL + k, :size] = high
            pair_ref[group * UNROLL + k, size:] = low


def split_tiles(tiles, place, pairs=None):
    length, size, _ = tiles.shape
    steps = length // STEP
    given = [] if pairs is None else [pairs]
    return pl.pallas_call(
        split_kernel,
        out_shape=jax.ShapeDtypeStruct((CORES * length, 2 * size, size), jnp.bfloat16),
        grid=(steps,),
        in_specs=[pl.BlockSpec((STEP, size, size), lambda i: (i, 0, 0))]
        + [pl.BlockSpec(memory_space=pltpu.HBM)] * len(given),
        out_specs=pl.BlockSpec((STEP, 2 * size, size), lambda i: (place * steps + i, 0, 0)),
        input_output_aliases={1: 0} if given else {},
        compiler_params=pltpu.CompilerParams(vmem_limit_bytes=VMEM),
        cost_estimate=pl.CostEstimate(
            flops=3 * length * size * size, bytes_accessed=8 * length * size * size, transcendentals=0
        ),
    )(tiles, *given)


def apply_kernel(span, skip, counts, has_base, ends_ref, order_ref, row_ref, col_ref, pairs_ref, *refs):
    ends, refs = refs[: len(counts)], refs[len(counts) :]
    base_ref, refs = (refs[0], refs[1:]) if has_base else (None, refs)
    *outs, flux_ref, sum_ref, held_ref, sem, held_sem = refs
    total = order_ref.shape[0]
    start, stop = ends_ref[span], ends_ref[span + 1]
    chunks = (stop - start + CHUNK - 1) // CHUNK

    def fetch(chunk):
        slot = lax.rem(chunk, SLOTS)
        for k in range(CHUNK):
            at = jnp.minimum(start + chunk * CHUNK + k, total - 1)
            pltpu.make_async_copy(
                pairs_ref.at[order_ref[at]], held_ref.at[slot, k], held_sem.at[slot]
            ).start()

    copies = [
        pltpu.make_async_copy(
            piece, flux_ref.at[pl.ds(sum(counts[:k]), counts[k])], sem.at[k]
        )
        for k, piece in enumerate(ends)
    ]
    if has_base:
        copies.append(pltpu.make_async_copy(base_ref, sum_ref, sem.at[len(counts)]))
    for copy in copies:
        copy.start()
    for chunk in range(SLOTS - 1):

        @pl.when(chunk < chunks)
        def _():
            fetch(jnp.int32(chunk))

    if not has_base:
        sum_ref[...] = jnp.zeros_like(sum_ref)
    for copy in copies:
        copy.wait()

    @pl.loop(0, chunks)
    def _(chunk):
        slot = lax.rem(chunk, SLOTS)
        pltpu.make_async_copy(
            pairs_ref.at[pl.ds(0, CHUNK)], held_ref.at[slot], held_sem.at[slot]
        ).wait()

        @pl.when(chunk + SLOTS - 1 < chunks)
        def _():
            fetch(chunk + SLOTS - 1)

        products, rows = [], []
        for k in range(CHUNK):
            at = start + chunk * CHUNK + k
            valid = jnp.where(at < stop, 1.0, 0.0)
            at = jnp.minimum(at, stop - 1)
            flux = flux_ref[col_ref[at]] * valid
            high = flux.astype(jnp.bfloat16)
            low = (flux - high.astype(jnp.float32)).astype(jnp.bfloat16)
            left = jnp.concatenate([high, low], axis=0)
            both = jnp.dot(
                jnp.concatenate([left, left], axis=1),
                held_ref[slot, k],
                preferred_element_type=jnp.float32,
            )
            temps = flux.shape[0]
            products.append(both[:temps] + both[temps:])
            rows.append(row_ref[at] - skip)
        for row, product in zip(rows, products):
            sum_ref[row] += product

    sizes = [out.shape[0] for out in outs]
    copies = [
        pltpu.make_async_copy(sum_ref.at[pl.ds(sum(sizes[:k]), sizes[k])], out, sem.at[k])
        for k, out in enumerate(outs)
    ]
    for copy in copies:
        copy.start()
    for copy in copies:
        copy.wait()


def apply_tiles(span, skip, places, pairs, flux, sizes, share, base=None):
    total, _, size = pairs.shape
    counts = [piece.shape[0] for piece in flux]
    temps = flux[0].shape[1]
    anywhere = pl.BlockSpec(memory_space=pltpu.HBM)
    given = [pairs, *flux] + ([] if base is None else [base])
    return pl.pallas_call(
        functools.partial(apply_kernel, span, skip, counts, base is not None),
        out_shape=[jax.ShapeDtypeStruct((n, temps, size), jnp.float32) for n in sizes],
        grid_spec=pltpu.PrefetchScalarGridSpec(
            num_scalar_prefetch=4,
            grid=(),
            in_specs=[anywhere] * len(given),
            out_specs=[anywhere] * len(sizes),
            scratch_shapes=[
                pltpu.VMEM((sum(counts), temps, size), jnp.float32),
                pltpu.VMEM((sum(sizes), temps, size), jnp.float32),
                pltpu.VMEM((SLOTS, CHUNK) + pairs.shape[1:], jnp.bfloat16),
                pltpu.SemaphoreType.DMA((len(counts) + 1,)),
                pltpu.SemaphoreType.DMA((SLOTS,)),
            ],
        ),
        compiler_params=pltpu.CompilerParams(vmem_limit_bytes=VMEM),
        cost_estimate=pl.CostEstimate(
            flops=int(share * total * size * size * temps * 8),
            bytes_accessed=int(share * total * size * size * 4) + 8 * sum(sizes) * temps * size,
            transcendentals=0,
        ),
    )(*places, *given)


def shards(
    tile_values, tile_owner, tile_row, tile_col, tile_count, relaxation, driving, heat_weight
):
    n_cols = lax.axis_size("x") * CORES
    chips = lax.axis_size(CHIPS)
    length, size, _ = tile_values.shape
    modes, columns = driving.shape
    per = modes // size
    chip_tiles = CORES * per
    num = chips * chip_tiles
    half = columns // CORES
    core = lax.axis_index("core")
    cores = ("core", 1)

    edges = [chip_tiles * k // len(NEAR) for k in range(len(NEAR) + 1)]

    def place(tile):
        chip, inside = tile // chip_tiles, tile % chip_tiles
        away, width = {}, 1
        for axis in reversed(CHIPS):
            n = lax.axis_size(axis)
            away[axis] = ((chip // width) % n) ^ lax.axis_index(axis)
            width *= n
        side, out = jnp.zeros_like(tile), jnp.zeros_like(tile)
        for part in range(len(NEAR)):
            low, high = edges[part], edges[part + 1]
            (first, _), *steps = near_steps(part)
            slot = jnp.zeros_like(tile)
            for axis, distance in steps + far_steps():
                slot = 2 * slot + (away[axis] // distance) % 2
            slot = chips // 2 * low + slot * (high - low) + inside - low
            out = jnp.where(inside >= low, slot, out)
            side = jnp.where(inside >= low, away[first] % 2, side)
        return side, out

    owners = tile_owner[:, 0]
    row_side, row = place((owners // n_cols) * (n_cols * per) + tile_row)
    col_side, col = place(((tile_col // per) * n_cols + owners % n_cols) * per + tile_col % per)
    used = jnp.arange(length, dtype=jnp.int32) < tile_count[0]
    kind = jnp.where(used, jnp.where(col_side == 0, 0, 2 - row_side), 3)
    row = jnp.where(row_side == 1, row, row + num // 2)
    code = (kind * num + row) * num + col
    code = jnp.concatenate([code, swap(code, cores)])
    kind = code // (num * num)
    slots = jnp.arange(CORES * length, dtype=jnp.int32)
    key = kind * (CORES * length) + slots
    rank = jnp.sum((key[None, :] < key[:, None]).astype(jnp.int32), axis=1)
    ends = jnp.sum((kind[None, :] < jnp.arange(4, dtype=jnp.int32)[:, None]).astype(jnp.int32), axis=1)
    sorts = rank[None, :] == slots[:, None]
    order = jnp.sum(jnp.where(sorts, slots[None, :], 0), axis=1)
    code = jnp.sum(jnp.where(sorts, code[None, :] % (num * num), 0), axis=1)
    places = (ends, order, code // num, code % num)

    def by_core(own, other):
        return jnp.concatenate(
            [jnp.where(core == 0, own, other), jnp.where(core == 0, other, own)], axis=0
        )

    drive = jnp.transpose(driving.reshape(per, size, columns), (0, 2, 1))
    relax = relaxation.reshape(per, 1, size)
    heat = heat_weight.reshape(per, 1, size)
    low, high = drive[:, :half], drive[:, half:]
    mine = jnp.where(core == 0, low, high)
    theirs = jnp.where(core == 0, high, low)
    packed = [theirs, jnp.broadcast_to(relax, (per, 8, size)), jnp.broadcast_to(heat, (per, 8, size))]
    got = swap(jnp.concatenate(packed, axis=1), cores)
    other_values = swap(after(tile_values, got), cores)
    drive_half = by_core(mine, got[:, :half])
    relax_both = by_core(relax, got[:, half : half + 1])
    heat_both = by_core(heat, got[:, half + 8 : half + 9])

    flux = relax_both * drive_half
    pairs = split_tiles(after(tile_values, flux), 0)
    heats = gather_far(heat_both * relax_both)
    beside = (pairs, *heats)
    sizes = [chips // 2 * (high - low) for low, high in zip(edges[:-1], edges[1:])]
    for sweep in range(ITERS):
        pieces = gather(flux, edges, beside)
        if sweep == 0:
            pairs, beside = split_tiles(other_values, 1, pairs), None
        near, far = [p for p, _ in pieces], [p for _, p in pieces]
        base = apply_tiles(0, 0, places, pairs, near, [num // 2, num // 2], 0.5)
        sends = apply_tiles(1, 0, places, pairs, far, sizes, 0.25, base[0])
        keeps = apply_tiles(2, num // 2, places, pairs, far, sizes, 0.25, base[1])
        blocks = reduce_near(keeps, sends)
        if sweep == ITERS - 1:
            weighted = sum(
                [jnp.sum(w * b, axis=(0, 2)) for w, b in zip(heats, blocks)],
                jnp.sum(heats[0] * drive_half, axis=(0, 2)),
            )
            totals = jnp.concatenate([weighted, jnp.sum(heat).reshape(1)])
            totals = jnp.pad(totals[None], ((0, 0), (0, size - half - 1)))
            totals = lax.all_to_all(
                jnp.broadcast_to(totals, (chips * CORES, size)), ALL, split_axis=0, concat_axis=0, tiled=True
            )
            totals = jnp.sum(totals.reshape(chips, CORES, size), axis=0)
            conductivity = totals[:, :half].reshape(columns) / jnp.sum(totals[:, half])
        summed = reduce_far(blocks)
        if sweep == ITERS - 1:
            summed = after(summed, conductivity)
        flux = relax_both * (drive_half + summed)
    first, second = flux[:per], flux[per:]
    mine = jnp.where(core == 0, first, second)
    got = swap(jnp.where(core == 0, second, first), cores)
    both = jnp.concatenate(
        [jnp.where(core == 0, mine, got), jnp.where(core == 0, got, mine)], axis=1
    )
    mode_flux = jnp.transpose(both, (0, 2, 1)).reshape(modes, columns)
    return (mode_flux, conductivity)


def solution(mesh):
    n_rows, n_cols = mesh.shape["row"], mesh.shape["col"]
    planes = depth_of(n_rows)
    chips = Mesh(mesh.devices.reshape(planes, n_rows // planes, n_cols // CORES, CORES), ALL)
    placed = (
        P(ALL, None, None),
        P(ALL, None),
        P(ALL),
        P(ALL),
        P(ALL),
        P(ALL),
        P(ALL, None),
        P(ALL),
    )
    return jax.shard_map(
        shards,
        mesh=chips,
        in_specs=placed,
        out_specs=(P(ALL, None), P()),
        check_vma=False,
    )
```

```python
import functools

import jax
import jax.numpy as jnp
from jax import lax
from jax.experimental import pallas as pl
from jax.experimental.pallas import tpu as pltpu
from jax.sharding import Mesh
from jax.sharding import PartitionSpec as P

ITERS = 3
CORES = 2
STEP = 16
UNROLL = 8
CHUNK = 8
SLOTS = 8
VMEM = 60 * 1024 * 1024
CHIPS = ("z", "y", "x")
ALL = ("z", "y", "x", "core")
NEAR = ("x", "y", "z")


def depth_of(n_rows):
    return min(n for n in range(1, n_rows + 1) if n_rows % n == 0 and n * n >= n_rows)


def far_steps():
    return [(a, 1 << k) for a in NEAR for k in range(1, lax.axis_size(a).bit_length() - 1)]


def near_steps(part):
    turn = part % len(NEAR)
    return [(a, 1) for a in NEAR[turn:] + NEAR[:turn]]


def swap(array, step):
    axis, distance = step
    pairs = [(i, i ^ distance) for i in range(lax.axis_size(axis))]
    return lax.ppermute(array, axis, pairs)


def after(value, *others):
    return lax.optimization_barrier((value,) + others)[0]


def halves(array):
    middle = array.shape[0] // 2
    return array[:middle], array[middle:]


def gather_far(block):
    blocks = [block]
    for step in reversed(far_steps()):
        got = swap(blocks[0] if len(blocks) == 1 else jnp.concatenate(blocks, axis=0), step)
        blocks = blocks + jnp.split(got, len(blocks))
    return blocks


def gather_near(blocks, edges):
    starts = [
        jnp.concatenate([b[low:high] for b in blocks], axis=0) for low, high in zip(edges[:-1], edges[1:])
    ]
    pieces = []
    for part, block in enumerate(lax.optimization_barrier(starts)):
        steps = near_steps(part)
        for step in reversed(steps[1:]):
            block = jnp.concatenate([block, swap(block, step)], axis=0)
        pieces.append((block, swap(block, steps[0])))
    return pieces


def reduce_near(keeps, sends):
    far = 1 << len(far_steps())
    parts = []
    for part, (keep, send) in enumerate(zip(keeps, sends)):
        steps = near_steps(part)
        got = swap(send, steps[0])
        terms = [keep]
        for step in steps[1:]:
            terms.append(got)
            got = swap(sum([halves(t)[1] for t in terms[1:]], halves(terms[0])[1]), step)
            *terms, got = lax.optimization_barrier((*terms, got))
            terms = [halves(t)[0] for t in terms]
        terms = [jnp.split(t, far) for t in (*terms, got)]
        parts.append([sum(t[1:], t[0]) for t in zip(*terms)])
    return [jnp.concatenate(group, axis=0) for group in zip(*parts)]


def reduce_far(blocks):
    for step in far_steps():
        middle = len(blocks) // 2
        send = blocks[middle:]
        got = swap(jnp.concatenate(send, axis=0) if middle > 1 else send[0], step)
        blocks = [b + g for b, g in zip(blocks[:middle], jnp.split(got, middle))]
    return blocks[0]


def sum_far(blocks):
    count = len(blocks)
    for place, step in enumerate(far_steps()):
        bit = count >> (place + 1)
        got = jnp.split(swap(jnp.concatenate(blocks, axis=0), step), count)
        blocks = [b + got[k ^ bit] for k, b in enumerate(blocks)]
    return blocks


def split_kernel(tile_ref, *refs):
    pair_ref = refs[-1]
    size = tile_ref.shape[1]

    @pl.loop(0, STEP // UNROLL)
    def _(group):
        for k in range(UNROLL):
            tile = jnp.transpose(tile_ref[group * UNROLL + k])
            high = tile.astype(jnp.bfloat16)
            low = (tile - high.astype(jnp.float32)).astype(jnp.bfloat16)
            pair_ref[group * UNROLL + k, :size] = high
            pair_ref[group * UNROLL + k, size:] = low


def split_tiles(tiles, place, pairs=None):
    length, size, _ = tiles.shape
    steps = length // STEP
    given = [] if pairs is None else [pairs]
    return pl.pallas_call(
        split_kernel,
        out_shape=jax.ShapeDtypeStruct((CORES * length, 2 * size, size), jnp.bfloat16),
        grid=(steps,),
        in_specs=[pl.BlockSpec((STEP, size, size), lambda i: (i, 0, 0))]
        + [pl.BlockSpec(memory_space=pltpu.HBM)] * len(given),
        out_specs=pl.BlockSpec((STEP, 2 * size, size), lambda i: (place * steps + i, 0, 0)),
        input_output_aliases={1: 0} if given else {},
        compiler_params=pltpu.CompilerParams(vmem_limit_bytes=VMEM),
        cost_estimate=pl.CostEstimate(
            flops=3 * length * size * size, bytes_accessed=8 * length * size * size, transcendentals=0
        ),
    )(tiles, *given)


def apply_kernel(span, skip, counts, has_base, ends_ref, order_ref, row_ref, col_ref, pairs_ref, *refs):
    ends, refs = refs[: len(counts)], refs[len(counts) :]
    base_ref, refs = (refs[0], refs[1:]) if has_base else (None, refs)
    *outs, flux_ref, sum_ref, held_ref, sem, held_sem = refs
    total = order_ref.shape[0]
    start, stop = ends_ref[span], ends_ref[span + 1]
    chunks = (stop - start + CHUNK - 1) // CHUNK

    def fetch(chunk):
        slot = lax.rem(chunk, SLOTS)
        for k in range(CHUNK):
            at = jnp.minimum(start + chunk * CHUNK + k, total - 1)
            pltpu.make_async_copy(
                pairs_ref.at[order_ref[at]], held_ref.at[slot, k], held_sem.at[slot]
            ).start()

    copies = [
        pltpu.make_async_copy(
            piece, flux_ref.at[pl.ds(sum(counts[:k]), counts[k])], sem.at[k]
        )
        for k, piece in enumerate(ends)
    ]
    if has_base:
        copies.append(pltpu.make_async_copy(base_ref, sum_ref, sem.at[len(counts)]))
    for copy in copies:
        copy.start()
    for chunk in range(SLOTS - 1):

        @pl.when(chunk < chunks)
        def _():
            fetch(jnp.int32(chunk))

    if not has_base:
        sum_ref[...] = jnp.zeros_like(sum_ref)
    for copy in copies:
        copy.wait()

    @pl.loop(0, chunks)
    def _(chunk):
        slot = lax.rem(chunk, SLOTS)
        pltpu.make_async_copy(
            pairs_ref.at[pl.ds(0, CHUNK)], held_ref.at[slot], held_sem.at[slot]
        ).wait()

        @pl.when(chunk + SLOTS - 1 < chunks)
        def _():
            fetch(chunk + SLOTS - 1)

        products, rows = [], []
        for k in range(CHUNK):
            at = start + chunk * CHUNK + k
            valid = jnp.where(at < stop, 1.0, 0.0)
            at = jnp.minimum(at, stop - 1)
            flux = flux_ref[col_ref[at]] * valid
            high = flux.astype(jnp.bfloat16)
            low = (flux - high.astype(jnp.float32)).astype(jnp.bfloat16)
            left = jnp.concatenate([high, low], axis=0)
            both = jnp.dot(
                jnp.concatenate([left, left], axis=1),
                held_ref[slot, k],
                preferred_element_type=jnp.float32,
            )
            temps = flux.shape[0]
            products.append(both[:temps] + both[temps:])
            rows.append(row_ref[at] - skip)
        for row, product in zip(rows, products):
            sum_ref[row] += product

    sizes = [out.shape[0] for out in outs]
    copies = [
        pltpu.make_async_copy(sum_ref.at[pl.ds(sum(sizes[:k]), sizes[k])], out, sem.at[k])
        for k, out in enumerate(outs)
    ]
    for copy in copies:
        copy.start()
    for copy in copies:
        copy.wait()


def apply_tiles(span, skip, places, pairs, flux, sizes, share, base=None):
    total, _, size = pairs.shape
    counts = [piece.shape[0] for piece in flux]
    temps = flux[0].shape[1]
    anywhere = pl.BlockSpec(memory_space=pltpu.HBM)
    given = [pairs, *flux] + ([] if base is None else [base])
    return pl.pallas_call(
        functools.partial(apply_kernel, span, skip, counts, base is not None),
        out_shape=[jax.ShapeDtypeStruct((n, temps, size), jnp.float32) for n in sizes],
        grid_spec=pltpu.PrefetchScalarGridSpec(
            num_scalar_prefetch=4,
            grid=(),
            in_specs=[anywhere] * len(given),
            out_specs=[anywhere] * len(sizes),
            scratch_shapes=[
                pltpu.VMEM((sum(counts), temps, size), jnp.float32),
                pltpu.VMEM((sum(sizes), temps, size), jnp.float32),
                pltpu.VMEM((SLOTS, CHUNK) + pairs.shape[1:], jnp.bfloat16),
                pltpu.SemaphoreType.DMA((len(counts) + 1,)),
                pltpu.SemaphoreType.DMA((SLOTS,)),
            ],
        ),
        compiler_params=pltpu.CompilerParams(vmem_limit_bytes=VMEM),
        cost_estimate=pl.CostEstimate(
            flops=int(share * total * size * size * temps * 8),
            bytes_accessed=int(share * total * size * size * 4) + 8 * sum(sizes) * temps * size,
            transcendentals=0,
        ),
    )(*places, *given)


def shards(
    tile_values, tile_owner, tile_row, tile_col, tile_count, relaxation, driving, heat_weight
):
    n_cols = lax.axis_size("x") * CORES
    chips = lax.axis_size(CHIPS)
    length, size, _ = tile_values.shape
    modes, columns = driving.shape
    per = modes // size
    chip_tiles = CORES * per
    num = chips * chip_tiles
    half = columns // CORES
    core = lax.axis_index("core")
    cores = ("core", 1)

    edges = [chip_tiles * k // len(NEAR) for k in range(len(NEAR) + 1)]

    def place(tile):
        chip, inside = tile // chip_tiles, tile % chip_tiles
        away, width = {}, 1
        for axis in reversed(CHIPS):
            n = lax.axis_size(axis)
            away[axis] = ((chip // width) % n) ^ lax.axis_index(axis)
            width *= n
        side, out = jnp.zeros_like(tile), jnp.zeros_like(tile)
        for part in range(len(NEAR)):
            low, high = edges[part], edges[part + 1]
            (first, _), *steps = near_steps(part)
            slot = jnp.zeros_like(tile)
            for axis, distance in steps + far_steps():
                slot = 2 * slot + (away[axis] // distance) % 2
            slot = chips // 2 * low + slot * (high - low) + inside - low
            out = jnp.where(inside >= low, slot, out)
            side = jnp.where(inside >= low, away[first] % 2, side)
        return side, out

    owners = tile_owner[:, 0]
    row_side, row = place((owners // n_cols) * (n_cols * per) + tile_row)
    col_side, col = place(((tile_col // per) * n_cols + owners % n_cols) * per + tile_col % per)
    used = jnp.arange(length, dtype=jnp.int32) < tile_count[0]
    kind = jnp.where(used, jnp.where(col_side == 0, 0, 2 - row_side), 3)
    row = jnp.where(row_side == 1, row, row + num // 2)
    code = (kind * num + row) * num + col
    other_code = swap(code, cores)
    code = jnp.concatenate([code, other_code])
    kind = code // (num * num)
    slots = jnp.arange(CORES * length, dtype=jnp.int32)
    key = kind * (CORES * length) + slots
    rank = jnp.sum((key[None, :] < key[:, None]).astype(jnp.int32), axis=1)
    ends = jnp.sum((kind[None, :] < jnp.arange(4, dtype=jnp.int32)[:, None]).astype(jnp.int32), axis=1)
    sorts = rank[None, :] == slots[:, None]
    order = jnp.sum(jnp.where(sorts, slots[None, :], 0), axis=1)
    code = jnp.sum(jnp.where(sorts, code[None, :] % (num * num), 0), axis=1)
    places = (ends, order, code // num, code % num)

    def by_core(own, other):
        return jnp.concatenate(
            [jnp.where(core == 0, own, other), jnp.where(core == 0, other, own)], axis=0
        )

    drive = jnp.transpose(driving.reshape(per, size, columns), (0, 2, 1))
    relax = relaxation.reshape(per, 1, size)
    heat = heat_weight.reshape(per, 1, size)
    low, high = drive[:, :half], drive[:, half:]
    mine = jnp.where(core == 0, low, high)
    theirs = jnp.where(core == 0, high, low)
    packed = [theirs, jnp.broadcast_to(relax, (per, 8, size)), jnp.broadcast_to(heat, (per, 8, size))]
    got = swap(jnp.concatenate(packed, axis=1), cores)
    tile_values = after(tile_values, got, other_code)
    other_values = swap(tile_values, cores)
    drive_half = by_core(mine, got[:, :half])
    relax_both = by_core(relax, got[:, half : half + 1])
    heat_both = by_core(heat, got[:, half + 8 : half + 9])

    drives = gather_far(drive_half)
    small = gather_far(jnp.concatenate([relax_both, heat_both * relax_both], axis=1))
    relaxes, heats = [s[:, :1] for s in small], [s[:, 1:] for s in small]
    pairs = split_tiles(tile_values, 0)
    drives[-1] = after(drives[-1], pairs)
    fluxes = [r * d for r, d in zip(relaxes, drives)]
    sizes = [chips // 2 * (high - low) for low, high in zip(edges[:-1], edges[1:])]
    for sweep in range(ITERS):
        pieces = gather_near(fluxes, edges)
        if sweep == 0:
            pairs = split_tiles(other_values, 1, pairs)
        near, far = [p for p, _ in pieces], [p for _, p in pieces]
        base = apply_tiles(0, 0, places, pairs, near, [num // 2, num // 2], 0.5)
        sends = apply_tiles(1, 0, places, pairs, far, sizes, 0.25, base[0])
        keeps = apply_tiles(2, num // 2, places, pairs, far, sizes, 0.25, base[1])
        blocks = reduce_near(keeps, sends)
        if sweep < ITERS - 1:
            fluxes = [r * (d + s) for r, d, s in zip(relaxes, drives, sum_far(blocks))]
    weighted = sum(
        [jnp.sum(w * b, axis=(0, 2)) for w, b in zip(heats, blocks)],
        jnp.sum(heats[0] * drive_half, axis=(0, 2)),
    )
    totals = jnp.concatenate([weighted, jnp.sum(heat).reshape(1)])
    totals = jnp.pad(totals[None], ((0, 0), (0, size - half - 1)))
    *blocks, totals = lax.optimization_barrier((*blocks, totals))
    totals = lax.all_to_all(
        jnp.broadcast_to(totals, (chips * CORES, size)), ALL, split_axis=0, concat_axis=0, tiled=True
    )
    totals = jnp.sum(totals.reshape(chips, CORES, size), axis=0)
    conductivity = totals[:, :half].reshape(columns) / jnp.sum(totals[:, half])
    flux = relax_both * (drive_half + after(reduce_far(blocks), conductivity))
    first, second = flux[:per], flux[per:]
    mine = jnp.where(core == 0, first, second)
    got = swap(jnp.where(core == 0, second, first), cores)
    both = jnp.concatenate(
        [jnp.where(core == 0, mine, got), jnp.where(core == 0, got, mine)], axis=1
    )
    mode_flux = jnp.transpose(both, (0, 2, 1)).reshape(modes, columns)
    return (mode_flux, conductivity)


def solution(mesh):
    n_rows, n_cols = mesh.shape["row"], mesh.shape["col"]
    planes = depth_of(n_rows)
    chips = Mesh(mesh.devices.reshape(planes, n_rows // planes, n_cols // CORES, CORES), ALL)
    placed = (
        P(ALL, None, None),
        P(ALL, None),
        P(ALL),
        P(ALL),
        P(ALL),
        P(ALL),
        P(ALL, None),
        P(ALL),
    )
    return jax.shard_map(
        shards,
        mesh=chips,
        in_specs=placed,
        out_specs=(P(ALL, None), P()),
        check_vma=False,
    )
```

```python
import functools

import jax
import jax.numpy as jnp
import numpy as np
from jax import lax
from jax.experimental import pallas as pl
from jax.experimental.pallas import tpu as pltpu
from jax.sharding import Mesh
from jax.sharding import PartitionSpec as P

ITERS = 3
CORES = 2
STEP = 16
UNROLL = 8
CHUNK = 8
SLOTS = 8
SPANS = 4
VMEM = 60 * 1024 * 1024
CHIPS = ("z", "y", "x")
ALL = ("z", "y", "x", "core")
AXES = ("x", "y", "z")
PARTS = ((2, ("xzy", "yxz")), (1, ("zyx", "zyx")))


def depth_of(n_rows):
    return min(n for n in range(1, n_rows + 1) if n_rows % n == 0 and n * n >= n_rows)


def far_steps():
    return [(a + a, 1 << k) for a in AXES for k in range(1, lax.axis_size(a).bit_length() - 1)]


def near_steps(part):
    return [(axes, 1) for axes in zip(*PARTS[part][1])]


def swap(array, step):
    axes, distance = step
    sizes = [lax.axis_size(a) for a in CHIPS]
    pairs = []
    for at in np.ndindex(*sizes, CORES):
        to = list(at)
        to[CHIPS.index(axes[at[-1]])] ^= distance
        pairs.append([int(np.ravel_multi_index(i, sizes + [CORES])) for i in (at, to)])
    return lax.ppermute(array, ALL, pairs)


def swap_cores(array):
    return lax.ppermute(array, "core", [(0, 1), (1, 0)])


def after(value, *others):
    return lax.optimization_barrier((value,) + others)[0]


def halves(array):
    middle = array.shape[0] // 2
    return array[:middle], array[middle:]


def gather_far(block):
    blocks = [block]
    for step in reversed(far_steps()):
        got = swap(blocks[0] if len(blocks) == 1 else jnp.concatenate(blocks, axis=0), step)
        blocks = blocks + jnp.split(got, len(blocks))
    return blocks


def gather_near(blocks, edges):
    starts = [
        jnp.concatenate([b[low:high] for b in blocks], axis=0) for low, high in zip(edges[:-1], edges[1:])
    ]
    starts = lax.optimization_barrier(starts)
    got = [swap(block, near_steps(part)[-1]) for part, block in enumerate(starts)]
    pieces = []
    for part, (block, more) in enumerate(zip(starts, lax.optimization_barrier(got))):
        block = jnp.concatenate([block, more], axis=0)
        steps = near_steps(part)
        for step in reversed(steps[1:-1]):
            block = jnp.concatenate([block, swap(block, step)], axis=0)
        pieces.append((block, swap(block, steps[0])))
    return pieces


def reduce_near(keeps, sends):
    far = 1 << len(far_steps())
    parts = []
    for part, (keep, send) in enumerate(zip(keeps, sends)):
        steps = near_steps(part)
        got = swap(send, steps[0])
        terms = [keep]
        for step in steps[1:]:
            terms.append(got)
            got = swap(sum([halves(t)[1] for t in terms[1:]], halves(terms[0])[1]), step)
            *terms, got = lax.optimization_barrier((*terms, got))
            terms = [halves(t)[0] for t in terms]
        terms = [jnp.split(t, far) for t in (*terms, got)]
        parts.append([sum(t[1:], t[0]) for t in zip(*terms)])
    return [jnp.concatenate(group, axis=0) for group in zip(*parts)]


def reduce_far(blocks, beside):
    for step in far_steps():
        middle = len(blocks) // 2
        send = blocks[middle:]
        got = swap(jnp.concatenate(send, axis=0) if middle > 1 else send[0], step)
        got = after(got, beside)
        blocks = [b + g for b, g in zip(blocks[:middle], jnp.split(got, middle))]
    return blocks[0]


def sum_far(blocks):
    count = len(blocks)
    for place, step in enumerate(far_steps()):
        bit = count >> (place + 1)
        got = jnp.split(swap(jnp.concatenate(blocks, axis=0), step), count)
        blocks = [b + got[k ^ bit] for k, b in enumerate(blocks)]
    return blocks


def split_kernel(tile_ref, *refs):
    pair_ref = refs[-1]
    size = tile_ref.shape[1]

    @pl.loop(0, STEP // UNROLL)
    def _(group):
        for k in range(UNROLL):
            tile = jnp.transpose(tile_ref[group * UNROLL + k])
            high = tile.astype(jnp.bfloat16)
            low = (tile - high.astype(jnp.float32)).astype(jnp.bfloat16)
            pair_ref[group * UNROLL + k, :size] = high
            pair_ref[group * UNROLL + k, size:] = low


def split_tiles(tiles, place, pairs=None):
    length, size, _ = tiles.shape
    steps = length // STEP
    given = [] if pairs is None else [pairs]
    return pl.pallas_call(
        split_kernel,
        out_shape=jax.ShapeDtypeStruct((CORES * length, 2 * size, size), jnp.bfloat16),
        grid=(steps,),
        in_specs=[pl.BlockSpec((STEP, size, size), lambda i: (i, 0, 0))]
        + [pl.BlockSpec(memory_space=pltpu.HBM)] * len(given),
        out_specs=pl.BlockSpec((STEP, 2 * size, size), lambda i: (place * steps + i, 0, 0)),
        input_output_aliases={1: 0} if given else {},
        compiler_params=pltpu.CompilerParams(vmem_limit_bytes=VMEM),
        cost_estimate=pl.CostEstimate(
            flops=3 * length * size * size, bytes_accessed=8 * length * size * size, transcendentals=0
        ),
    )(tiles, *given)


def apply_kernel(span, skip, counts, has_base, places_ref, pairs_ref, *refs):
    ends, refs = refs[: len(counts)], refs[len(counts) :]
    base_ref, refs = (refs[0], refs[1:]) if has_base else (None, refs)
    *outs, flux_ref, sum_ref, held_ref, sem, held_sem = refs
    total = pairs_ref.shape[0]
    start, stop = places_ref[span], places_ref[span + 1]
    chunks = (stop - start + CHUNK - 1) // CHUNK

    def fetch(chunk):
        slot = lax.rem(chunk, SLOTS)
        for k in range(CHUNK):
            at = jnp.minimum(start + chunk * CHUNK + k, total - 1)
            pltpu.make_async_copy(
                pairs_ref.at[places_ref[SPANS + at]], held_ref.at[slot, k], held_sem.at[slot]
            ).start()

    copies = [
        pltpu.make_async_copy(
            piece, flux_ref.at[pl.ds(sum(counts[:k]), counts[k])], sem.at[k]
        )
        for k, piece in enumerate(ends)
    ]
    if has_base:
        copies.append(pltpu.make_async_copy(base_ref, sum_ref, sem.at[len(counts)]))
    for copy in copies:
        copy.start()
    for chunk in range(SLOTS - 1):

        @pl.when(chunk < chunks)
        def _():
            fetch(jnp.int32(chunk))

    if not has_base:
        sum_ref[...] = jnp.zeros_like(sum_ref)
    for copy in copies:
        copy.wait()

    @pl.loop(0, chunks)
    def _(chunk):
        slot = lax.rem(chunk, SLOTS)
        pltpu.make_async_copy(
            pairs_ref.at[pl.ds(0, CHUNK)], held_ref.at[slot], held_sem.at[slot]
        ).wait()

        @pl.when(chunk + SLOTS - 1 < chunks)
        def _():
            fetch(chunk + SLOTS - 1)

        products, rows = [], []
        for k in range(CHUNK):
            at = start + chunk * CHUNK + k
            valid = jnp.where(at < stop, 1.0, 0.0)
            at = jnp.minimum(at, stop - 1)
            flux = flux_ref[places_ref[SPANS + 2 * total + at]] * valid
            high = flux.astype(jnp.bfloat16)
            low = (flux - high.astype(jnp.float32)).astype(jnp.bfloat16)
            left = jnp.concatenate([high, low], axis=0)
            both = jnp.dot(
                jnp.concatenate([left, left], axis=1),
                held_ref[slot, k],
                preferred_element_type=jnp.float32,
            )
            temps = flux.shape[0]
            products.append(both[:temps] + both[temps:])
            rows.append(places_ref[SPANS + total + at] - skip)
        for row, product in zip(rows, products):
            sum_ref[row] += product

    sizes = [out.shape[0] for out in outs]
    copies = [
        pltpu.make_async_copy(sum_ref.at[pl.ds(sum(sizes[:k]), sizes[k])], out, sem.at[k])
        for k, out in enumerate(outs)
    ]
    for copy in copies:
        copy.start()
    for copy in copies:
        copy.wait()


def apply_tiles(span, skip, places, pairs, flux, sizes, share, base=None):
    total, _, size = pairs.shape
    counts = [piece.shape[0] for piece in flux]
    temps = flux[0].shape[1]
    anywhere = pl.BlockSpec(memory_space=pltpu.HBM)
    given = [pairs, *flux] + ([] if base is None else [base])
    return pl.pallas_call(
        functools.partial(apply_kernel, span, skip, counts, base is not None),
        out_shape=[jax.ShapeDtypeStruct((n, temps, size), jnp.float32) for n in sizes],
        grid_spec=pltpu.PrefetchScalarGridSpec(
            num_scalar_prefetch=1,
            grid=(),
            in_specs=[anywhere] * len(given),
            out_specs=[anywhere] * len(sizes),
            scratch_shapes=[
                pltpu.VMEM((sum(counts), temps, size), jnp.float32),
                pltpu.VMEM((sum(sizes), temps, size), jnp.float32),
                pltpu.VMEM((SLOTS, CHUNK) + pairs.shape[1:], jnp.bfloat16),
                pltpu.SemaphoreType.DMA((len(counts) + 1,)),
                pltpu.SemaphoreType.DMA((SLOTS,)),
            ],
        ),
        compiler_params=pltpu.CompilerParams(vmem_limit_bytes=VMEM),
        cost_estimate=pl.CostEstimate(
            flops=int(share * total * size * size * temps * 8),
            bytes_accessed=int(share * total * size * size * 4) + 8 * sum(sizes) * temps * size,
            transcendentals=0,
        ),
    )(places, *given)


def shards(
    tile_values, tile_owner, tile_row, tile_col, tile_count, relaxation, driving, heat_weight
):
    n_cols = lax.axis_size("x") * CORES
    chips = lax.axis_size(CHIPS)
    length, size, _ = tile_values.shape
    modes, columns = driving.shape
    per = modes // size
    chip_tiles = CORES * per
    num = chips * chip_tiles
    half = columns // CORES
    core = lax.axis_index("core")

    thirds = [sum(third for third, _ in PARTS[:k]) for k in range(len(PARTS) + 1)]
    edges = [chip_tiles * third // thirds[-1] for third in thirds]

    def place(tile):
        chip, inside = tile // chip_tiles, tile % chip_tiles
        away, width = {}, 1
        for axis in reversed(CHIPS):
            n = lax.axis_size(axis)
            away[axis] = ((chip // width) % n) ^ lax.axis_index(axis)
            width *= n
        side, out = jnp.zeros_like(tile), jnp.zeros_like(tile)
        for part in range(len(PARTS)):
            low, high = edges[part], edges[part + 1]
            bits = [
                (jnp.where(core == 0, away[axes[0]], away[axes[1]]) // distance) % 2
                for axes, distance in near_steps(part) + far_steps()
            ]
            slot = jnp.zeros_like(tile)
            for bit in bits[1:]:
                slot = 2 * slot + bit
            slot = chips // 2 * low + slot * (high - low) + inside - low
            out = jnp.where(inside >= low, slot, out)
            side = jnp.where(inside >= low, bits[0], side)
        return side, out

    owners = tile_owner[:, 0]
    row = (owners // n_cols) * (n_cols * per) + tile_row
    col = ((tile_col // per) * n_cols + owners % n_cols) * per + tile_col % per
    used = jnp.arange(length, dtype=jnp.int32) < tile_count[0]
    code = jnp.where(used, row * num + col, num * num)
    other_code = swap_cores(code)
    code = jnp.concatenate([code, other_code])
    row_side, row = place(code // num % num)
    col_side, col = place(code % num)
    kind = jnp.where(code < num * num, jnp.where(col_side == 0, 0, 2 - row_side), 3)
    row = jnp.where(row_side == 1, row, row + num // 2)
    slots = jnp.arange(CORES * length, dtype=jnp.int32)
    key = kind * (CORES * length) + slots
    rank = jnp.sum((key[None, :] < key[:, None]).astype(jnp.int32), axis=1)
    ends = jnp.sum((kind[None, :] < jnp.arange(SPANS, dtype=jnp.int32)[:, None]).astype(jnp.int32), axis=1)
    sorts = rank[None, :] == slots[:, None]
    order = jnp.sum(jnp.where(sorts, slots[None, :], 0), axis=1)
    code = jnp.sum(jnp.where(sorts, (row * num + col)[None, :], 0), axis=1)
    places = jnp.concatenate([ends, order, code // num, code % num])

    def by_core(own, other):
        return jnp.concatenate(
            [jnp.where(core == 0, own, other), jnp.where(core == 0, other, own)], axis=0
        )

    drive = jnp.transpose(driving.reshape(per, size, columns), (0, 2, 1))
    relax = relaxation.reshape(per, 1, size)
    heat = heat_weight.reshape(per, 1, size)
    low, high = drive[:, :half], drive[:, half:]
    mine = jnp.where(core == 0, low, high)
    theirs = jnp.where(core == 0, high, low)
    packed = [theirs, jnp.broadcast_to(relax, (per, 8, size)), jnp.broadcast_to(heat, (per, 8, size))]
    got = swap_cores(jnp.concatenate(packed, axis=1))
    tile_values = after(tile_values, got, other_code)
    other_values = swap_cores(tile_values)
    drive_half = by_core(mine, got[:, :half])
    relax_both = by_core(relax, got[:, half : half + 1])
    heat_both = by_core(heat, got[:, half + 8 : half + 9])

    drives = gather_far(drive_half)
    small = gather_far(jnp.concatenate([relax_both, heat_both * relax_both], axis=1))
    relaxes, heats = [s[:, :1] for s in small], [s[:, 1:] for s in small]
    pairs = split_tiles(tile_values, 0)
    drives[-1] = after(drives[-1], pairs)
    fluxes = [r * d for r, d in zip(relaxes, drives)]
    sizes = [chips // 2 * (high - low) for low, high in zip(edges[:-1], edges[1:])]
    for sweep in range(ITERS):
        pieces = gather_near(fluxes, edges)
        if sweep == 0:
            pairs = split_tiles(other_values, 1, pairs)
        near, far = [p for p, _ in pieces], [p for _, p in pieces]
        base = apply_tiles(0, 0, places, pairs, near, [num // 2, num // 2], 0.5)
        sends = apply_tiles(1, 0, places, pairs, far, sizes, 0.25, base[0])
        keeps = apply_tiles(2, num // 2, places, pairs, far, sizes, 0.25, base[1])
        blocks = reduce_near(keeps, sends)
        if sweep < ITERS - 1:
            fluxes = [r * (d + s) for r, d, s in zip(relaxes, drives, sum_far(blocks))]
    weighted = sum(
        [jnp.sum(w * b, axis=(0, 2)) for w, b in zip(heats, blocks)],
        jnp.sum(heats[0] * drive_half, axis=(0, 2)),
    )
    totals = jnp.concatenate([weighted, jnp.sum(heat).reshape(1)])
    totals = jnp.pad(totals[None], ((0, 0), (0, size - half - 1)))
    totals = lax.all_to_all(
        jnp.broadcast_to(totals, (chips * CORES, size)), ALL, split_axis=0, concat_axis=0, tiled=True
    )
    totals = jnp.sum(totals.reshape(chips, CORES, size), axis=0)
    conductivity = totals[:, :half].reshape(columns) / jnp.sum(totals[:, half])
    flux = relax_both * (drive_half + reduce_far(blocks, conductivity))
    first, second = flux[:per], flux[per:]
    mine = jnp.where(core == 0, first, second)
    got = swap_cores(jnp.where(core == 0, second, first))
    both = jnp.concatenate(
        [jnp.where(core == 0, mine, got), jnp.where(core == 0, got, mine)], axis=1
    )
    mode_flux = jnp.transpose(both, (0, 2, 1)).reshape(modes, columns)
    return (mode_flux, conductivity)


def solution(mesh):
    n_rows, n_cols = mesh.shape["row"], mesh.shape["col"]
    planes = depth_of(n_rows)
    chips = Mesh(mesh.devices.reshape(planes, n_rows // planes, n_cols // CORES, CORES), ALL)
    placed = (
        P(ALL, None, None),
        P(ALL, None),
        P(ALL),
        P(ALL),
        P(ALL),
        P(ALL),
        P(ALL, None),
        P(ALL),
    )
    return jax.shard_map(
        shards,
        mesh=chips,
        in_specs=placed,
        out_specs=(P(ALL, None), P()),
        check_vma=False,
    )
```

```python
import functools

import jax
import jax.numpy as jnp
from jax import lax
from jax.experimental import pallas as pl
from jax.experimental.pallas import tpu as pltpu
from jax.sharding import Mesh
from jax.sharding import PartitionSpec as P

ITERS = 3
CORES = 2
STEP = 16
UNROLL = 8
CHUNK = 8
SLOTS = 8
SPANS = 4
VMEM = 60 * 1024 * 1024
CHIPS = ("z", "y", "x")
ALL = ("z", "y", "x", "core")
NEAR = ("x", "y", "z")


def depth_of(n_rows):
    return min(n for n in range(1, n_rows + 1) if n_rows % n == 0 and n * n >= n_rows)


def far_steps():
    return [(a, 1 << k) for a in NEAR for k in range(1, lax.axis_size(a).bit_length() - 1)]


def near_steps(part):
    turn = part % len(NEAR)
    return [(a, 1) for a in NEAR[turn:] + NEAR[:turn]]


def label(place):
    return place ^ (place >> 1)


def swap(array, step):
    axis, distance = step
    at = {label(i): i for i in range(lax.axis_size(axis))}
    return lax.ppermute(array, axis, [(i, at[n ^ distance]) for n, i in at.items()])


def after(value, *others):
    return lax.optimization_barrier((value,) + others)[0]


def halves(array):
    middle = array.shape[0] // 2
    return array[:middle], array[middle:]


def gather_far(block):
    blocks = [block]
    for step in reversed(far_steps()):
        got = swap(blocks[0] if len(blocks) == 1 else jnp.concatenate(blocks, axis=0), step)
        blocks = blocks + jnp.split(got, len(blocks))
    return blocks


def gather_near(blocks, edges):
    starts = [
        jnp.concatenate([b[low:high] for b in blocks], axis=0) for low, high in zip(edges[:-1], edges[1:])
    ]
    pieces = []
    for part, block in enumerate(lax.optimization_barrier(starts)):
        steps = near_steps(part)
        for step in reversed(steps[1:]):
            block = jnp.concatenate([block, swap(block, step)], axis=0)
        pieces.append((block, swap(block, steps[0])))
    return pieces


def reduce_near(keeps, sends):
    far = 1 << len(far_steps())
    parts = []
    for part, (keep, send) in enumerate(zip(keeps, sends)):
        steps = near_steps(part)
        got = swap(send, steps[0])
        terms = [keep]
        for step in steps[1:]:
            terms.append(got)
            got = swap(sum([halves(t)[1] for t in terms[1:]], halves(terms[0])[1]), step)
            *terms, got = lax.optimization_barrier((*terms, got))
            terms = [halves(t)[0] for t in terms]
        terms = [jnp.split(t, far) for t in (*terms, got)]
        parts.append([sum(t[1:], t[0]) for t in zip(*terms)])
    return [jnp.concatenate(group, axis=0) for group in zip(*parts)]


def reduce_far(blocks):
    for step in far_steps():
        middle = len(blocks) // 2
        send = blocks[middle:]
        got = swap(jnp.concatenate(send, axis=0) if middle > 1 else send[0], step)
        blocks = [b + g for b, g in zip(blocks[:middle], jnp.split(got, middle))]
    return blocks[0]


def sum_far(blocks):
    count = len(blocks)
    for place, step in enumerate(far_steps()):
        bit = count >> (place + 1)
        got = jnp.split(swap(jnp.concatenate(blocks, axis=0), step), count)
        blocks = [b + got[k ^ bit] for k, b in enumerate(blocks)]
    return blocks


def split_kernel(tile_ref, *refs):
    pair_ref = refs[-1]
    size = tile_ref.shape[1]

    @pl.loop(0, STEP // UNROLL)
    def _(group):
        for k in range(UNROLL):
            tile = jnp.transpose(tile_ref[group * UNROLL + k])
            high = tile.astype(jnp.bfloat16)
            low = (tile - high.astype(jnp.float32)).astype(jnp.bfloat16)
            pair_ref[group * UNROLL + k, :size] = high
            pair_ref[group * UNROLL + k, size:] = low


def split_tiles(tiles, place, pairs=None):
    length, size, _ = tiles.shape
    steps = length // STEP
    given = [] if pairs is None else [pairs]
    return pl.pallas_call(
        split_kernel,
        out_shape=jax.ShapeDtypeStruct((CORES * length, 2 * size, size), jnp.bfloat16),
        grid=(steps,),
        in_specs=[pl.BlockSpec((STEP, size, size), lambda i: (i, 0, 0))]
        + [pl.BlockSpec(memory_space=pltpu.HBM)] * len(given),
        out_specs=pl.BlockSpec((STEP, 2 * size, size), lambda i: (place * steps + i, 0, 0)),
        input_output_aliases={1: 0} if given else {},
        compiler_params=pltpu.CompilerParams(vmem_limit_bytes=VMEM),
        cost_estimate=pl.CostEstimate(
            flops=3 * length * size * size, bytes_accessed=8 * length * size * size, transcendentals=0
        ),
    )(tiles, *given)


def apply_kernel(span, skip, counts, has_base, places_ref, pairs_ref, *refs):
    ends, refs = refs[: len(counts)], refs[len(counts) :]
    base_ref, refs = (refs[0], refs[1:]) if has_base else (None, refs)
    *outs, flux_ref, sum_ref, held_ref, sem, held_sem = refs
    total = pairs_ref.shape[0]
    start, stop = places_ref[span], places_ref[span + 1]
    chunks = (stop - start + CHUNK - 1) // CHUNK

    def fetch(chunk):
        slot = lax.rem(chunk, SLOTS)
        for k in range(CHUNK):
            at = jnp.minimum(start + chunk * CHUNK + k, total - 1)
            pltpu.make_async_copy(
                pairs_ref.at[places_ref[SPANS + at]], held_ref.at[slot, k], held_sem.at[slot]
            ).start()

    copies = [
        pltpu.make_async_copy(
            piece, flux_ref.at[pl.ds(sum(counts[:k]), counts[k])], sem.at[k]
        )
        for k, piece in enumerate(ends)
    ]
    if has_base:
        copies.append(pltpu.make_async_copy(base_ref, sum_ref, sem.at[len(counts)]))
    for copy in copies:
        copy.start()
    for chunk in range(SLOTS - 1):

        @pl.when(chunk < chunks)
        def _():
            fetch(jnp.int32(chunk))

    if not has_base:
        sum_ref[...] = jnp.zeros_like(sum_ref)
    for copy in copies:
        copy.wait()

    @pl.loop(0, chunks)
    def _(chunk):
        slot = lax.rem(chunk, SLOTS)
        pltpu.make_async_copy(
            pairs_ref.at[pl.ds(0, CHUNK)], held_ref.at[slot], held_sem.at[slot]
        ).wait()

        @pl.when(chunk + SLOTS - 1 < chunks)
        def _():
            fetch(chunk + SLOTS - 1)

        products, rows = [], []
        for k in range(CHUNK):
            at = start + chunk * CHUNK + k
            valid = jnp.where(at < stop, 1.0, 0.0)
            at = jnp.minimum(at, stop - 1)
            flux = flux_ref[places_ref[SPANS + 2 * total + at]] * valid
            high = flux.astype(jnp.bfloat16)
            low = (flux - high.astype(jnp.float32)).astype(jnp.bfloat16)
            left = jnp.concatenate([high, low], axis=0)
            both = jnp.dot(
                jnp.concatenate([left, left], axis=1),
                held_ref[slot, k],
                preferred_element_type=jnp.float32,
            )
            temps = flux.shape[0]
            products.append(both[:temps] + both[temps:])
            rows.append(places_ref[SPANS + total + at] - skip)
        for row, product in zip(rows, products):
            sum_ref[row] += product

    sizes = [out.shape[0] for out in outs]
    copies = [
        pltpu.make_async_copy(sum_ref.at[pl.ds(sum(sizes[:k]), sizes[k])], out, sem.at[k])
        for k, out in enumerate(outs)
    ]
    for copy in copies:
        copy.start()
    for copy in copies:
        copy.wait()


def apply_tiles(span, skip, places, pairs, flux, sizes, share, base=None, vmem=VMEM):
    total, _, size = pairs.shape
    counts = [piece.shape[0] for piece in flux]
    temps = flux[0].shape[1]
    anywhere = pl.BlockSpec(memory_space=pltpu.HBM)
    given = [pairs, *flux] + ([] if base is None else [base])
    return pl.pallas_call(
        functools.partial(apply_kernel, span, skip, counts, base is not None),
        out_shape=[jax.ShapeDtypeStruct((n, temps, size), jnp.float32) for n in sizes],
        grid_spec=pltpu.PrefetchScalarGridSpec(
            num_scalar_prefetch=1,
            grid=(),
            in_specs=[anywhere] * len(given),
            out_specs=[anywhere] * len(sizes),
            scratch_shapes=[
                pltpu.VMEM((sum(counts), temps, size), jnp.float32),
                pltpu.VMEM((sum(sizes), temps, size), jnp.float32),
                pltpu.VMEM((SLOTS, CHUNK) + pairs.shape[1:], jnp.bfloat16),
                pltpu.SemaphoreType.DMA((len(counts) + 1,)),
                pltpu.SemaphoreType.DMA((SLOTS,)),
            ],
        ),
        compiler_params=pltpu.CompilerParams(vmem_limit_bytes=vmem),
        cost_estimate=pl.CostEstimate(
            flops=int(share * total * size * size * temps * 8),
            bytes_accessed=int(share * total * size * size * 4) + 8 * sum(sizes) * temps * size,
            transcendentals=0,
        ),
    )(places, *given)


def shards(
    tile_values, tile_owner, tile_row, tile_col, tile_count, relaxation, driving, heat_weight
):
    n_cols = lax.axis_size("x") * CORES
    chips = lax.axis_size(CHIPS)
    length, size, _ = tile_values.shape
    modes, columns = driving.shape
    per = modes // size
    chip_tiles = CORES * per
    num = chips * chip_tiles
    half = columns // CORES
    core = lax.axis_index("core")
    cores = ("core", 1)

    edges = [chip_tiles * k // len(NEAR) for k in range(len(NEAR) + 1)]

    def place(tile):
        chip, inside = tile // chip_tiles, tile % chip_tiles
        away, width = {}, 1
        for axis in reversed(CHIPS):
            n = lax.axis_size(axis)
            away[axis] = label((chip // width) % n) ^ label(lax.axis_index(axis))
            width *= n
        side, out = jnp.zeros_like(tile), jnp.zeros_like(tile)
        for part in range(len(NEAR)):
            low, high = edges[part], edges[part + 1]
            (first, _), *steps = near_steps(part)
            slot = jnp.zeros_like(tile)
            for axis, distance in steps + far_steps():
                slot = 2 * slot + (away[axis] // distance) % 2
            slot = chips // 2 * low + slot * (high - low) + inside - low
            out = jnp.where(inside >= low, slot, out)
            side = jnp.where(inside >= low, away[first] % 2, side)
        return side, out

    owners = tile_owner[:, 0]
    row_side, row = place((owners // n_cols) * (n_cols * per) + tile_row)
    col_side, col = place(((tile_col // per) * n_cols + owners % n_cols) * per + tile_col % per)
    used = jnp.arange(length, dtype=jnp.int32) < tile_count[0]
    kind = jnp.where(used, jnp.where(col_side == 0, 0, 2 - row_side), 3)
    row = jnp.where(row_side == 1, row, row + num // 2)
    code = (kind * num + row) * num + col
    other_code = swap(code, cores)
    code = jnp.concatenate([code, other_code])
    kind = code // (num * num)
    slots = jnp.arange(CORES * length, dtype=jnp.int32)
    key = kind * (CORES * length) + slots
    rank = jnp.sum((key[None, :] < key[:, None]).astype(jnp.int32), axis=1)
    ends = jnp.sum((kind[None, :] < jnp.arange(SPANS, dtype=jnp.int32)[:, None]).astype(jnp.int32), axis=1)
    sorts = rank[None, :] == slots[:, None]
    order = jnp.sum(jnp.where(sorts, slots[None, :], 0), axis=1)
    code = jnp.sum(jnp.where(sorts, code[None, :] % (num * num), 0), axis=1)
    places = jnp.concatenate([ends, order, code // num, code % num])

    def by_core(own, other):
        return jnp.concatenate(
            [jnp.where(core == 0, own, other), jnp.where(core == 0, other, own)], axis=0
        )

    drive = jnp.transpose(driving.reshape(per, size, columns), (0, 2, 1))
    relax = relaxation.reshape(per, 1, size)
    heat = heat_weight.reshape(per, 1, size)
    low, high = drive[:, :half], drive[:, half:]
    mine = jnp.where(core == 0, low, high)
    theirs = jnp.where(core == 0, high, low)
    packed = [theirs, jnp.broadcast_to(relax, (per, 8, size)), jnp.broadcast_to(heat, (per, 8, size))]
    got = swap(jnp.concatenate(packed, axis=1), cores)
    tile_values = after(tile_values, got, other_code)
    other_values = swap(tile_values, cores)
    drive_half = by_core(mine, got[:, :half])
    relax_both = by_core(relax, got[:, half : half + 1])
    heat_both = by_core(heat, got[:, half + 8 : half + 9])

    drives = gather_far(drive_half)
    small = gather_far(jnp.concatenate([relax_both, heat_both * relax_both], axis=1))
    relaxes, heats = [s[:, :1] for s in small], [s[:, 1:] for s in small]
    pairs = split_tiles(tile_values, 0)
    drives[-1] = after(drives[-1], pairs)
    fluxes = [r * d for r, d in zip(relaxes, drives)]
    sizes = [chips // 2 * (high - low) for low, high in zip(edges[:-1], edges[1:])]
    for sweep in range(ITERS):
        pieces = gather_near(fluxes, edges)
        if sweep == 0:
            pairs = split_tiles(other_values, 1, pairs)
        near, far = [p for p, _ in pieces], [p for _, p in pieces]
        base = apply_tiles(0, 0, places, pairs, near, [num // 2, num // 2], 0.5)
        sends = apply_tiles(1, 0, places, pairs, far, sizes, 0.25, base[0], VMEM // 2)
        keeps = apply_tiles(2, num // 2, places, pairs, far, sizes, 0.25, base[1])
        blocks = reduce_near(keeps, sends)
        if sweep < ITERS - 1:
            fluxes = [r * (d + s) for r, d, s in zip(relaxes, drives, sum_far(blocks))]
    weighted = sum(
        [jnp.sum(w * b, axis=(0, 2)) for w, b in zip(heats, blocks)],
        jnp.sum(heats[0] * drive_half, axis=(0, 2)),
    )
    totals = jnp.concatenate([weighted, jnp.sum(heat).reshape(1)])
    totals = jnp.pad(totals[None], ((0, 0), (0, size - half - 1)))
    *blocks, totals = lax.optimization_barrier((*blocks, totals))
    totals = lax.all_to_all(
        jnp.broadcast_to(totals, (chips * CORES, size)), ALL, split_axis=0, concat_axis=0, tiled=True
    )
    totals = jnp.sum(totals.reshape(chips, CORES, size), axis=0)
    conductivity = totals[:, :half].reshape(columns) / jnp.sum(totals[:, half])
    flux = relax_both * (drive_half + after(reduce_far(blocks), conductivity))
    first, second = flux[:per], flux[per:]
    mine = jnp.where(core == 0, first, second)
    got = swap(jnp.where(core == 0, second, first), cores)
    both = jnp.concatenate(
        [jnp.where(core == 0, mine, got), jnp.where(core == 0, got, mine)], axis=1
    )
    mode_flux = jnp.transpose(both, (0, 2, 1)).reshape(modes, columns)
    return (mode_flux, conductivity)


def solution(mesh):
    n_rows, n_cols = mesh.shape["row"], mesh.shape["col"]
    planes = depth_of(n_rows)
    chips = Mesh(mesh.devices.reshape(planes, n_rows // planes, n_cols // CORES, CORES), ALL)
    placed = (
        P(ALL, None, None),
        P(ALL, None),
        P(ALL),
        P(ALL),
        P(ALL),
        P(ALL),
        P(ALL, None),
        P(ALL),
    )
    return jax.shard_map(
        shards,
        mesh=chips,
        in_specs=placed,
        out_specs=(P(ALL, None), P()),
        check_vma=False,
    )
```

```python
import functools

import jax
import jax.numpy as jnp
from jax import lax
from jax.experimental import pallas as pl
from jax.experimental.pallas import tpu as pltpu
from jax.sharding import Mesh
from jax.sharding import PartitionSpec as P

ITERS = 3
CORES = 2
STEP = 16
UNROLL = 8
CHUNK = 8
SLOTS = 8
SPANS = 4
VMEM = 63 * 1024 * 1024
CHIPS = ("z", "y", "x")
ALL = ("z", "y", "x", "core")
NEAR = ("x", "y", "z")


def depth_of(n_rows):
    return min(n for n in range(1, n_rows + 1) if n_rows % n == 0 and n * n >= n_rows)


def far_steps():
    return [(a, 1 << k) for a in NEAR for k in range(1, lax.axis_size(a).bit_length() - 1)]


def near_steps(part):
    turn = part % len(NEAR)
    return [(a, 1) for a in NEAR[turn:] + NEAR[:turn]]


def label(place):
    return place ^ (place >> 1)


def swap(array, step):
    axis, distance = step
    at = {label(i): i for i in range(lax.axis_size(axis))}
    return lax.ppermute(array, axis, [(i, at[n ^ distance]) for n, i in at.items()])


def after(value, *others):
    return lax.optimization_barrier((value,) + others)[0]


def halves(array):
    middle = array.shape[0] // 2
    return array[:middle], array[middle:]


def gather_far(block):
    blocks = [block]
    for step in reversed(far_steps()):
        got = swap(blocks[0] if len(blocks) == 1 else jnp.concatenate(blocks, axis=0), step)
        blocks = blocks + jnp.split(got, len(blocks))
    return blocks


def gather_near(blocks, edges):
    starts = [
        jnp.concatenate([b[low:high] for b in blocks], axis=0) for low, high in zip(edges[:-1], edges[1:])
    ]
    pieces = []
    for part, block in enumerate(lax.optimization_barrier(starts)):
        steps = near_steps(part)
        for step in reversed(steps[1:]):
            block = jnp.concatenate([block, swap(block, step)], axis=0)
        pieces.append((block, swap(block, steps[0])))
    return pieces


def reduce_near(keeps, sends):
    far = 1 << len(far_steps())
    parts = []
    for part, (keep, send) in enumerate(zip(keeps, sends)):
        steps = near_steps(part)
        got = swap(send, steps[0])
        terms = [keep]
        for step in steps[1:]:
            terms.append(got)
            got = swap(sum([halves(t)[1] for t in terms[1:]], halves(terms[0])[1]), step)
            *terms, got = lax.optimization_barrier((*terms, got))
            terms = [halves(t)[0] for t in terms]
        terms = [jnp.split(t, far) for t in (*terms, got)]
        parts.append([sum(t[1:], t[0]) for t in zip(*terms)])
    return [jnp.concatenate(group, axis=0) for group in zip(*parts)]


def reduce_far(blocks):
    for step in far_steps():
        middle = len(blocks) // 2
        send = blocks[middle:]
        got = swap(jnp.concatenate(send, axis=0) if middle > 1 else send[0], step)
        blocks = [b + g for b, g in zip(blocks[:middle], jnp.split(got, middle))]
    return blocks[0]


def sum_far(blocks):
    count = len(blocks)
    for place, step in enumerate(far_steps()):
        bit = count >> (place + 1)
        got = jnp.split(swap(jnp.concatenate(blocks, axis=0), step), count)
        blocks = [b + got[k ^ bit] for k, b in enumerate(blocks)]
    return blocks


def split_kernel(tile_ref, *refs):
    pair_ref = refs[-1]
    size = tile_ref.shape[1]

    @pl.loop(0, STEP // UNROLL)
    def _(group):
        for k in range(UNROLL):
            tile = jnp.transpose(tile_ref[group * UNROLL + k])
            high = tile.astype(jnp.bfloat16)
            low = (tile - high.astype(jnp.float32)).astype(jnp.bfloat16)
            pair_ref[group * UNROLL + k, :size] = high
            pair_ref[group * UNROLL + k, size:] = low


def split_tiles(tiles, place, pairs=None):
    length, size, _ = tiles.shape
    steps = length // STEP
    given = [] if pairs is None else [pairs]
    return pl.pallas_call(
        split_kernel,
        out_shape=jax.ShapeDtypeStruct((CORES * length, 2 * size, size), jnp.bfloat16),
        grid=(steps,),
        in_specs=[pl.BlockSpec((STEP, size, size), lambda i: (i, 0, 0))]
        + [pl.BlockSpec(memory_space=pltpu.HBM)] * len(given),
        out_specs=pl.BlockSpec((STEP, 2 * size, size), lambda i: (place * steps + i, 0, 0)),
        input_output_aliases={1: 0} if given else {},
        compiler_params=pltpu.CompilerParams(vmem_limit_bytes=VMEM),
        cost_estimate=pl.CostEstimate(
            flops=3 * length * size * size, bytes_accessed=8 * length * size * size, transcendentals=0
        ),
    )(tiles, *given)


def apply_kernel(span, skip, counts, has_base, places_ref, pairs_ref, *refs):
    ends, refs = refs[: len(counts)], refs[len(counts) :]
    base_ref, refs = (refs[0], refs[1:]) if has_base else (None, refs)
    *outs, flux_ref, sum_ref, held_ref, sem, held_sem = refs
    total = pairs_ref.shape[0]
    start, stop = places_ref[span], places_ref[span + 1]
    chunks = (stop - start + CHUNK - 1) // CHUNK

    def fetch(chunk):
        slot = lax.rem(chunk, SLOTS)
        for k in range(CHUNK):
            at = jnp.minimum(start + chunk * CHUNK + k, total - 1)
            pltpu.make_async_copy(
                pairs_ref.at[places_ref[SPANS + at]], held_ref.at[slot, k], held_sem.at[slot]
            ).start()

    copies = [
        pltpu.make_async_copy(
            piece, flux_ref.at[pl.ds(sum(counts[:k]), counts[k])], sem.at[k]
        )
        for k, piece in enumerate(ends)
    ]
    if has_base:
        copies.append(pltpu.make_async_copy(base_ref, sum_ref, sem.at[len(counts)]))
    for copy in copies:
        copy.start()
    for chunk in range(SLOTS - 1):

        @pl.when(chunk < chunks)
        def _():
            fetch(jnp.int32(chunk))

    if not has_base:
        sum_ref[...] = jnp.zeros_like(sum_ref)
    for copy in copies:
        copy.wait()

    @pl.loop(0, chunks)
    def _(chunk):
        slot = lax.rem(chunk, SLOTS)
        pltpu.make_async_copy(
            pairs_ref.at[pl.ds(0, CHUNK)], held_ref.at[slot], held_sem.at[slot]
        ).wait()

        @pl.when(chunk + SLOTS - 1 < chunks)
        def _():
            fetch(chunk + SLOTS - 1)

        products, rows = [], []
        for k in range(CHUNK):
            at = start + chunk * CHUNK + k
            valid = jnp.where(at < stop, 1.0, 0.0)
            at = jnp.minimum(at, stop - 1)
            flux = flux_ref[places_ref[SPANS + 2 * total + at]] * valid
            high = flux.astype(jnp.bfloat16)
            low = (flux - high.astype(jnp.float32)).astype(jnp.bfloat16)
            left = jnp.concatenate([high, low], axis=0)
            both = jnp.dot(
                jnp.concatenate([left, left], axis=1),
                held_ref[slot, k],
                preferred_element_type=jnp.float32,
            )
            temps = flux.shape[0]
            products.append(both[:temps] + both[temps:])
            rows.append(places_ref[SPANS + total + at] - skip)
        for row, product in zip(rows, products):
            sum_ref[row] += product

    sizes = [out.shape[0] for out in outs]
    copies = [
        pltpu.make_async_copy(sum_ref.at[pl.ds(sum(sizes[:k]), sizes[k])], out, sem.at[k])
        for k, out in enumerate(outs)
    ]
    for copy in copies:
        copy.start()
    for copy in copies:
        copy.wait()


def apply_tiles(span, skip, places, pairs, flux, sizes, share, base=None):
    total, _, size = pairs.shape
    counts = [piece.shape[0] for piece in flux]
    temps = flux[0].shape[1]
    anywhere = pl.BlockSpec(memory_space=pltpu.HBM)
    given = [pairs, *flux] + ([] if base is None else [base])
    return pl.pallas_call(
        functools.partial(apply_kernel, span, skip, counts, base is not None),
        out_shape=[jax.ShapeDtypeStruct((n, temps, size), jnp.float32) for n in sizes],
        grid_spec=pltpu.PrefetchScalarGridSpec(
            num_scalar_prefetch=1,
            grid=(),
            in_specs=[anywhere] * len(given),
            out_specs=[anywhere] * len(sizes),
            scratch_shapes=[
                pltpu.VMEM((sum(counts), temps, size), jnp.float32),
                pltpu.VMEM((sum(sizes), temps, size), jnp.float32),
                pltpu.VMEM((SLOTS, CHUNK) + pairs.shape[1:], jnp.bfloat16),
                pltpu.SemaphoreType.DMA((len(counts) + 1,)),
                pltpu.SemaphoreType.DMA((SLOTS,)),
            ],
        ),
        compiler_params=pltpu.CompilerParams(vmem_limit_bytes=VMEM),
        cost_estimate=pl.CostEstimate(
            flops=int(share * total * size * size * temps * 8),
            bytes_accessed=int(share * total * size * size * 4) + 8 * sum(sizes) * temps * size,
            transcendentals=0,
        ),
    )(places, *given)


def shards(
    tile_values, tile_owner, tile_row, tile_col, tile_count, relaxation, driving, heat_weight
):
    n_cols = lax.axis_size("x") * CORES
    chips = lax.axis_size(CHIPS)
    length, size, _ = tile_values.shape
    modes, columns = driving.shape
    per = modes // size
    chip_tiles = CORES * per
    num = chips * chip_tiles
    half = columns // CORES
    core = lax.axis_index("core")
    cores = ("core", 1)

    edges = [chip_tiles * k // len(NEAR) for k in range(len(NEAR) + 1)]

    def place(tile):
        chip, inside = tile // chip_tiles, tile % chip_tiles
        away, width = {}, 1
        for axis in reversed(CHIPS):
            n = lax.axis_size(axis)
            away[axis] = label((chip // width) % n) ^ label(lax.axis_index(axis))
            width *= n
        side, out = jnp.zeros_like(tile), jnp.zeros_like(tile)
        for part in range(len(NEAR)):
            low, high = edges[part], edges[part + 1]
            (first, _), *steps = near_steps(part)
            slot = jnp.zeros_like(tile)
            for axis, distance in steps + far_steps():
                slot = 2 * slot + (away[axis] // distance) % 2
            slot = chips // 2 * low + slot * (high - low) + inside - low
            out = jnp.where(inside >= low, slot, out)
            side = jnp.where(inside >= low, away[first] % 2, side)
        return side, out

    owners = tile_owner[:, 0]
    row_side, row = place((owners // n_cols) * (n_cols * per) + tile_row)
    col_side, col = place(((tile_col // per) * n_cols + owners % n_cols) * per + tile_col % per)
    used = jnp.arange(length, dtype=jnp.int32) < tile_count[0]
    kind = jnp.where(used, jnp.where(col_side == 0, 0, 2 - row_side), 3)
    row = jnp.where(row_side == 1, row, row + num // 2)
    code = (kind * num + row) * num + col
    other_code = swap(code, cores)
    code = jnp.concatenate([code, other_code])
    kind = code // (num * num)
    slots = jnp.arange(CORES * length, dtype=jnp.int32)
    key = kind * (CORES * length) + slots
    rank = jnp.sum((key[None, :] < key[:, None]).astype(jnp.int32), axis=1)
    ends = jnp.sum((kind[None, :] < jnp.arange(SPANS, dtype=jnp.int32)[:, None]).astype(jnp.int32), axis=1)
    sorts = rank[None, :] == slots[:, None]
    order = jnp.sum(jnp.where(sorts, slots[None, :], 0), axis=1)
    code = jnp.sum(jnp.where(sorts, code[None, :] % (num * num), 0), axis=1)
    places = jnp.concatenate([ends, order, code // num, code % num])

    def by_core(own, other):
        return jnp.concatenate(
            [jnp.where(core == 0, own, other), jnp.where(core == 0, other, own)], axis=0
        )

    drive = jnp.transpose(driving.reshape(per, size, columns), (0, 2, 1))
    relax = relaxation.reshape(per, 1, size)
    heat = heat_weight.reshape(per, 1, size)
    low, high = drive[:, :half], drive[:, half:]
    mine = jnp.where(core == 0, low, high)
    theirs = jnp.where(core == 0, high, low)
    packed = [theirs, jnp.broadcast_to(relax, (per, 8, size)), jnp.broadcast_to(heat, (per, 8, size))]
    got = swap(jnp.concatenate(packed, axis=1), cores)
    tile_values = after(tile_values, got, other_code)
    other_values = swap(tile_values, cores)
    drive_half = by_core(mine, got[:, :half])
    relax_both = by_core(relax, got[:, half : half + 1])
    heat_both = by_core(heat, got[:, half + 8 : half + 9])

    drives = gather_far(drive_half)
    small = gather_far(jnp.concatenate([relax_both, heat_both * relax_both], axis=1))
    relaxes, heats = [s[:, :1] for s in small], [s[:, 1:] for s in small]
    pairs = split_tiles(tile_values, 0)
    drives[-1] = after(drives[-1], pairs)
    fluxes = [r * d for r, d in zip(relaxes, drives)]
    sizes = [chips // 2 * (high - low) for low, high in zip(edges[:-1], edges[1:])]
    for sweep in range(ITERS):
        pieces = gather_near(fluxes, edges)
        if sweep == 0:
            pairs = split_tiles(other_values, 1, pairs)
        near, far = [p for p, _ in pieces], [p for _, p in pieces]
        base = apply_tiles(0, 0, places, pairs, near, [num // 2, num // 2], 0.5)
        sends = apply_tiles(1, 0, places, pairs, far, sizes, 0.25, base[0])
        keeps = apply_tiles(2, num // 2, places, pairs, far, sizes, 0.25, base[1])
        blocks = reduce_near(keeps, sends)
        if sweep < ITERS - 1:
            fluxes = [r * (d + s) for r, d, s in zip(relaxes, drives, sum_far(blocks))]
    weighted = sum(
        [jnp.sum(w * b, axis=(0, 2)) for w, b in zip(heats, blocks)],
        jnp.sum(heats[0] * drive_half, axis=(0, 2)),
    )
    totals = jnp.concatenate([weighted, jnp.sum(heat).reshape(1)])
    totals = jnp.pad(totals[None], ((0, 0), (0, size - half - 1)))
    *blocks, totals = lax.optimization_barrier((*blocks, totals))
    totals = lax.all_to_all(
        jnp.broadcast_to(totals, (chips * CORES, size)), ALL, split_axis=0, concat_axis=0, tiled=True
    )
    totals = jnp.sum(totals.reshape(chips, CORES, size), axis=0)
    conductivity = totals[:, :half].reshape(columns) / jnp.sum(totals[:, half])
    flux = relax_both * (drive_half + after(reduce_far(blocks), conductivity))
    first, second = flux[:per], flux[per:]
    mine = jnp.where(core == 0, first, second)
    got = swap(jnp.where(core == 0, second, first), cores)
    both = jnp.concatenate(
        [jnp.where(core == 0, mine, got), jnp.where(core == 0, got, mine)], axis=1
    )
    mode_flux = jnp.transpose(both, (0, 2, 1)).reshape(modes, columns)
    return (mode_flux, conductivity)


def solution(mesh):
    n_rows, n_cols = mesh.shape["row"], mesh.shape["col"]
    planes = depth_of(n_rows)
    chips = Mesh(mesh.devices.reshape(planes, n_rows // planes, n_cols // CORES, CORES), ALL)
    placed = (
        P(ALL, None, None),
        P(ALL, None),
        P(ALL),
        P(ALL),
        P(ALL),
        P(ALL),
        P(ALL, None),
        P(ALL),
    )
    return jax.shard_map(
        shards,
        mesh=chips,
        in_specs=placed,
        out_specs=(P(ALL, None), P()),
        check_vma=False,
    )
```

```python
import functools

import jax
import jax.numpy as jnp
from jax import lax
from jax.experimental import pallas as pl
from jax.experimental.pallas import tpu as pltpu
from jax.sharding import Mesh
from jax.sharding import PartitionSpec as P

ITERS = 3
CORES = 2
STEP = 16
UNROLL = 8
CHUNK = 8
SLOTS = 8
SPANS = 4
VMEM = 60 * 1024 * 1024
CHIPS = ("z", "y", "x")
ALL = ("z", "y", "x", "core")
NEAR = ("x", "y", "z")


def depth_of(n_rows):
    return min(n for n in range(1, n_rows + 1) if n_rows % n == 0 and n * n >= n_rows)


def far_steps():
    return [(a, 1 << k) for a in NEAR for k in range(1, lax.axis_size(a).bit_length() - 1)]


def near_steps(part):
    turn = part % len(NEAR)
    return [(a, 1) for a in NEAR[turn:] + NEAR[:turn]]


def label(place):
    return place ^ (place >> 1)


def swap(array, step):
    axis, distance = step
    at = {label(i): i for i in range(lax.axis_size(axis))}
    return lax.ppermute(array, axis, [(i, at[n ^ distance]) for n, i in at.items()])


def after(value, *others):
    return lax.optimization_barrier((value,) + others)[0]


def halves(array):
    middle = array.shape[0] // 2
    return array[:middle], array[middle:]


def gather_far(block):
    blocks = [block]
    for step in reversed(far_steps()):
        got = swap(blocks[0] if len(blocks) == 1 else jnp.concatenate(blocks, axis=0), step)
        blocks = blocks + jnp.split(got, len(blocks))
    return blocks


def gather_near(blocks, edges):
    starts = [
        jnp.concatenate([b[low:high] for b in blocks], axis=0) for low, high in zip(edges[:-1], edges[1:])
    ]
    pieces = []
    for part, block in enumerate(lax.optimization_barrier(starts)):
        steps = near_steps(part)
        for step in reversed(steps[1:]):
            block = jnp.concatenate([block, swap(block, step)], axis=0)
        pieces.append((block, swap(block, steps[0])))
    return pieces


def reduce_near(keeps, sends):
    far = 1 << len(far_steps())
    parts = []
    for part, (keep, send) in enumerate(zip(keeps, sends)):
        steps = near_steps(part)
        got = swap(send, steps[0])
        terms = [keep]
        for step in steps[1:]:
            terms.append(got)
            got = swap(sum([halves(t)[1] for t in terms[1:]], halves(terms[0])[1]), step)
            *terms, got = lax.optimization_barrier((*terms, got))
            terms = [halves(t)[0] for t in terms]
        terms = [jnp.split(t, far) for t in (*terms, got)]
        parts.append([sum(t[1:], t[0]) for t in zip(*terms)])
    return [jnp.concatenate(group, axis=0) for group in zip(*parts)]


def reduce_far(blocks):
    for step in far_steps():
        middle = len(blocks) // 2
        send = blocks[middle:]
        got = swap(jnp.concatenate(send, axis=0) if middle > 1 else send[0], step)
        blocks = [b + g for b, g in zip(blocks[:middle], jnp.split(got, middle))]
    return blocks[0]


def sum_far(blocks):
    count = len(blocks)
    for place, step in enumerate(far_steps()):
        bit = count >> (place + 1)
        got = jnp.split(swap(jnp.concatenate(blocks, axis=0), step), count)
        blocks = [b + got[k ^ bit] for k, b in enumerate(blocks)]
    return blocks


def split_kernel(tile_ref, *refs):
    pair_ref = refs[-1]
    size = tile_ref.shape[1]

    @pl.loop(0, STEP // UNROLL)
    def _(group):
        for k in range(UNROLL):
            tile = tile_ref[group * UNROLL + k]
            high = tile.astype(jnp.bfloat16)
            low = (tile - high.astype(jnp.float32)).astype(jnp.bfloat16)
            pair_ref[group * UNROLL + k, :, :size] = high
            pair_ref[group * UNROLL + k, :, size:] = low


def split_tiles(tiles, place, pairs=None):
    length, size, _ = tiles.shape
    steps = length // STEP
    given = [] if pairs is None else [pairs]
    return pl.pallas_call(
        split_kernel,
        out_shape=jax.ShapeDtypeStruct((CORES * length, size, 2 * size), jnp.bfloat16),
        grid=(steps,),
        in_specs=[pl.BlockSpec((STEP, size, size), lambda i: (i, 0, 0))]
        + [pl.BlockSpec(memory_space=pltpu.HBM)] * len(given),
        out_specs=pl.BlockSpec((STEP, size, 2 * size), lambda i: (place * steps + i, 0, 0)),
        input_output_aliases={1: 0} if given else {},
        compiler_params=pltpu.CompilerParams(vmem_limit_bytes=VMEM),
        cost_estimate=pl.CostEstimate(
            flops=3 * length * size * size, bytes_accessed=8 * length * size * size, transcendentals=0
        ),
    )(tiles, *given)


def apply_kernel(span, skip, counts, has_base, places_ref, pairs_ref, *refs):
    ends, refs = refs[: len(counts)], refs[len(counts) :]
    base_ref, refs = (refs[0], refs[1:]) if has_base else (None, refs)
    *outs, flux_ref, sum_ref, held_ref, sem, held_sem = refs
    total = pairs_ref.shape[0]
    start, stop = places_ref[span], places_ref[span + 1]
    chunks = (stop - start + CHUNK - 1) // CHUNK

    def fetch(chunk):
        slot = lax.rem(chunk, SLOTS)
        for k in range(CHUNK):
            at = jnp.minimum(start + chunk * CHUNK + k, total - 1)
            pltpu.make_async_copy(
                pairs_ref.at[places_ref[SPANS + at]], held_ref.at[slot, k], held_sem.at[slot]
            ).start()

    copies = [
        pltpu.make_async_copy(
            piece, flux_ref.at[pl.ds(sum(counts[:k]), counts[k])], sem.at[k]
        )
        for k, piece in enumerate(ends)
    ]
    if has_base:
        copies.append(pltpu.make_async_copy(base_ref, sum_ref, sem.at[len(counts)]))
    for copy in copies:
        copy.start()
    for chunk in range(SLOTS - 1):

        @pl.when(chunk < chunks)
        def _():
            fetch(jnp.int32(chunk))

    if not has_base:
        sum_ref[...] = jnp.zeros_like(sum_ref)
    for copy in copies:
        copy.wait()

    @pl.loop(0, chunks)
    def _(chunk):
        slot = lax.rem(chunk, SLOTS)
        pltpu.make_async_copy(
            pairs_ref.at[pl.ds(0, CHUNK)], held_ref.at[slot], held_sem.at[slot]
        ).wait()

        @pl.when(chunk + SLOTS - 1 < chunks)
        def _():
            fetch(chunk + SLOTS - 1)

        products, rows = [], []
        for k in range(CHUNK):
            at = start + chunk * CHUNK + k
            valid = jnp.where(at < stop, 1.0, 0.0)
            at = jnp.minimum(at, stop - 1)
            flux = flux_ref[places_ref[SPANS + 2 * total + at]] * valid
            high = flux.astype(jnp.bfloat16)
            low = (flux - high.astype(jnp.float32)).astype(jnp.bfloat16)
            left = jnp.concatenate([high, low], axis=0)
            both = lax.dot_general(
                jnp.concatenate([left, left], axis=1),
                held_ref[slot, k],
                (((1,), (1,)), ((), ())),
                preferred_element_type=jnp.float32,
            )
            temps = flux.shape[0]
            products.append(both[:temps] + both[temps:])
            rows.append(places_ref[SPANS + total + at] - skip)
        for row, product in zip(rows, products):
            sum_ref[row] += product

    sizes = [out.shape[0] for out in outs]
    copies = [
        pltpu.make_async_copy(sum_ref.at[pl.ds(sum(sizes[:k]), sizes[k])], out, sem.at[k])
        for k, out in enumerate(outs)
    ]
    for copy in copies:
        copy.start()
    for copy in copies:
        copy.wait()


def apply_tiles(span, skip, places, pairs, flux, sizes, share, base=None):
    total, size, _ = pairs.shape
    counts = [piece.shape[0] for piece in flux]
    temps = flux[0].shape[1]
    anywhere = pl.BlockSpec(memory_space=pltpu.HBM)
    given = [pairs, *flux] + ([] if base is None else [base])
    return pl.pallas_call(
        functools.partial(apply_kernel, span, skip, counts, base is not None),
        out_shape=[jax.ShapeDtypeStruct((n, temps, size), jnp.float32) for n in sizes],
        grid_spec=pltpu.PrefetchScalarGridSpec(
            num_scalar_prefetch=1,
            grid=(),
            in_specs=[anywhere] * len(given),
            out_specs=[anywhere] * len(sizes),
            scratch_shapes=[
                pltpu.VMEM((sum(counts), temps, size), jnp.float32),
                pltpu.VMEM((sum(sizes), temps, size), jnp.float32),
                pltpu.VMEM((SLOTS, CHUNK) + pairs.shape[1:], jnp.bfloat16),
                pltpu.SemaphoreType.DMA((len(counts) + 1,)),
                pltpu.SemaphoreType.DMA((SLOTS,)),
            ],
        ),
        compiler_params=pltpu.CompilerParams(vmem_limit_bytes=VMEM),
        cost_estimate=pl.CostEstimate(
            flops=int(share * total * size * size * temps * 8),
            bytes_accessed=int(share * total * size * size * 4) + 8 * sum(sizes) * temps * size,
            transcendentals=0,
        ),
    )(places, *given)


def shards(
    tile_values, tile_owner, tile_row, tile_col, tile_count, relaxation, driving, heat_weight
):
    n_cols = lax.axis_size("x") * CORES
    chips = lax.axis_size(CHIPS)
    length, size, _ = tile_values.shape
    modes, columns = driving.shape
    per = modes // size
    chip_tiles = CORES * per
    num = chips * chip_tiles
    half = columns // CORES
    core = lax.axis_index("core")
    cores = ("core", 1)

    edges = [chip_tiles * k // len(NEAR) for k in range(len(NEAR) + 1)]

    def place(tile):
        chip, inside = tile // chip_tiles, tile % chip_tiles
        away, width = {}, 1
        for axis in reversed(CHIPS):
            n = lax.axis_size(axis)
            away[axis] = label((chip // width) % n) ^ label(lax.axis_index(axis))
            width *= n
        side, out = jnp.zeros_like(tile), jnp.zeros_like(tile)
        for part in range(len(NEAR)):
            low, high = edges[part], edges[part + 1]
            (first, _), *steps = near_steps(part)
            slot = jnp.zeros_like(tile)
            for axis, distance in steps + far_steps():
                slot = 2 * slot + (away[axis] // distance) % 2
            slot = chips // 2 * low + slot * (high - low) + inside - low
            out = jnp.where(inside >= low, slot, out)
            side = jnp.where(inside >= low, away[first] % 2, side)
        return side, out

    owners = tile_owner[:, 0]
    row_side, row = place((owners // n_cols) * (n_cols * per) + tile_row)
    col_side, col = place(((tile_col // per) * n_cols + owners % n_cols) * per + tile_col % per)
    used = jnp.arange(length, dtype=jnp.int32) < tile_count[0]
    kind = jnp.where(used, jnp.where(col_side == 0, 0, 2 - row_side), 3)
    row = jnp.where(row_side == 1, row, row + num // 2)
    code = (kind * num + row) * num + col
    other_code = swap(code, cores)
    code = jnp.concatenate([code, other_code])
    kind = code // (num * num)
    slots = jnp.arange(CORES * length, dtype=jnp.int32)
    key = kind * (CORES * length) + slots
    rank = jnp.sum((key[None, :] < key[:, None]).astype(jnp.int32), axis=1)
    ends = jnp.sum((kind[None, :] < jnp.arange(SPANS, dtype=jnp.int32)[:, None]).astype(jnp.int32), axis=1)
    sorts = rank[None, :] == slots[:, None]
    order = jnp.sum(jnp.where(sorts, slots[None, :], 0), axis=1)
    code = jnp.sum(jnp.where(sorts, code[None, :] % (num * num), 0), axis=1)
    places = jnp.concatenate([ends, order, code // num, code % num])

    def by_core(own, other):
        return jnp.concatenate(
            [jnp.where(core == 0, own, other), jnp.where(core == 0, other, own)], axis=0
        )

    drive = jnp.transpose(driving.reshape(per, size, columns), (0, 2, 1))
    relax = relaxation.reshape(per, 1, size)
    heat = heat_weight.reshape(per, 1, size)
    low, high = drive[:, :half], drive[:, half:]
    mine = jnp.where(core == 0, low, high)
    theirs = jnp.where(core == 0, high, low)
    packed = [theirs, jnp.broadcast_to(relax, (per, 8, size)), jnp.broadcast_to(heat, (per, 8, size))]
    got = swap(jnp.concatenate(packed, axis=1), cores)
    tile_values = after(tile_values, got, other_code)
    other_values = swap(tile_values, cores)
    drive_half = by_core(mine, got[:, :half])
    relax_both = by_core(relax, got[:, half : half + 1])
    heat_both = by_core(heat, got[:, half + 8 : half + 9])

    drives = gather_far(drive_half)
    small = gather_far(jnp.concatenate([relax_both, heat_both * relax_both], axis=1))
    relaxes, heats = [s[:, :1] for s in small], [s[:, 1:] for s in small]
    pairs = split_tiles(tile_values, 0)
    drives[-1] = after(drives[-1], pairs)
    fluxes = [r * d for r, d in zip(relaxes, drives)]
    sizes = [chips // 2 * (high - low) for low, high in zip(edges[:-1], edges[1:])]
    for sweep in range(ITERS):
        pieces = gather_near(fluxes, edges)
        if sweep == 0:
            pairs = split_tiles(other_values, 1, pairs)
        near, far = [p for p, _ in pieces], [p for _, p in pieces]
        base = apply_tiles(0, 0, places, pairs, near, [num // 2, num // 2], 0.5)
        sends = apply_tiles(1, 0, places, pairs, far, sizes, 0.25, base[0])
        keeps = apply_tiles(2, num // 2, places, pairs, far, sizes, 0.25, base[1])
        blocks = reduce_near(keeps, sends)
        if sweep < ITERS - 1:
            fluxes = [r * (d + s) for r, d, s in zip(relaxes, drives, sum_far(blocks))]
    weighted = sum(
        [jnp.sum(w * b, axis=(0, 2)) for w, b in zip(heats, blocks)],
        jnp.sum(heats[0] * drive_half, axis=(0, 2)),
    )
    totals = jnp.concatenate([weighted, jnp.sum(heat).reshape(1)])
    totals = jnp.pad(totals[None], ((0, 0), (0, size - half - 1)))
    *blocks, totals = lax.optimization_barrier((*blocks, totals))
    totals = lax.all_to_all(
        jnp.broadcast_to(totals, (chips * CORES, size)), ALL, split_axis=0, concat_axis=0, tiled=True
    )
    totals = jnp.sum(totals.reshape(chips, CORES, size), axis=0)
    conductivity = totals[:, :half].reshape(columns) / jnp.sum(totals[:, half])
    flux = relax_both * (drive_half + after(reduce_far(blocks), conductivity))
    first, second = flux[:per], flux[per:]
    mine = jnp.where(core == 0, first, second)
    got = swap(jnp.where(core == 0, second, first), cores)
    both = jnp.concatenate(
        [jnp.where(core == 0, mine, got), jnp.where(core == 0, got, mine)], axis=1
    )
    mode_flux = jnp.transpose(both, (0, 2, 1)).reshape(modes, columns)
    return (mode_flux, conductivity)


def solution(mesh):
    n_rows, n_cols = mesh.shape["row"], mesh.shape["col"]
    planes = depth_of(n_rows)
    chips = Mesh(mesh.devices.reshape(planes, n_rows // planes, n_cols // CORES, CORES), ALL)
    placed = (
        P(ALL, None, None),
        P(ALL, None),
        P(ALL),
        P(ALL),
        P(ALL),
        P(ALL),
        P(ALL, None),
        P(ALL),
    )
    return jax.shard_map(
        shards,
        mesh=chips,
        in_specs=placed,
        out_specs=(P(ALL, None), P()),
        check_vma=False,
    )
```

```python
import functools

import jax
import jax.numpy as jnp
import numpy as np
from jax import lax
from jax.experimental import pallas as pl
from jax.experimental.pallas import tpu as pltpu
from jax.sharding import Mesh
from jax.sharding import PartitionSpec as P

ITERS = 3
CORES = 2
STEP = 16
UNROLL = 8
CHUNK = 8
SLOTS = 8
SPANS = 4
VMEM = 60 * 1024 * 1024
CHIPS = ("z", "y", "x")
ALL = ("z", "y", "x", "core")
NEAR = ("x", "y", "z")


def depth_of(n_rows):
    return min(n for n in range(1, n_rows + 1) if n_rows % n == 0 and n * n >= n_rows)


def far_steps():
    return [(a, 1 << k) for a in NEAR for k in range(1, lax.axis_size(a).bit_length() - 1)]


def near_steps(part):
    turn = part % len(NEAR)
    return [(a, 1) for a in NEAR[turn:] + NEAR[:turn]]


def later_moves(part):
    steps = near_steps(part)[1:]
    count = len(steps)
    return [
        [step for place, step in enumerate(steps) if n >> (count - 1 - place) & 1] for n in range(1, 1 << count)
    ]


def label(place):
    return place ^ (place >> 1)


def swap(array, *steps):
    sizes = [lax.axis_size(a) for a in CHIPS]
    pairs = []
    for at in np.ndindex(*sizes):
        to = list(at)
        for axis, distance in steps:
            k = CHIPS.index(axis)
            places = {label(i): i for i in range(sizes[k])}
            to[k] = places[label(to[k]) ^ distance]
        pairs.append([int(np.ravel_multi_index(i, sizes)) for i in (at, to)])
    return lax.ppermute(array, CHIPS, pairs)


def swap_cores(array):
    return lax.ppermute(array, "core", [(0, 1), (1, 0)])


def after(value, *others):
    return lax.optimization_barrier((value,) + others)[0]


def gather_far(block):
    blocks = [block]
    for step in reversed(far_steps()):
        got = swap(blocks[0] if len(blocks) == 1 else jnp.concatenate(blocks, axis=0), step)
        blocks = blocks + jnp.split(got, len(blocks))
    return blocks


def gather_near(blocks, edges):
    starts = [
        jnp.concatenate([b[low:high] for b in blocks], axis=0) for low, high in zip(edges[:-1], edges[1:])
    ]
    pieces = []
    for part, block in enumerate(lax.optimization_barrier(starts)):
        block = jnp.concatenate([block] + [swap(block, *moves) for moves in later_moves(part)], axis=0)
        pieces.append((block, swap(block, near_steps(part)[0])))
    return pieces


def reduce_near(keeps, sends):
    far = 1 << len(far_steps())
    parts = []
    for part, (keep, send) in enumerate(zip(keeps, sends)):
        got = swap(send, near_steps(part)[0])
        moves = later_moves(part)
        length = keep.shape[0] // (1 + len(moves))
        sends = [keep[k * length : (k + 1) * length] + got[k * length : (k + 1) * length] for k in range(1, 1 + len(moves))]
        terms = [swap(send, *steps) for send, steps in zip(sends, moves)]
        keep, got, *terms = lax.optimization_barrier((keep, got, *terms))
        terms = [keep[:length], got[:length]] + terms
        terms = [jnp.split(t, far) for t in terms]
        parts.append([sum(t[1:], t[0]) for t in zip(*terms)])
    return [jnp.concatenate(group, axis=0) for group in zip(*parts)]


def reduce_far(blocks):
    for step in far_steps():
        middle = len(blocks) // 2
        send = blocks[middle:]
        got = swap(jnp.concatenate(send, axis=0) if middle > 1 else send[0], step)
        blocks = [b + g for b, g in zip(blocks[:middle], jnp.split(got, middle))]
    return blocks[0]


def sum_far(blocks):
    count = len(blocks)
    for place, step in enumerate(far_steps()):
        bit = count >> (place + 1)
        got = jnp.split(swap(jnp.concatenate(blocks, axis=0), step), count)
        blocks = [b + got[k ^ bit] for k, b in enumerate(blocks)]
    return blocks


def split_kernel(tile_ref, *refs):
    pair_ref = refs[-1]
    size = tile_ref.shape[1]

    @pl.loop(0, STEP // UNROLL)
    def _(group):
        for k in range(UNROLL):
            tile = jnp.transpose(tile_ref[group * UNROLL + k])
            high = tile.astype(jnp.bfloat16)
            low = (tile - high.astype(jnp.float32)).astype(jnp.bfloat16)
            pair_ref[group * UNROLL + k, :size] = high
            pair_ref[group * UNROLL + k, size:] = low


def split_tiles(tiles, place, pairs=None):
    length, size, _ = tiles.shape
    steps = length // STEP
    given = [] if pairs is None else [pairs]
    return pl.pallas_call(
        split_kernel,
        out_shape=jax.ShapeDtypeStruct((CORES * length, 2 * size, size), jnp.bfloat16),
        grid=(steps,),
        in_specs=[pl.BlockSpec((STEP, size, size), lambda i: (i, 0, 0))]
        + [pl.BlockSpec(memory_space=pltpu.HBM)] * len(given),
        out_specs=pl.BlockSpec((STEP, 2 * size, size), lambda i: (place * steps + i, 0, 0)),
        input_output_aliases={1: 0} if given else {},
        compiler_params=pltpu.CompilerParams(vmem_limit_bytes=VMEM),
        cost_estimate=pl.CostEstimate(
            flops=3 * length * size * size, bytes_accessed=8 * length * size * size, transcendentals=0
        ),
    )(tiles, *given)


def apply_kernel(span, skip, counts, has_base, places_ref, pairs_ref, *refs):
    ends, refs = refs[: len(counts)], refs[len(counts) :]
    base_ref, refs = (refs[0], refs[1:]) if has_base else (None, refs)
    *outs, flux_ref, sum_ref, held_ref, sem, held_sem = refs
    total = pairs_ref.shape[0]
    start, stop = places_ref[span], places_ref[span + 1]
    chunks = (stop - start + CHUNK - 1) // CHUNK

    def fetch(chunk):
        slot = lax.rem(chunk, SLOTS)
        for k in range(CHUNK):
            at = jnp.minimum(start + chunk * CHUNK + k, total - 1)
            pltpu.make_async_copy(
                pairs_ref.at[places_ref[SPANS + at]], held_ref.at[slot, k], held_sem.at[slot]
            ).start()

    copies = [
        pltpu.make_async_copy(
            piece, flux_ref.at[pl.ds(sum(counts[:k]), counts[k])], sem.at[k]
        )
        for k, piece in enumerate(ends)
    ]
    if has_base:
        copies.append(pltpu.make_async_copy(base_ref, sum_ref, sem.at[len(counts)]))
    for copy in copies:
        copy.start()
    for chunk in range(SLOTS - 1):

        @pl.when(chunk < chunks)
        def _():
            fetch(jnp.int32(chunk))

    if not has_base:
        sum_ref[...] = jnp.zeros_like(sum_ref)
    for copy in copies:
        copy.wait()

    @pl.loop(0, chunks)
    def _(chunk):
        slot = lax.rem(chunk, SLOTS)
        pltpu.make_async_copy(
            pairs_ref.at[pl.ds(0, CHUNK)], held_ref.at[slot], held_sem.at[slot]
        ).wait()

        @pl.when(chunk + SLOTS - 1 < chunks)
        def _():
            fetch(chunk + SLOTS - 1)

        products, rows = [], []
        for k in range(CHUNK):
            at = start + chunk * CHUNK + k
            valid = jnp.where(at < stop, 1.0, 0.0)
            at = jnp.minimum(at, stop - 1)
            flux = flux_ref[places_ref[SPANS + 2 * total + at]] * valid
            high = flux.astype(jnp.bfloat16)
            low = (flux - high.astype(jnp.float32)).astype(jnp.bfloat16)
            left = jnp.concatenate([high, low], axis=0)
            both = jnp.dot(
                jnp.concatenate([left, left], axis=1),
                held_ref[slot, k],
                preferred_element_type=jnp.float32,
            )
            temps = flux.shape[0]
            products.append(both[:temps] + both[temps:])
            rows.append(places_ref[SPANS + total + at] - skip)
        for row, product in zip(rows, products):
            sum_ref[row] += product

    sizes = [out.shape[0] for out in outs]
    copies = [
        pltpu.make_async_copy(sum_ref.at[pl.ds(sum(sizes[:k]), sizes[k])], out, sem.at[k])
        for k, out in enumerate(outs)
    ]
    for copy in copies:
        copy.start()
    for copy in copies:
        copy.wait()


def apply_tiles(span, skip, places, pairs, flux, sizes, share, base=None):
    total, _, size = pairs.shape
    counts = [piece.shape[0] for piece in flux]
    temps = flux[0].shape[1]
    anywhere = pl.BlockSpec(memory_space=pltpu.HBM)
    given = [pairs, *flux] + ([] if base is None else [base])
    return pl.pallas_call(
        functools.partial(apply_kernel, span, skip, counts, base is not None),
        out_shape=[jax.ShapeDtypeStruct((n, temps, size), jnp.float32) for n in sizes],
        grid_spec=pltpu.PrefetchScalarGridSpec(
            num_scalar_prefetch=1,
            grid=(),
            in_specs=[anywhere] * len(given),
            out_specs=[anywhere] * len(sizes),
            scratch_shapes=[
                pltpu.VMEM((sum(counts), temps, size), jnp.float32),
                pltpu.VMEM((sum(sizes), temps, size), jnp.float32),
                pltpu.VMEM((SLOTS, CHUNK) + pairs.shape[1:], jnp.bfloat16),
                pltpu.SemaphoreType.DMA((len(counts) + 1,)),
                pltpu.SemaphoreType.DMA((SLOTS,)),
            ],
        ),
        compiler_params=pltpu.CompilerParams(vmem_limit_bytes=VMEM),
        cost_estimate=pl.CostEstimate(
            flops=int(share * total * size * size * temps * 8),
            bytes_accessed=int(share * total * size * size * 4) + 8 * sum(sizes) * temps * size,
            transcendentals=0,
        ),
    )(places, *given)


def shards(
    tile_values, tile_owner, tile_row, tile_col, tile_count, relaxation, driving, heat_weight
):
    n_cols = lax.axis_size("x") * CORES
    chips = lax.axis_size(CHIPS)
    length, size, _ = tile_values.shape
    modes, columns = driving.shape
    per = modes // size
    chip_tiles = CORES * per
    num = chips * chip_tiles
    half = columns // CORES
    core = lax.axis_index("core")

    edges = [chip_tiles * k // len(NEAR) for k in range(len(NEAR) + 1)]

    def place(tile):
        chip, inside = tile // chip_tiles, tile % chip_tiles
        away, width = {}, 1
        for axis in reversed(CHIPS):
            n = lax.axis_size(axis)
            away[axis] = label((chip // width) % n) ^ label(lax.axis_index(axis))
            width *= n
        side, out = jnp.zeros_like(tile), jnp.zeros_like(tile)
        for part in range(len(NEAR)):
            low, high = edges[part], edges[part + 1]
            (first, _), *steps = near_steps(part)
            slot = jnp.zeros_like(tile)
            for axis, distance in steps + far_steps():
                slot = 2 * slot + (away[axis] // distance) % 2
            slot = chips // 2 * low + slot * (high - low) + inside - low
            out = jnp.where(inside >= low, slot, out)
            side = jnp.where(inside >= low, away[first] % 2, side)
        return side, out

    owners = tile_owner[:, 0]
    row_side, row = place((owners // n_cols) * (n_cols * per) + tile_row)
    col_side, col = place(((tile_col // per) * n_cols + owners % n_cols) * per + tile_col % per)
    used = jnp.arange(length, dtype=jnp.int32) < tile_count[0]
    kind = jnp.where(used, jnp.where(col_side == 0, 0, 2 - row_side), 3)
    row = jnp.where(row_side == 1, row, row + num // 2)
    code = (kind * num + row) * num + col
    other_code = swap_cores(code)
    code = jnp.concatenate([code, other_code])
    kind = code // (num * num)
    slots = jnp.arange(CORES * length, dtype=jnp.int32)
    key = kind * (CORES * length) + slots
    rank = jnp.sum((key[None, :] < key[:, None]).astype(jnp.int32), axis=1)
    ends = jnp.sum((kind[None, :] < jnp.arange(SPANS, dtype=jnp.int32)[:, None]).astype(jnp.int32), axis=1)
    sorts = rank[None, :] == slots[:, None]
    order = jnp.sum(jnp.where(sorts, slots[None, :], 0), axis=1)
    code = jnp.sum(jnp.where(sorts, code[None, :] % (num * num), 0), axis=1)
    places = jnp.concatenate([ends, order, code // num, code % num])

    def by_core(own, other):
        return jnp.concatenate(
            [jnp.where(core == 0, own, other), jnp.where(core == 0, other, own)], axis=0
        )

    drive = jnp.transpose(driving.reshape(per, size, columns), (0, 2, 1))
    relax = relaxation.reshape(per, 1, size)
    heat = heat_weight.reshape(per, 1, size)
    low, high = drive[:, :half], drive[:, half:]
    mine = jnp.where(core == 0, low, high)
    theirs = jnp.where(core == 0, high, low)
    packed = [theirs, jnp.broadcast_to(relax, (per, 8, size)), jnp.broadcast_to(heat, (per, 8, size))]
    got = swap_cores(jnp.concatenate(packed, axis=1))
    tile_values = after(tile_values, got, other_code)
    other_values = swap_cores(tile_values)
    drive_half = by_core(mine, got[:, :half])
    relax_both = by_core(relax, got[:, half : half + 1])
    heat_both = by_core(heat, got[:, half + 8 : half + 9])

    drives = gather_far(drive_half)
    small = gather_far(jnp.concatenate([relax_both, heat_both * relax_both], axis=1))
    relaxes, heats = [s[:, :1] for s in small], [s[:, 1:] for s in small]
    pairs = split_tiles(tile_values, 0)
    drives[-1] = after(drives[-1], pairs)
    fluxes = [r * d for r, d in zip(relaxes, drives)]
    sizes = [chips // 2 * (high - low) for low, high in zip(edges[:-1], edges[1:])]
    for sweep in range(ITERS):
        pieces = gather_near(fluxes, edges)
        if sweep == 0:
            pairs = split_tiles(other_values, 1, pairs)
        near, far = [p for p, _ in pieces], [p for _, p in pieces]
        base = apply_tiles(0, 0, places, pairs, near, [num // 2, num // 2], 0.5)
        sends = apply_tiles(1, 0, places, pairs, far, sizes, 0.25, base[0])
        keeps = apply_tiles(2, num // 2, places, pairs, far, sizes, 0.25, base[1])
        blocks = reduce_near(keeps, sends)
        if sweep < ITERS - 1:
            fluxes = [r * (d + s) for r, d, s in zip(relaxes, drives, sum_far(blocks))]
    weighted = sum(
        [jnp.sum(w * b, axis=(0, 2)) for w, b in zip(heats, blocks)],
        jnp.sum(heats[0] * drive_half, axis=(0, 2)),
    )
    totals = jnp.concatenate([weighted, jnp.sum(heat).reshape(1)])
    totals = jnp.pad(totals[None], ((0, 0), (0, size - half - 1)))
    *blocks, totals = lax.optimization_barrier((*blocks, totals))
    totals = lax.all_to_all(
        jnp.broadcast_to(totals, (chips * CORES, size)), ALL, split_axis=0, concat_axis=0, tiled=True
    )
    totals = jnp.sum(totals.reshape(chips, CORES, size), axis=0)
    conductivity = totals[:, :half].reshape(columns) / jnp.sum(totals[:, half])
    flux = relax_both * (drive_half + after(reduce_far(blocks), conductivity))
    first, second = flux[:per], flux[per:]
    mine = jnp.where(core == 0, first, second)
    got = swap_cores(jnp.where(core == 0, second, first))
    both = jnp.concatenate(
        [jnp.where(core == 0, mine, got), jnp.where(core == 0, got, mine)], axis=1
    )
    mode_flux = jnp.transpose(both, (0, 2, 1)).reshape(modes, columns)
    return (mode_flux, conductivity)


def solution(mesh):
    n_rows, n_cols = mesh.shape["row"], mesh.shape["col"]
    planes = depth_of(n_rows)
    chips = Mesh(mesh.devices.reshape(planes, n_rows // planes, n_cols // CORES, CORES), ALL)
    placed = (
        P(ALL, None, None),
        P(ALL, None),
        P(ALL),
        P(ALL),
        P(ALL),
        P(ALL),
        P(ALL, None),
        P(ALL),
    )
    return jax.shard_map(
        shards,
        mesh=chips,
        in_specs=placed,
        out_specs=(P(ALL, None), P()),
        check_vma=False,
    )
```

```python
import functools

import jax
import jax.numpy as jnp
from jax import lax
from jax.experimental import pallas as pl
from jax.experimental.pallas import tpu as pltpu
from jax.sharding import Mesh
from jax.sharding import PartitionSpec as P

ITERS = 3
CORES = 2
STEP = 16
UNROLL = 8
CHUNK = 8
SLOTS = 8
SPANS = 4
VMEM = 56 * 1024 * 1024
CHIPS = ("z", "y", "x")
ALL = ("z", "y", "x", "core")
NEAR = ("x", "y", "z")


def depth_of(n_rows):
    return min(n for n in range(1, n_rows + 1) if n_rows % n == 0 and n * n >= n_rows)


def far_steps():
    return [(a, 1 << k) for a in NEAR for k in range(1, lax.axis_size(a).bit_length() - 1)]


def near_steps(part):
    turn = part % len(NEAR)
    return [(a, 1) for a in NEAR[turn:] + NEAR[:turn]]


def swap(array, step):
    axis, distance = step
    return lax.ppermute(array, axis, [(i, i ^ distance) for i in range(lax.axis_size(axis))])


def after(value, *others):
    return lax.optimization_barrier((value,) + others)[0]


def halves(array):
    middle = array.shape[0] // 2
    return array[:middle], array[middle:]


def gather_far(block):
    blocks = [block]
    for step in reversed(far_steps()):
        got = swap(blocks[0] if len(blocks) == 1 else jnp.concatenate(blocks, axis=0), step)
        blocks = blocks + jnp.split(got, len(blocks))
    return blocks


def gather_near(blocks, edges):
    starts = [
        jnp.concatenate([b[low:high] for b in blocks], axis=0) for low, high in zip(edges[:-1], edges[1:])
    ]
    pieces = []
    for part, block in enumerate(lax.optimization_barrier(starts)):
        steps = near_steps(part)
        for step in reversed(steps[1:]):
            block = jnp.concatenate([block, swap(block, step)], axis=0)
        pieces.append((block, swap(block, steps[0])))
    return pieces


def reduce_near(keeps, sends):
    far = 1 << len(far_steps())
    parts = []
    for part, (keep, send) in enumerate(zip(keeps, sends)):
        steps = near_steps(part)
        got = swap(send, steps[0])
        terms = [keep]
        for step in steps[1:]:
            terms.append(got)
            got = swap(sum([halves(t)[1] for t in terms[1:]], halves(terms[0])[1]), step)
            *terms, got = lax.optimization_barrier((*terms, got))
            terms = [halves(t)[0] for t in terms]
        terms = [jnp.split(t, far) for t in (*terms, got)]
        parts.append([sum(t[1:], t[0]) for t in zip(*terms)])
    return [jnp.concatenate(group, axis=0) for group in zip(*parts)]


def reduce_far(blocks):
    for step in far_steps():
        middle = len(blocks) // 2
        send = blocks[middle:]
        got = swap(jnp.concatenate(send, axis=0) if middle > 1 else send[0], step)
        blocks = [b + g for b, g in zip(blocks[:middle], jnp.split(got, middle))]
    return blocks[0]


def sum_far(blocks):
    count = len(blocks)
    for place, step in enumerate(far_steps()):
        bit = count >> (place + 1)
        got = jnp.split(swap(jnp.concatenate(blocks, axis=0), step), count)
        blocks = [b + got[k ^ bit] for k, b in enumerate(blocks)]
    return blocks


def split_kernel(tile_ref, *refs):
    pair_ref = refs[-1]
    size = tile_ref.shape[1]

    @pl.loop(0, STEP // UNROLL)
    def _(group):
        for k in range(UNROLL):
            tile = jnp.transpose(tile_ref[group * UNROLL + k])
            high = tile.astype(jnp.bfloat16)
            low = (tile - high.astype(jnp.float32)).astype(jnp.bfloat16)
            pair_ref[group * UNROLL + k, :size] = high
            pair_ref[group * UNROLL + k, size:] = low


def split_tiles(tiles, place, pairs=None):
    length, size, _ = tiles.shape
    steps = length // STEP
    given = [] if pairs is None else [pairs]
    return pl.pallas_call(
        split_kernel,
        out_shape=jax.ShapeDtypeStruct((CORES * length, 2 * size, size), jnp.bfloat16),
        grid=(steps,),
        in_specs=[pl.BlockSpec((STEP, size, size), lambda i: (i, 0, 0))]
        + [pl.BlockSpec(memory_space=pltpu.HBM)] * len(given),
        out_specs=pl.BlockSpec((STEP, 2 * size, size), lambda i: (place * steps + i, 0, 0)),
        input_output_aliases={1: 0} if given else {},
        compiler_params=pltpu.CompilerParams(vmem_limit_bytes=VMEM),
        cost_estimate=pl.CostEstimate(
            flops=3 * length * size * size, bytes_accessed=8 * length * size * size, transcendentals=0
        ),
    )(tiles, *given)


def apply_kernel(span, skip, counts, has_base, places_ref, pairs_ref, *refs):
    ends, refs = refs[: len(counts)], refs[len(counts) :]
    base_ref, refs = (refs[0], refs[1:]) if has_base else (None, refs)
    *outs, flux_ref, sum_ref, held_ref, sem, held_sem = refs
    total = pairs_ref.shape[0]
    start, stop = places_ref[span], places_ref[span + 1]
    chunks = (stop - start + CHUNK - 1) // CHUNK

    def fetch(chunk):
        slot = lax.rem(chunk, SLOTS)
        for k in range(CHUNK):
            at = jnp.minimum(start + chunk * CHUNK + k, total - 1)
            pltpu.make_async_copy(
                pairs_ref.at[places_ref[SPANS + at]], held_ref.at[slot, k], held_sem.at[slot]
            ).start()

    copies = [
        pltpu.make_async_copy(
            piece, flux_ref.at[pl.ds(sum(counts[:k]), counts[k])], sem.at[k]
        )
        for k, piece in enumerate(ends)
    ]
    if has_base:
        copies.append(pltpu.make_async_copy(base_ref, sum_ref, sem.at[len(counts)]))
    for copy in copies:
        copy.start()
    for chunk in range(SLOTS - 1):

        @pl.when(chunk < chunks)
        def _():
            fetch(jnp.int32(chunk))

    if not has_base:
        sum_ref[...] = jnp.zeros_like(sum_ref)
    for copy in copies:
        copy.wait()

    @pl.loop(0, chunks)
    def _(chunk):
        slot = lax.rem(chunk, SLOTS)
        pltpu.make_async_copy(
            pairs_ref.at[pl.ds(0, CHUNK)], held_ref.at[slot], held_sem.at[slot]
        ).wait()

        @pl.when(chunk + SLOTS - 1 < chunks)
        def _():
            fetch(chunk + SLOTS - 1)

        products, rows = [], []
        for k in range(CHUNK):
            at = start + chunk * CHUNK + k
            valid = jnp.where(at < stop, 1.0, 0.0)
            at = jnp.minimum(at, stop - 1)
            flux = flux_ref[places_ref[SPANS + 2 * total + at]] * valid
            high = flux.astype(jnp.bfloat16)
            low = (flux - high.astype(jnp.float32)).astype(jnp.bfloat16)
            left = jnp.concatenate([high, low], axis=0)
            both = jnp.dot(
                jnp.concatenate([left, left], axis=1),
                held_ref[slot, k],
                preferred_element_type=jnp.float32,
            )
            temps = flux.shape[0]
            products.append(both[:temps] + both[temps:])
            rows.append(places_ref[SPANS + total + at] - skip)
        for row, product in zip(rows, products):
            sum_ref[row] += product

    sizes = [out.shape[0] for out in outs]
    copies = [
        pltpu.make_async_copy(sum_ref.at[pl.ds(sum(sizes[:k]), sizes[k])], out, sem.at[k])
        for k, out in enumerate(outs)
    ]
    for copy in copies:
        copy.start()
    for copy in copies:
        copy.wait()


def apply_tiles(span, skip, places, pairs, flux, sizes, share, base=None):
    total, _, size = pairs.shape
    counts = [piece.shape[0] for piece in flux]
    temps = flux[0].shape[1]
    anywhere = pl.BlockSpec(memory_space=pltpu.HBM)
    given = [pairs, *flux] + ([] if base is None else [base])
    return pl.pallas_call(
        functools.partial(apply_kernel, span, skip, counts, base is not None),
        out_shape=[jax.ShapeDtypeStruct((n, temps, size), jnp.float32) for n in sizes],
        grid_spec=pltpu.PrefetchScalarGridSpec(
            num_scalar_prefetch=1,
            grid=(),
            in_specs=[anywhere] * len(given),
            out_specs=[anywhere] * len(sizes),
            scratch_shapes=[
                pltpu.VMEM((sum(counts), temps, size), jnp.float32),
                pltpu.VMEM((sum(sizes), temps, size), jnp.float32),
                pltpu.VMEM((SLOTS, CHUNK) + pairs.shape[1:], jnp.bfloat16),
                pltpu.SemaphoreType.DMA((len(counts) + 1,)),
                pltpu.SemaphoreType.DMA((SLOTS,)),
            ],
        ),
        compiler_params=pltpu.CompilerParams(vmem_limit_bytes=VMEM),
        cost_estimate=pl.CostEstimate(
            flops=int(share * total * size * size * temps * 8),
            bytes_accessed=int(share * total * size * size * 4) + 8 * sum(sizes) * temps * size,
            transcendentals=0,
        ),
    )(places, *given)


def shards(
    tile_values, tile_owner, tile_row, tile_col, tile_count, relaxation, driving, heat_weight
):
    n_cols = lax.axis_size("x") * CORES
    chips = lax.axis_size(CHIPS)
    length, size, _ = tile_values.shape
    modes, columns = driving.shape
    per = modes // size
    chip_tiles = CORES * per
    num = chips * chip_tiles
    half = columns // CORES
    core = lax.axis_index("core")
    cores = ("core", 1)

    edges = [chip_tiles * k // len(NEAR) for k in range(len(NEAR) + 1)]

    def place(tile):
        chip, inside = tile // chip_tiles, tile % chip_tiles
        away, width = {}, 1
        for axis in reversed(CHIPS):
            n = lax.axis_size(axis)
            away[axis] = ((chip // width) % n) ^ lax.axis_index(axis)
            width *= n
        side, out = jnp.zeros_like(tile), jnp.zeros_like(tile)
        for part in range(len(NEAR)):
            low, high = edges[part], edges[part + 1]
            (first, _), *steps = near_steps(part)
            slot = jnp.zeros_like(tile)
            for axis, distance in steps + far_steps():
                slot = 2 * slot + (away[axis] // distance) % 2
            slot = chips // 2 * low + slot * (high - low) + inside - low
            out = jnp.where(inside >= low, slot, out)
            side = jnp.where(inside >= low, away[first] % 2, side)
        return side, out

    owners = tile_owner[:, 0]
    row_side, row = place((owners // n_cols) * (n_cols * per) + tile_row)
    col_side, col = place(((tile_col // per) * n_cols + owners % n_cols) * per + tile_col % per)
    used = jnp.arange(length, dtype=jnp.int32) < tile_count[0]
    kind = jnp.where(used, jnp.where(col_side == 0, 0, 2 - row_side), 3)
    row = jnp.where(row_side == 1, row, row + num // 2)
    code = (kind * num + row) * num + col
    other_code = swap(code, cores)
    code = jnp.concatenate([code, other_code])
    kind = code // (num * num)
    slots = jnp.arange(CORES * length, dtype=jnp.int32)
    key = kind * (CORES * length) + slots
    rank = jnp.sum((key[None, :] < key[:, None]).astype(jnp.int32), axis=1)
    ends = jnp.sum((kind[None, :] < jnp.arange(SPANS, dtype=jnp.int32)[:, None]).astype(jnp.int32), axis=1)
    sorts = rank[None, :] == slots[:, None]
    order = jnp.sum(jnp.where(sorts, slots[None, :], 0), axis=1)
    code = jnp.sum(jnp.where(sorts, code[None, :] % (num * num), 0), axis=1)
    places = jnp.concatenate([ends, order, code // num, code % num])

    def by_core(own, other):
        return jnp.concatenate(
            [jnp.where(core == 0, own, other), jnp.where(core == 0, other, own)], axis=0
        )

    drive = jnp.transpose(driving.reshape(per, size, columns), (0, 2, 1))
    relax = relaxation.reshape(per, 1, size)
    heat = heat_weight.reshape(per, 1, size)
    low, high = drive[:, :half], drive[:, half:]
    mine = jnp.where(core == 0, low, high)
    theirs = jnp.where(core == 0, high, low)
    packed = [theirs, jnp.broadcast_to(relax, (per, 8, size)), jnp.broadcast_to(heat, (per, 8, size))]
    got = swap(jnp.concatenate(packed, axis=1), cores)
    tile_values = after(tile_values, got, other_code)
    other_values = swap(tile_values, cores)
    drive_half = by_core(mine, got[:, :half])
    relax_both = by_core(relax, got[:, half : half + 1])
    heat_both = by_core(heat, got[:, half + 8 : half + 9])

    drives = gather_far(drive_half)
    small = gather_far(jnp.concatenate([relax_both, heat_both * relax_both], axis=1))
    relaxes, heats = [s[:, :1] for s in small], [s[:, 1:] for s in small]
    pairs = split_tiles(tile_values, 0)
    drives[-1] = after(drives[-1], pairs)
    fluxes = [r * d for r, d in zip(relaxes, drives)]
    sizes = [chips // 2 * (high - low) for low, high in zip(edges[:-1], edges[1:])]
    for sweep in range(ITERS):
        pieces = gather_near(fluxes, edges)
        if sweep == 0:
            pairs = split_tiles(other_values, 1, pairs)
        near, far = [p for p, _ in pieces], [p for _, p in pieces]
        base = apply_tiles(0, 0, places, pairs, near, [num // 2, num // 2], 0.5)
        sends = apply_tiles(1, 0, places, pairs, far, sizes, 0.25, base[0])
        keeps = apply_tiles(2, num // 2, places, pairs, far, sizes, 0.25, base[1])
        blocks = reduce_near(keeps, sends)
        if sweep < ITERS - 1:
            fluxes = [r * (d + s) for r, d, s in zip(relaxes, drives, sum_far(blocks))]
    weighted = sum(
        [jnp.sum(w * b, axis=(0, 2)) for w, b in zip(heats, blocks)],
        jnp.sum(heats[0] * drive_half, axis=(0, 2)),
    )
    totals = jnp.concatenate([weighted, jnp.sum(heat).reshape(1)])
    totals = jnp.pad(totals[None], ((0, 0), (0, size - half - 1)))
    *blocks, totals = lax.optimization_barrier((*blocks, totals))
    totals = lax.all_to_all(
        jnp.broadcast_to(totals, (chips * CORES, size)), ALL, split_axis=0, concat_axis=0, tiled=True
    )
    totals = jnp.sum(totals.reshape(chips, CORES, size), axis=0)
    conductivity = totals[:, :half].reshape(columns) / jnp.sum(totals[:, half])
    flux = relax_both * (drive_half + after(reduce_far(blocks), conductivity))
    first, second = flux[:per], flux[per:]
    mine = jnp.where(core == 0, first, second)
    got = swap(jnp.where(core == 0, second, first), cores)
    both = jnp.concatenate(
        [jnp.where(core == 0, mine, got), jnp.where(core == 0, got, mine)], axis=1
    )
    mode_flux = jnp.transpose(both, (0, 2, 1)).reshape(modes, columns)
    return (mode_flux, conductivity)


def solution(mesh):
    n_rows, n_cols = mesh.shape["row"], mesh.shape["col"]
    planes = depth_of(n_rows)
    chips = Mesh(mesh.devices.reshape(planes, n_rows // planes, n_cols // CORES, CORES), ALL)
    placed = (
        P(ALL, None, None),
        P(ALL, None),
        P(ALL),
        P(ALL),
        P(ALL),
        P(ALL),
        P(ALL, None),
        P(ALL),
    )
    return jax.shard_map(
        shards,
        mesh=chips,
        in_specs=placed,
        out_specs=(P(ALL, None), P()),
        check_vma=False,
    )
```

```python
import functools

import jax
import jax.numpy as jnp
from jax import lax
from jax.experimental import pallas as pl
from jax.experimental.pallas import tpu as pltpu
from jax.sharding import Mesh
from jax.sharding import PartitionSpec as P

ITERS = 3
CORES = 2
STEP = 16
UNROLL = 8
CHUNK = 8
SLOTS = 8
SPANS = 4
VMEM = 56 * 1024 * 1024
CHIPS = ("z", "y", "x")
ALL = ("z", "y", "x", "core")
NEAR = ("x", "y", "z")


def depth_of(n_rows):
    return min(n for n in range(1, n_rows + 1) if n_rows % n == 0 and n * n >= n_rows)


def far_steps():
    return [(a, 1 << k) for a in NEAR for k in range(1, lax.axis_size(a).bit_length() - 1)]


def near_steps(part):
    turn = part % len(NEAR)
    return [(a, 1) for a in NEAR[turn:] + NEAR[:turn]]


def swap(array, step):
    axis, distance = step
    return lax.ppermute(array, axis, [(i, i ^ distance) for i in range(lax.axis_size(axis))])


def after(value, *others):
    return lax.optimization_barrier((value,) + others)[0]


def halves(array):
    middle = array.shape[0] // 2
    return array[:middle], array[middle:]


def gather_far(block):
    blocks = [block]
    for step in reversed(far_steps()):
        got = swap(blocks[0] if len(blocks) == 1 else jnp.concatenate(blocks, axis=0), step)
        blocks = blocks + jnp.split(got, len(blocks))
    return blocks


def gather_near(blocks, edges):
    starts = [
        jnp.concatenate([b[low:high] for b in blocks], axis=0) for low, high in zip(edges[:-1], edges[1:])
    ]
    pieces = []
    for part, block in enumerate(lax.optimization_barrier(starts)):
        steps = near_steps(part)
        for step in reversed(steps[1:]):
            block = jnp.concatenate([block, swap(block, step)], axis=0)
        pieces.append((block, swap(block, steps[0])))
    return pieces


def reduce_near(keeps, sends):
    far = 1 << len(far_steps())
    parts = []
    for part, (keep, send) in enumerate(zip(keeps, sends)):
        steps = near_steps(part)
        got = swap(send, steps[0])
        terms = [keep]
        for step in steps[1:]:
            terms.append(got)
            got = swap(sum([halves(t)[1] for t in terms[1:]], halves(terms[0])[1]), step)
            *terms, got = lax.optimization_barrier((*terms, got))
            terms = [halves(t)[0] for t in terms]
        terms = [jnp.split(t, far) for t in (*terms, got)]
        parts.append([sum(t[1:], t[0]) for t in zip(*terms)])
    return [jnp.concatenate(group, axis=0) for group in zip(*parts)]


def reduce_far(blocks):
    for step in far_steps():
        middle = len(blocks) // 2
        send = blocks[middle:]
        got = swap(jnp.concatenate(send, axis=0) if middle > 1 else send[0], step)
        blocks = [b + g for b, g in zip(blocks[:middle], jnp.split(got, middle))]
    return blocks[0]


def sum_far(blocks):
    count = len(blocks)
    for place, step in enumerate(far_steps()):
        bit = count >> (place + 1)
        got = jnp.split(swap(jnp.concatenate(blocks, axis=0), step), count)
        blocks = [b + got[k ^ bit] for k, b in enumerate(blocks)]
    return blocks


def split_kernel(tile_ref, *refs):
    pair_ref = refs[-1]
    size = tile_ref.shape[1]

    @pl.loop(0, STEP // UNROLL)
    def _(group):
        for k in range(UNROLL):
            tile = jnp.transpose(tile_ref[group * UNROLL + k])
            high = tile.astype(jnp.bfloat16)
            low = (tile - high.astype(jnp.float32)).astype(jnp.bfloat16)
            pair_ref[group * UNROLL + k, :size] = high
            pair_ref[group * UNROLL + k, size:] = low


def split_tiles(tiles, place, pairs=None):
    length, size, _ = tiles.shape
    steps = length // STEP
    given = [] if pairs is None else [pairs]
    return pl.pallas_call(
        split_kernel,
        out_shape=jax.ShapeDtypeStruct((CORES * length, 2 * size, size), jnp.bfloat16),
        grid=(steps,),
        in_specs=[pl.BlockSpec((STEP, size, size), lambda i: (i, 0, 0))]
        + [pl.BlockSpec(memory_space=pltpu.HBM)] * len(given),
        out_specs=pl.BlockSpec((STEP, 2 * size, size), lambda i: (place * steps + i, 0, 0)),
        input_output_aliases={1: 0} if given else {},
        compiler_params=pltpu.CompilerParams(vmem_limit_bytes=VMEM),
        cost_estimate=pl.CostEstimate(
            flops=3 * length * size * size, bytes_accessed=8 * length * size * size, transcendentals=0
        ),
    )(tiles, *given)


def apply_kernel(span, skip, pieces, has_base, places_ref, pairs_ref, *refs):
    flux, refs = refs[:pieces], refs[pieces:]
    base_ref, refs = (refs[0], refs[1:]) if has_base else (None, refs)
    *outs, flux_ref, sum_ref, held_ref, held_sem = refs
    total = pairs_ref.shape[0]
    start, stop = places_ref[span], places_ref[span + 1]
    chunks = (stop - start + CHUNK - 1) // CHUNK

    def fetch(chunk):
        slot = lax.rem(chunk, SLOTS)
        for k in range(CHUNK):
            at = jnp.minimum(start + chunk * CHUNK + k, total - 1)
            pltpu.make_async_copy(
                pairs_ref.at[places_ref[SPANS + at]], held_ref.at[slot, k], held_sem.at[slot]
            ).start()

    for chunk in range(SLOTS - 1):

        @pl.when(chunk < chunks)
        def _():
            fetch(jnp.int32(chunk))

    done = 0
    for piece in flux:
        flux_ref[done : done + piece.shape[0]] = piece[...]
        done += piece.shape[0]
    if has_base:
        sum_ref[...] = base_ref[...]
    else:
        sum_ref[...] = jnp.zeros_like(sum_ref)

    @pl.loop(0, chunks)
    def _(chunk):
        slot = lax.rem(chunk, SLOTS)
        pltpu.make_async_copy(
            pairs_ref.at[pl.ds(0, CHUNK)], held_ref.at[slot], held_sem.at[slot]
        ).wait()

        @pl.when(chunk + SLOTS - 1 < chunks)
        def _():
            fetch(chunk + SLOTS - 1)

        products, rows = [], []
        for k in range(CHUNK):
            at = start + chunk * CHUNK + k
            valid = jnp.where(at < stop, 1.0, 0.0)
            at = jnp.minimum(at, stop - 1)
            values = flux_ref[places_ref[SPANS + 2 * total + at]] * valid
            high = values.astype(jnp.bfloat16)
            low = (values - high.astype(jnp.float32)).astype(jnp.bfloat16)
            left = jnp.concatenate([high, low], axis=0)
            both = jnp.dot(
                jnp.concatenate([left, left], axis=1),
                held_ref[slot, k],
                preferred_element_type=jnp.float32,
            )
            temps = values.shape[0]
            products.append(both[:temps] + both[temps:])
            rows.append(places_ref[SPANS + total + at] - skip)
        for row, product in zip(rows, products):
            sum_ref[row] += product

    done = 0
    for out in outs:
        out[...] = sum_ref[done : done + out.shape[0]]
        done += out.shape[0]


def apply_tiles(span, skip, places, pairs, flux, sizes, share, base=None):
    total, _, size = pairs.shape
    temps = flux[0].shape[1]
    rows = sum(sizes)
    inside = pl.BlockSpec(memory_space=pltpu.VMEM)
    given = [*flux] + ([] if base is None else [base])
    return pl.pallas_call(
        functools.partial(apply_kernel, span, skip, len(flux), base is not None),
        out_shape=[jax.ShapeDtypeStruct((n, temps, size), jnp.float32) for n in sizes],
        grid_spec=pltpu.PrefetchScalarGridSpec(
            num_scalar_prefetch=1,
            grid=(),
            in_specs=[pl.BlockSpec(memory_space=pltpu.HBM)] + [inside] * len(given),
            out_specs=[inside] * len(sizes),
            scratch_shapes=[
                pltpu.VMEM((sum(piece.shape[0] for piece in flux), temps, size), jnp.float32),
                pltpu.VMEM((rows, temps, size), jnp.float32),
                pltpu.VMEM((SLOTS, CHUNK) + pairs.shape[1:], jnp.bfloat16),
                pltpu.SemaphoreType.DMA((SLOTS,)),
            ],
        ),
        compiler_params=pltpu.CompilerParams(vmem_limit_bytes=VMEM),
        cost_estimate=pl.CostEstimate(
            flops=int(share * total * size * size * temps * 8),
            bytes_accessed=int(share * total * size * size * 4) + 8 * rows * temps * size,
            transcendentals=0,
        ),
    )(places, pairs, *given)


def shards(
    tile_values, tile_owner, tile_row, tile_col, tile_count, relaxation, driving, heat_weight
):
    n_cols = lax.axis_size("x") * CORES
    chips = lax.axis_size(CHIPS)
    length, size, _ = tile_values.shape
    modes, columns = driving.shape
    per = modes // size
    chip_tiles = CORES * per
    num = chips * chip_tiles
    half = columns // CORES
    core = lax.axis_index("core")
    cores = ("core", 1)

    edges = [chip_tiles * k // len(NEAR) for k in range(len(NEAR) + 1)]

    def place(tile):
        chip, inside = tile // chip_tiles, tile % chip_tiles
        away, width = {}, 1
        for axis in reversed(CHIPS):
            n = lax.axis_size(axis)
            away[axis] = ((chip // width) % n) ^ lax.axis_index(axis)
            width *= n
        side, out = jnp.zeros_like(tile), jnp.zeros_like(tile)
        for part in range(len(NEAR)):
            low, high = edges[part], edges[part + 1]
            (first, _), *steps = near_steps(part)
            slot = jnp.zeros_like(tile)
            for axis, distance in steps + far_steps():
                slot = 2 * slot + (away[axis] // distance) % 2
            slot = chips // 2 * low + slot * (high - low) + inside - low
            out = jnp.where(inside >= low, slot, out)
            side = jnp.where(inside >= low, away[first] % 2, side)
        return side, out

    owners = tile_owner[:, 0]
    row_side, row = place((owners // n_cols) * (n_cols * per) + tile_row)
    col_side, col = place(((tile_col // per) * n_cols + owners % n_cols) * per + tile_col % per)
    used = jnp.arange(length, dtype=jnp.int32) < tile_count[0]
    kind = jnp.where(used, jnp.where(col_side == 0, 0, 2 - row_side), 3)
    row = jnp.where(row_side == 1, row, row + num // 2)
    code = (kind * num + row) * num + col
    other_code = swap(code, cores)
    code = jnp.concatenate([code, other_code])
    kind = code // (num * num)
    slots = jnp.arange(CORES * length, dtype=jnp.int32)
    key = kind * (CORES * length) + slots
    rank = jnp.sum((key[None, :] < key[:, None]).astype(jnp.int32), axis=1)
    ends = jnp.sum((kind[None, :] < jnp.arange(SPANS, dtype=jnp.int32)[:, None]).astype(jnp.int32), axis=1)
    sorts = rank[None, :] == slots[:, None]
    order = jnp.sum(jnp.where(sorts, slots[None, :], 0), axis=1)
    code = jnp.sum(jnp.where(sorts, code[None, :] % (num * num), 0), axis=1)
    places = jnp.concatenate([ends, order, code // num, code % num])

    def by_core(own, other):
        return jnp.concatenate(
            [jnp.where(core == 0, own, other), jnp.where(core == 0, other, own)], axis=0
        )

    drive = jnp.transpose(driving.reshape(per, size, columns), (0, 2, 1))
    relax = relaxation.reshape(per, 1, size)
    heat = heat_weight.reshape(per, 1, size)
    low, high = drive[:, :half], drive[:, half:]
    mine = jnp.where(core == 0, low, high)
    theirs = jnp.where(core == 0, high, low)
    packed = [theirs, jnp.broadcast_to(relax, (per, 8, size)), jnp.broadcast_to(heat, (per, 8, size))]
    got = swap(jnp.concatenate(packed, axis=1), cores)
    tile_values = after(tile_values, got, other_code)
    other_values = swap(tile_values, cores)
    drive_half = by_core(mine, got[:, :half])
    relax_both = by_core(relax, got[:, half : half + 1])
    heat_both = by_core(heat, got[:, half + 8 : half + 9])

    drives = gather_far(drive_half)
    small = gather_far(jnp.concatenate([relax_both, heat_both * relax_both], axis=1))
    relaxes, heats = [s[:, :1] for s in small], [s[:, 1:] for s in small]
    pairs = split_tiles(tile_values, 0)
    drives[-1] = after(drives[-1], pairs)
    fluxes = [r * d for r, d in zip(relaxes, drives)]
    sizes = [chips // 2 * (high - low) for low, high in zip(edges[:-1], edges[1:])]
    for sweep in range(ITERS):
        pieces = gather_near(fluxes, edges)
        if sweep == 0:
            pairs = split_tiles(other_values, 1, pairs)
        near, far = [p for p, _ in pieces], [p for _, p in pieces]
        base = apply_tiles(0, 0, places, pairs, near, [num // 2, num // 2], 0.5)
        sends = apply_tiles(1, 0, places, pairs, far, sizes, 0.25, base[0])
        keeps = apply_tiles(2, num // 2, places, pairs, far, sizes, 0.25, base[1])
        blocks = reduce_near(keeps, sends)
        if sweep < ITERS - 1:
            fluxes = [r * (d + s) for r, d, s in zip(relaxes, drives, sum_far(blocks))]
    weighted = sum(
        [jnp.sum(w * b, axis=(0, 2)) for w, b in zip(heats, blocks)],
        jnp.sum(heats[0] * drive_half, axis=(0, 2)),
    )
    totals = jnp.concatenate([weighted, jnp.sum(heat).reshape(1)])
    totals = jnp.pad(totals[None], ((0, 0), (0, size - half - 1)))
    *blocks, totals = lax.optimization_barrier((*blocks, totals))
    totals = lax.all_to_all(
        jnp.broadcast_to(totals, (chips * CORES, size)), ALL, split_axis=0, concat_axis=0, tiled=True
    )
    totals = jnp.sum(totals.reshape(chips, CORES, size), axis=0)
    conductivity = totals[:, :half].reshape(columns) / jnp.sum(totals[:, half])
    flux = relax_both * (drive_half + after(reduce_far(blocks), conductivity))
    first, second = flux[:per], flux[per:]
    mine = jnp.where(core == 0, first, second)
    got = swap(jnp.where(core == 0, second, first), cores)
    both = jnp.concatenate(
        [jnp.where(core == 0, mine, got), jnp.where(core == 0, got, mine)], axis=1
    )
    mode_flux = jnp.transpose(both, (0, 2, 1)).reshape(modes, columns)
    return (mode_flux, conductivity)


def solution(mesh):
    n_rows, n_cols = mesh.shape["row"], mesh.shape["col"]
    planes = depth_of(n_rows)
    chips = Mesh(mesh.devices.reshape(planes, n_rows // planes, n_cols // CORES, CORES), ALL)
    placed = (
        P(ALL, None, None),
        P(ALL, None),
        P(ALL),
        P(ALL),
        P(ALL),
        P(ALL),
        P(ALL, None),
        P(ALL),
    )
    return jax.shard_map(
        shards,
        mesh=chips,
        in_specs=placed,
        out_specs=(P(ALL, None), P()),
        check_vma=False,
    )
```

```python
import functools

import jax
import jax.numpy as jnp
from jax import lax
from jax.experimental import pallas as pl
from jax.experimental.pallas import tpu as pltpu
from jax.sharding import Mesh
from jax.sharding import PartitionSpec as P

ITERS = 3
CORES = 2
STEP = 16
UNROLL = 8
CHUNK = 8
SLOTS = 8
SPANS = 4
VMEM = 48 * 1024 * 1024
SPLIT_VMEM = 62 * 1024 * 1024
CHIPS = ("z", "y", "x")
ALL = ("z", "y", "x", "core")
NEAR = ("x", "y", "z")


def depth_of(n_rows):
    return min(n for n in range(1, n_rows + 1) if n_rows % n == 0 and n * n >= n_rows)


def far_steps():
    return [(a, 1 << k) for a in NEAR for k in range(1, lax.axis_size(a).bit_length() - 1)]


def near_steps(part):
    turn = part % len(NEAR)
    return [(a, 1) for a in NEAR[turn:] + NEAR[:turn]]


def swap(array, step):
    axis, distance = step
    return lax.ppermute(array, axis, [(i, i ^ distance) for i in range(lax.axis_size(axis))])


def after(value, *others):
    return lax.optimization_barrier((value,) + others)[0]


def halves(array):
    middle = array.shape[0] // 2
    return array[:middle], array[middle:]


def gather_far(block):
    blocks = [block]
    for step in reversed(far_steps()):
        got = swap(blocks[0] if len(blocks) == 1 else jnp.concatenate(blocks, axis=0), step)
        blocks = blocks + jnp.split(got, len(blocks))
    return blocks


def gather_near(blocks, edges):
    starts = [
        jnp.concatenate([b[low:high] for b in blocks], axis=0) for low, high in zip(edges[:-1], edges[1:])
    ]
    pieces = []
    for part, block in enumerate(lax.optimization_barrier(starts)):
        steps = near_steps(part)
        for step in reversed(steps[1:]):
            block = jnp.concatenate([block, swap(block, step)], axis=0)
        pieces.append((block, swap(block, steps[0])))
    return pieces


def reduce_near(keeps, sends):
    far = 1 << len(far_steps())
    parts = []
    for part, (keep, send) in enumerate(zip(keeps, sends)):
        steps = near_steps(part)
        got = swap(send, steps[0])
        terms = [keep]
        for step in steps[1:]:
            terms.append(got)
            got = swap(sum([halves(t)[1] for t in terms[1:]], halves(terms[0])[1]), step)
            *terms, got = lax.optimization_barrier((*terms, got))
            terms = [halves(t)[0] for t in terms]
        terms = [jnp.split(t, far) for t in (*terms, got)]
        parts.append([sum(t[1:], t[0]) for t in zip(*terms)])
    return [jnp.concatenate(group, axis=0) for group in zip(*parts)]


def reduce_far(blocks):
    for step in far_steps():
        middle = len(blocks) // 2
        send = blocks[middle:]
        got = swap(jnp.concatenate(send, axis=0) if middle > 1 else send[0], step)
        blocks = [b + g for b, g in zip(blocks[:middle], jnp.split(got, middle))]
    return blocks[0]


def sum_far(blocks):
    count = len(blocks)
    for place, step in enumerate(far_steps()):
        bit = count >> (place + 1)
        got = jnp.split(swap(jnp.concatenate(blocks, axis=0), step), count)
        blocks = [b + got[k ^ bit] for k, b in enumerate(blocks)]
    return blocks


def split_kernel(tile_ref, *refs):
    pair_ref = refs[-1]
    size = tile_ref.shape[1]

    @pl.loop(0, STEP // UNROLL)
    def _(group):
        for k in range(UNROLL):
            tile = jnp.transpose(tile_ref[group * UNROLL + k])
            high = tile.astype(jnp.bfloat16)
            low = (tile - high.astype(jnp.float32)).astype(jnp.bfloat16)
            pair_ref[group * UNROLL + k, :size] = high
            pair_ref[group * UNROLL + k, size:] = low


def split_tiles(tiles, place, pairs=None):
    length, size, _ = tiles.shape
    steps = length // STEP
    given = [] if pairs is None else [pairs]
    return pl.pallas_call(
        split_kernel,
        out_shape=jax.ShapeDtypeStruct((CORES * length, 2 * size, size), jnp.bfloat16),
        grid=(steps,),
        in_specs=[pl.BlockSpec((STEP, size, size), lambda i: (i, 0, 0))]
        + [pl.BlockSpec(memory_space=pltpu.HBM)] * len(given),
        out_specs=pl.BlockSpec((STEP, 2 * size, size), lambda i: (place * steps + i, 0, 0)),
        input_output_aliases={1: 0} if given else {},
        compiler_params=pltpu.CompilerParams(vmem_limit_bytes=SPLIT_VMEM),
        cost_estimate=pl.CostEstimate(
            flops=3 * length * size * size, bytes_accessed=8 * length * size * size, transcendentals=0
        ),
    )(tiles, *given)


def apply_kernel(span, skip, pieces, has_base, places_ref, pairs_ref, *refs):
    flux, refs = refs[:pieces], refs[pieces:]
    base_ref, refs = (refs[0], refs[1:]) if has_base else (None, refs)
    *outs, flux_ref, sum_ref, held_ref, held_sem = refs
    total = pairs_ref.shape[0]
    start, stop = places_ref[span], places_ref[span + 1]
    chunks = (stop - start + CHUNK - 1) // CHUNK

    def fetch(chunk):
        slot = lax.rem(chunk, SLOTS)
        for k in range(CHUNK):
            at = jnp.minimum(start + chunk * CHUNK + k, total - 1)
            pltpu.make_async_copy(
                pairs_ref.at[places_ref[SPANS + at]], held_ref.at[slot, k], held_sem.at[slot]
            ).start()

    for chunk in range(SLOTS - 1):

        @pl.when(chunk < chunks)
        def _():
            fetch(jnp.int32(chunk))

    done = 0
    for piece in flux:
        flux_ref[done : done + piece.shape[0]] = piece[...]
        done += piece.shape[0]
    if has_base:
        sum_ref[...] = base_ref[...]
    else:
        sum_ref[...] = jnp.zeros_like(sum_ref)

    @pl.loop(0, chunks)
    def _(chunk):
        slot = lax.rem(chunk, SLOTS)
        pltpu.make_async_copy(
            pairs_ref.at[pl.ds(0, CHUNK)], held_ref.at[slot], held_sem.at[slot]
        ).wait()

        @pl.when(chunk + SLOTS - 1 < chunks)
        def _():
            fetch(chunk + SLOTS - 1)

        products, rows = [], []
        for k in range(CHUNK):
            at = start + chunk * CHUNK + k
            valid = jnp.where(at < stop, 1.0, 0.0)
            at = jnp.minimum(at, stop - 1)
            values = flux_ref[places_ref[SPANS + 2 * total + at]] * valid
            high = values.astype(jnp.bfloat16)
            low = (values - high.astype(jnp.float32)).astype(jnp.bfloat16)
            left = jnp.concatenate([high, low], axis=0)
            both = jnp.dot(
                jnp.concatenate([left, left], axis=1),
                held_ref[slot, k],
                preferred_element_type=jnp.float32,
            )
            temps = values.shape[0]
            products.append(both[:temps] + both[temps:])
            rows.append(places_ref[SPANS + total + at] - skip)
        for row, product in zip(rows, products):
            sum_ref[row] += product

    done = 0
    for out in outs:
        out[...] = sum_ref[done : done + out.shape[0]]
        done += out.shape[0]


def apply_tiles(span, skip, places, pairs, flux, sizes, share, base=None):
    total, _, size = pairs.shape
    temps = flux[0].shape[1]
    rows = sum(sizes)
    inside = pl.BlockSpec(memory_space=pltpu.VMEM)
    given = [*flux] + ([] if base is None else [base])
    return pl.pallas_call(
        functools.partial(apply_kernel, span, skip, len(flux), base is not None),
        out_shape=[jax.ShapeDtypeStruct((n, temps, size), jnp.float32) for n in sizes],
        grid_spec=pltpu.PrefetchScalarGridSpec(
            num_scalar_prefetch=1,
            grid=(),
            in_specs=[pl.BlockSpec(memory_space=pltpu.HBM)] + [inside] * len(given),
            out_specs=[inside] * len(sizes),
            scratch_shapes=[
                pltpu.VMEM((sum(piece.shape[0] for piece in flux), temps, size), jnp.float32),
                pltpu.VMEM((rows, temps, size), jnp.float32),
                pltpu.VMEM((SLOTS, CHUNK) + pairs.shape[1:], jnp.bfloat16),
                pltpu.SemaphoreType.DMA((SLOTS,)),
            ],
        ),
        compiler_params=pltpu.CompilerParams(vmem_limit_bytes=VMEM),
        cost_estimate=pl.CostEstimate(
            flops=int(share * total * size * size * temps * 8),
            bytes_accessed=int(share * total * size * size * 4) + 8 * rows * temps * size,
            transcendentals=0,
        ),
    )(places, pairs, *given)


def shards(
    tile_values, tile_owner, tile_row, tile_col, tile_count, relaxation, driving, heat_weight
):
    n_cols = lax.axis_size("x") * CORES
    chips = lax.axis_size(CHIPS)
    length, size, _ = tile_values.shape
    modes, columns = driving.shape
    per = modes // size
    chip_tiles = CORES * per
    num = chips * chip_tiles
    half = columns // CORES
    core = lax.axis_index("core")
    cores = ("core", 1)

    edges = [chip_tiles * k // len(NEAR) for k in range(len(NEAR) + 1)]

    def place(tile):
        chip, inside = tile // chip_tiles, tile % chip_tiles
        away, width = {}, 1
        for axis in reversed(CHIPS):
            n = lax.axis_size(axis)
            away[axis] = ((chip // width) % n) ^ lax.axis_index(axis)
            width *= n
        side, out = jnp.zeros_like(tile), jnp.zeros_like(tile)
        for part in range(len(NEAR)):
            low, high = edges[part], edges[part + 1]
            (first, _), *steps = near_steps(part)
            slot = jnp.zeros_like(tile)
            for axis, distance in steps + far_steps():
                slot = 2 * slot + (away[axis] // distance) % 2
            slot = chips // 2 * low + slot * (high - low) + inside - low
            out = jnp.where(inside >= low, slot, out)
            side = jnp.where(inside >= low, away[first] % 2, side)
        return side, out

    owners = tile_owner[:, 0]
    row_side, row = place((owners // n_cols) * (n_cols * per) + tile_row)
    col_side, col = place(((tile_col // per) * n_cols + owners % n_cols) * per + tile_col % per)
    used = jnp.arange(length, dtype=jnp.int32) < tile_count[0]
    kind = jnp.where(used, jnp.where(col_side == 0, 0, 2 - row_side), 3)
    row = jnp.where(row_side == 1, row, row + num // 2)
    code = (kind * num + row) * num + col
    other_code = swap(code, cores)
    code = jnp.concatenate([code, other_code])
    kind = code // (num * num)
    slots = jnp.arange(CORES * length, dtype=jnp.int32)
    key = kind * (CORES * length) + slots
    rank = jnp.sum((key[None, :] < key[:, None]).astype(jnp.int32), axis=1)
    ends = jnp.sum((kind[None, :] < jnp.arange(SPANS, dtype=jnp.int32)[:, None]).astype(jnp.int32), axis=1)
    sorts = rank[None, :] == slots[:, None]
    order = jnp.sum(jnp.where(sorts, slots[None, :], 0), axis=1)
    code = jnp.sum(jnp.where(sorts, code[None, :] % (num * num), 0), axis=1)
    places = jnp.concatenate([ends, order, code // num, code % num])

    def by_core(own, other):
        return jnp.concatenate(
            [jnp.where(core == 0, own, other), jnp.where(core == 0, other, own)], axis=0
        )

    drive = jnp.transpose(driving.reshape(per, size, columns), (0, 2, 1))
    relax = relaxation.reshape(per, 1, size)
    heat = heat_weight.reshape(per, 1, size)
    low, high = drive[:, :half], drive[:, half:]
    mine = jnp.where(core == 0, low, high)
    theirs = jnp.where(core == 0, high, low)
    packed = [theirs, jnp.broadcast_to(relax, (per, 8, size)), jnp.broadcast_to(heat, (per, 8, size))]
    got = swap(jnp.concatenate(packed, axis=1), cores)
    tile_values = after(tile_values, got, other_code)
    other_values = swap(tile_values, cores)
    drive_half = by_core(mine, got[:, :half])
    relax_both = by_core(relax, got[:, half : half + 1])
    heat_both = by_core(heat, got[:, half + 8 : half + 9])

    drives = gather_far(drive_half)
    small = gather_far(jnp.concatenate([relax_both, heat_both * relax_both], axis=1))
    relaxes, heats = [s[:, :1] for s in small], [s[:, 1:] for s in small]
    pairs = split_tiles(tile_values, 0)
    drives[-1] = after(drives[-1], pairs)
    fluxes = [r * d for r, d in zip(relaxes, drives)]
    sizes = [chips // 2 * (high - low) for low, high in zip(edges[:-1], edges[1:])]
    for sweep in range(ITERS):
        pieces = gather_near(fluxes, edges)
        if sweep == 0:
            pairs = split_tiles(other_values, 1, pairs)
        near, far = [p for p, _ in pieces], [p for _, p in pieces]
        base = apply_tiles(0, 0, places, pairs, near, [num // 2, num // 2], 0.5)
        sends = apply_tiles(1, 0, places, pairs, far, sizes, 0.25, base[0])
        keeps = apply_tiles(2, num // 2, places, pairs, far, sizes, 0.25, base[1])
        blocks = reduce_near(keeps, sends)
        if sweep < ITERS - 1:
            fluxes = [r * (d + s) for r, d, s in zip(relaxes, drives, sum_far(blocks))]
    weighted = sum(
        [jnp.sum(w * b, axis=(0, 2)) for w, b in zip(heats, blocks)],
        jnp.sum(heats[0] * drive_half, axis=(0, 2)),
    )
    totals = jnp.concatenate([weighted, jnp.sum(heat).reshape(1)])
    totals = jnp.pad(totals[None], ((0, 0), (0, size - half - 1)))
    *blocks, totals = lax.optimization_barrier((*blocks, totals))
    totals = lax.all_to_all(
        jnp.broadcast_to(totals, (chips * CORES, size)), ALL, split_axis=0, concat_axis=0, tiled=True
    )
    totals = jnp.sum(totals.reshape(chips, CORES, size), axis=0)
    conductivity = totals[:, :half].reshape(columns) / jnp.sum(totals[:, half])
    flux = relax_both * (drive_half + after(reduce_far(blocks), conductivity))
    first, second = flux[:per], flux[per:]
    mine = jnp.where(core == 0, first, second)
    got = swap(jnp.where(core == 0, second, first), cores)
    both = jnp.concatenate(
        [jnp.where(core == 0, mine, got), jnp.where(core == 0, got, mine)], axis=1
    )
    mode_flux = jnp.transpose(both, (0, 2, 1)).reshape(modes, columns)
    return (mode_flux, conductivity)


def solution(mesh):
    n_rows, n_cols = mesh.shape["row"], mesh.shape["col"]
    planes = depth_of(n_rows)
    chips = Mesh(mesh.devices.reshape(planes, n_rows // planes, n_cols // CORES, CORES), ALL)
    placed = (
        P(ALL, None, None),
        P(ALL, None),
        P(ALL),
        P(ALL),
        P(ALL),
        P(ALL),
        P(ALL, None),
        P(ALL),
    )
    return jax.shard_map(
        shards,
        mesh=chips,
        in_specs=placed,
        out_specs=(P(ALL, None), P()),
        check_vma=False,
    )
```

```python
import functools

import jax
import jax.numpy as jnp
from jax import lax
from jax.experimental import pallas as pl
from jax.experimental.pallas import tpu as pltpu
from jax.sharding import Mesh
from jax.sharding import PartitionSpec as P

ITERS = 3
CORES = 2
CHUNK = 8
SLOTS = 8
SPANS = 4
VMEM = 48 * 1024 * 1024
CHIPS = ("z", "y", "x")
ALL = ("z", "y", "x", "core")
NEAR = ("x", "y", "z")


def depth_of(n_rows):
    return min(n for n in range(1, n_rows + 1) if n_rows % n == 0 and n * n >= n_rows)


def far_steps():
    return [(a, 1 << k) for a in NEAR for k in range(1, lax.axis_size(a).bit_length() - 1)]


def near_steps(part):
    turn = part % len(NEAR)
    return [(a, 1) for a in NEAR[turn:] + NEAR[:turn]]


def swap(array, step):
    axis, distance = step
    return lax.ppermute(array, axis, [(i, i ^ distance) for i in range(lax.axis_size(axis))])


def after(value, *others):
    return lax.optimization_barrier((value,) + others)[0]


def halves(array):
    middle = array.shape[0] // 2
    return array[:middle], array[middle:]


def gather_far(block):
    blocks = [block]
    for step in reversed(far_steps()):
        got = swap(blocks[0] if len(blocks) == 1 else jnp.concatenate(blocks, axis=0), step)
        blocks = blocks + jnp.split(got, len(blocks))
    return blocks


def gather_near(blocks, edges):
    starts = [
        jnp.concatenate([b[low:high] for b in blocks], axis=0) for low, high in zip(edges[:-1], edges[1:])
    ]
    pieces = []
    for part, block in enumerate(lax.optimization_barrier(starts)):
        steps = near_steps(part)
        for step in reversed(steps[1:]):
            block = jnp.concatenate([block, swap(block, step)], axis=0)
        pieces.append((block, swap(block, steps[0])))
    return pieces


def reduce_near(keeps, sends):
    far = 1 << len(far_steps())
    parts = []
    for part, (keep, send) in enumerate(zip(keeps, sends)):
        steps = near_steps(part)
        got = swap(send, steps[0])
        terms = [keep]
        for step in steps[1:]:
            terms.append(got)
            got = swap(sum([halves(t)[1] for t in terms[1:]], halves(terms[0])[1]), step)
            *terms, got = lax.optimization_barrier((*terms, got))
            terms = [halves(t)[0] for t in terms]
        terms = [jnp.split(t, far) for t in (*terms, got)]
        parts.append([sum(t[1:], t[0]) for t in zip(*terms)])
    return [jnp.concatenate(group, axis=0) for group in zip(*parts)]


def reduce_far(blocks):
    for step in far_steps():
        middle = len(blocks) // 2
        send = blocks[middle:]
        got = swap(jnp.concatenate(send, axis=0) if middle > 1 else send[0], step)
        blocks = [b + g for b, g in zip(blocks[:middle], jnp.split(got, middle))]
    return blocks[0]


def sum_far(blocks):
    count = len(blocks)
    for place, step in enumerate(far_steps()):
        bit = count >> (place + 1)
        got = jnp.split(swap(jnp.concatenate(blocks, axis=0), step), count)
        blocks = [b + got[k ^ bit] for k, b in enumerate(blocks)]
    return blocks


def apply_kernel(span, skip, pieces, has_base, places_ref, own_ref, other_ref, *refs):
    flux, refs = refs[:pieces], refs[pieces:]
    base_ref, refs = (refs[0], refs[1:]) if has_base else (None, refs)
    *outs, flux_ref, sum_ref, held_ref, held_sem = refs
    length = own_ref.shape[0]
    total = 2 * length
    start, stop = places_ref[span], places_ref[span + 1]
    chunks = (stop - start + CHUNK - 1) // CHUNK

    def fetch(chunk):
        slot = lax.rem(chunk, SLOTS)
        for k in range(CHUNK):
            at = places_ref[SPANS + jnp.minimum(start + chunk * CHUNK + k, total - 1)]
            for tiles_ref, low in ((own_ref, 0), (other_ref, length)):

                @pl.when((at >= low) & (at < low + length))
                def _():
                    pltpu.make_async_copy(
                        tiles_ref.at[at - low], held_ref.at[slot, k], held_sem.at[slot]
                    ).start()

    for chunk in range(SLOTS - 1):

        @pl.when(chunk < chunks)
        def _():
            fetch(jnp.int32(chunk))

    done = 0
    for piece in flux:
        flux_ref[done : done + piece.shape[0]] = piece[...]
        done += piece.shape[0]
    if has_base:
        sum_ref[...] = base_ref[...]
    else:
        sum_ref[...] = jnp.zeros_like(sum_ref)

    @pl.loop(0, chunks)
    def _(chunk):
        slot = lax.rem(chunk, SLOTS)
        pltpu.make_async_copy(
            own_ref.at[pl.ds(0, CHUNK)], held_ref.at[slot], held_sem.at[slot]
        ).wait()

        @pl.when(chunk + SLOTS - 1 < chunks)
        def _():
            fetch(chunk + SLOTS - 1)

        products, rows = [], []
        for k in range(CHUNK):
            at = start + chunk * CHUNK + k
            valid = jnp.where(at < stop, 1.0, 0.0)
            at = jnp.minimum(at, stop - 1)
            values = flux_ref[places_ref[SPANS + 2 * total + at]] * valid
            high = values.astype(jnp.bfloat16)
            low = (values - high.astype(jnp.float32)).astype(jnp.bfloat16)
            left = jnp.concatenate([high, low], axis=0)
            tile = held_ref[slot, k]
            high = tile.astype(jnp.bfloat16)
            low = (tile - high.astype(jnp.float32)).astype(jnp.bfloat16)
            both = lax.dot_general(
                jnp.concatenate([left, left], axis=1),
                jnp.concatenate([high, low], axis=1),
                (((1,), (1,)), ((), ())),
                preferred_element_type=jnp.float32,
            )
            temps = values.shape[0]
            products.append(both[:temps] + both[temps:])
            rows.append(places_ref[SPANS + total + at] - skip)
        for row, product in zip(rows, products):
            sum_ref[row] += product

    done = 0
    for out in outs:
        out[...] = sum_ref[done : done + out.shape[0]]
        done += out.shape[0]


def apply_tiles(span, skip, places, tiles, flux, sizes, share, base=None):
    length, size, _ = tiles[0].shape
    temps = flux[0].shape[1]
    rows = sum(sizes)
    inside = pl.BlockSpec(memory_space=pltpu.VMEM)
    given = [*flux] + ([] if base is None else [base])
    return pl.pallas_call(
        functools.partial(apply_kernel, span, skip, len(flux), base is not None),
        out_shape=[jax.ShapeDtypeStruct((n, temps, size), jnp.float32) for n in sizes],
        grid_spec=pltpu.PrefetchScalarGridSpec(
            num_scalar_prefetch=1,
            grid=(),
            in_specs=[pl.BlockSpec(memory_space=pltpu.HBM)] * 2 + [inside] * len(given),
            out_specs=[inside] * len(sizes),
            scratch_shapes=[
                pltpu.VMEM((sum(piece.shape[0] for piece in flux), temps, size), jnp.float32),
                pltpu.VMEM((rows, temps, size), jnp.float32),
                pltpu.VMEM((SLOTS, CHUNK, size, size), jnp.float32),
                pltpu.SemaphoreType.DMA((SLOTS,)),
            ],
        ),
        compiler_params=pltpu.CompilerParams(vmem_limit_bytes=VMEM),
        cost_estimate=pl.CostEstimate(
            flops=int(share * 2 * length * size * size * temps * 8),
            bytes_accessed=int(share * 2 * length * size * size * 4) + 8 * rows * temps * size,
            transcendentals=0,
        ),
    )(places, *tiles, *given)


def shards(
    tile_values, tile_owner, tile_row, tile_col, tile_count, relaxation, driving, heat_weight
):
    n_cols = lax.axis_size("x") * CORES
    chips = lax.axis_size(CHIPS)
    length, size, _ = tile_values.shape
    modes, columns = driving.shape
    per = modes // size
    chip_tiles = CORES * per
    num = chips * chip_tiles
    half = columns // CORES
    core = lax.axis_index("core")
    cores = ("core", 1)

    edges = [chip_tiles * k // len(NEAR) for k in range(len(NEAR) + 1)]

    def place(tile):
        chip, inside = tile // chip_tiles, tile % chip_tiles
        away, width = {}, 1
        for axis in reversed(CHIPS):
            n = lax.axis_size(axis)
            away[axis] = ((chip // width) % n) ^ lax.axis_index(axis)
            width *= n
        side, out = jnp.zeros_like(tile), jnp.zeros_like(tile)
        for part in range(len(NEAR)):
            low, high = edges[part], edges[part + 1]
            (first, _), *steps = near_steps(part)
            slot = jnp.zeros_like(tile)
            for axis, distance in steps + far_steps():
                slot = 2 * slot + (away[axis] // distance) % 2
            slot = chips // 2 * low + slot * (high - low) + inside - low
            out = jnp.where(inside >= low, slot, out)
            side = jnp.where(inside >= low, away[first] % 2, side)
        return side, out

    owners = tile_owner[:, 0]
    row_side, row = place((owners // n_cols) * (n_cols * per) + tile_row)
    col_side, col = place(((tile_col // per) * n_cols + owners % n_cols) * per + tile_col % per)
    used = jnp.arange(length, dtype=jnp.int32) < tile_count[0]
    kind = jnp.where(used, jnp.where(col_side == 0, 0, 2 - row_side), 3)
    row = jnp.where(row_side == 1, row, row + num // 2)
    code = (kind * num + row) * num + col
    other_code = swap(code, cores)
    code = jnp.concatenate([code, other_code])
    kind = code // (num * num)
    slots = jnp.arange(CORES * length, dtype=jnp.int32)
    key = kind * (CORES * length) + slots
    rank = jnp.sum((key[None, :] < key[:, None]).astype(jnp.int32), axis=1)
    ends = jnp.sum((kind[None, :] < jnp.arange(SPANS, dtype=jnp.int32)[:, None]).astype(jnp.int32), axis=1)
    sorts = rank[None, :] == slots[:, None]
    order = jnp.sum(jnp.where(sorts, slots[None, :], 0), axis=1)
    code = jnp.sum(jnp.where(sorts, code[None, :] % (num * num), 0), axis=1)
    places = jnp.concatenate([ends, order, code // num, code % num])

    def by_core(own, other):
        return jnp.concatenate(
            [jnp.where(core == 0, own, other), jnp.where(core == 0, other, own)], axis=0
        )

    drive = jnp.transpose(driving.reshape(per, size, columns), (0, 2, 1))
    relax = relaxation.reshape(per, 1, size)
    heat = heat_weight.reshape(per, 1, size)
    low, high = drive[:, :half], drive[:, half:]
    mine = jnp.where(core == 0, low, high)
    theirs = jnp.where(core == 0, high, low)
    packed = [theirs, jnp.broadcast_to(relax, (per, 8, size)), jnp.broadcast_to(heat, (per, 8, size))]
    got = swap(jnp.concatenate(packed, axis=1), cores)
    tile_values = after(tile_values, got, other_code)
    other_values = swap(tile_values, cores)
    drive_half = by_core(mine, got[:, :half])
    relax_both = by_core(relax, got[:, half : half + 1])
    heat_both = by_core(heat, got[:, half + 8 : half + 9])

    drives = gather_far(drive_half)
    small = gather_far(jnp.concatenate([relax_both, heat_both * relax_both], axis=1))
    relaxes, heats = [s[:, :1] for s in small], [s[:, 1:] for s in small]
    drives[-1], other_values = lax.optimization_barrier((drives[-1], other_values))
    fluxes = [r * d for r, d in zip(relaxes, drives)]
    tiles = (tile_values, other_values)
    sizes = [chips // 2 * (high - low) for low, high in zip(edges[:-1], edges[1:])]
    for sweep in range(ITERS):
        pieces = gather_near(fluxes, edges)
        near, far = [p for p, _ in pieces], [p for _, p in pieces]
        base = apply_tiles(0, 0, places, tiles, near, [num // 2, num // 2], 0.5)
        sends = apply_tiles(1, 0, places, tiles, far, sizes, 0.25, base[0])
        keeps = apply_tiles(2, num // 2, places, tiles, far, sizes, 0.25, base[1])
        blocks = reduce_near(keeps, sends)
        if sweep < ITERS - 1:
            fluxes = [r * (d + s) for r, d, s in zip(relaxes, drives, sum_far(blocks))]
    weighted = sum(
        [jnp.sum(w * b, axis=(0, 2)) for w, b in zip(heats, blocks)],
        jnp.sum(heats[0] * drive_half, axis=(0, 2)),
    )
    totals = jnp.concatenate([weighted, jnp.sum(heat).reshape(1)])
    totals = jnp.pad(totals[None], ((0, 0), (0, size - half - 1)))
    *blocks, totals = lax.optimization_barrier((*blocks, totals))
    totals = lax.all_to_all(
        jnp.broadcast_to(totals, (chips * CORES, size)), ALL, split_axis=0, concat_axis=0, tiled=True
    )
    totals = jnp.sum(totals.reshape(chips, CORES, size), axis=0)
    conductivity = totals[:, :half].reshape(columns) / jnp.sum(totals[:, half])
    flux = relax_both * (drive_half + after(reduce_far(blocks), conductivity))
    first, second = flux[:per], flux[per:]
    mine = jnp.where(core == 0, first, second)
    got = swap(jnp.where(core == 0, second, first), cores)
    both = jnp.concatenate(
        [jnp.where(core == 0, mine, got), jnp.where(core == 0, got, mine)], axis=1
    )
    mode_flux = jnp.transpose(both, (0, 2, 1)).reshape(modes, columns)
    return (mode_flux, conductivity)


def solution(mesh):
    n_rows, n_cols = mesh.shape["row"], mesh.shape["col"]
    planes = depth_of(n_rows)
    chips = Mesh(mesh.devices.reshape(planes, n_rows // planes, n_cols // CORES, CORES), ALL)
    placed = (
        P(ALL, None, None),
        P(ALL, None),
        P(ALL),
        P(ALL),
        P(ALL),
        P(ALL),
        P(ALL, None),
        P(ALL),
    )
    return jax.shard_map(
        shards,
        mesh=chips,
        in_specs=placed,
        out_specs=(P(ALL, None), P()),
        check_vma=False,
    )
```

```python
import functools

import jax
import jax.numpy as jnp
from jax import lax
from jax.experimental import pallas as pl
from jax.experimental.pallas import tpu as pltpu
from jax.sharding import Mesh
from jax.sharding import PartitionSpec as P

ITERS = 3
CORES = 2
CHUNK = 8
SLOTS = 8
SPANS = 4
VMEM = 48 * 1024 * 1024
CHIPS = ("z", "y", "x")
ALL = ("z", "y", "x", "core")
NEAR = ("x", "y", "z")


def depth_of(n_rows):
    return min(n for n in range(1, n_rows + 1) if n_rows % n == 0 and n * n >= n_rows)


def far_steps():
    return [(a, 1 << k) for a in NEAR for k in range(1, lax.axis_size(a).bit_length() - 1)]


def near_steps(part):
    turn = part % len(NEAR)
    return [(a, 1) for a in NEAR[turn:] + NEAR[:turn]]


def swap(array, step):
    axis, distance = step
    return lax.ppermute(array, axis, [(i, i ^ distance) for i in range(lax.axis_size(axis))])


def after(value, *others):
    return lax.optimization_barrier((value,) + others)[0]


def halves(array):
    middle = array.shape[0] // 2
    return array[:middle], array[middle:]


def gather_far(block):
    blocks = [block]
    for step in reversed(far_steps()):
        got = swap(blocks[0] if len(blocks) == 1 else jnp.concatenate(blocks, axis=0), step)
        blocks = blocks + jnp.split(got, len(blocks))
    return blocks


def gather_near(blocks, edges):
    starts = [
        jnp.concatenate([b[low:high] for b in blocks], axis=0) for low, high in zip(edges[:-1], edges[1:])
    ]
    pieces = []
    for part, block in enumerate(lax.optimization_barrier(starts)):
        steps = near_steps(part)
        for step in reversed(steps[1:]):
            block = jnp.concatenate([block, swap(block, step)], axis=0)
        pieces.append((block, swap(block, steps[0])))
    return pieces


def reduce_near(keeps, sends):
    far = 1 << len(far_steps())
    parts = []
    for part, (keep, send) in enumerate(zip(keeps, sends)):
        steps = near_steps(part)
        got = swap(send, steps[0])
        terms = [keep]
        for step in steps[1:]:
            terms.append(got)
            got = swap(sum([halves(t)[1] for t in terms[1:]], halves(terms[0])[1]), step)
            *terms, got = lax.optimization_barrier((*terms, got))
            terms = [halves(t)[0] for t in terms]
        terms = [jnp.split(t, far) for t in (*terms, got)]
        parts.append([sum(t[1:], t[0]) for t in zip(*terms)])
    return [jnp.concatenate(group, axis=0) for group in zip(*parts)]


def reduce_far(blocks):
    for step in far_steps():
        middle = len(blocks) // 2
        send = blocks[middle:]
        got = swap(jnp.concatenate(send, axis=0) if middle > 1 else send[0], step)
        blocks = [b + g for b, g in zip(blocks[:middle], jnp.split(got, middle))]
    return blocks[0]


def sum_far(blocks):
    count = len(blocks)
    for place, step in enumerate(far_steps()):
        bit = count >> (place + 1)
        got = jnp.split(swap(jnp.concatenate(blocks, axis=0), step), count)
        blocks = [b + got[k ^ bit] for k, b in enumerate(blocks)]
    return blocks


def apply_kernel(span, skip, pieces, has_base, places_ref, own_ref, other_ref, *refs):
    flux, refs = refs[:pieces], refs[pieces:]
    base_ref, refs = (refs[0], refs[1:]) if has_base else (None, refs)
    *outs, flux_ref, sum_ref, held_ref, held_sem = refs
    length = own_ref.shape[0]
    total = 2 * length
    start, stop = places_ref[span], places_ref[span + 1]
    chunks = (stop - start + CHUNK - 1) // CHUNK

    def fetch(chunk):
        slot = lax.rem(chunk, SLOTS)
        for k in range(CHUNK):
            at = places_ref[SPANS + jnp.minimum(start + chunk * CHUNK + k, total - 1)]
            for tiles_ref, low in ((own_ref, 0), (other_ref, length)):

                @pl.when((at >= low) & (at < low + length))
                def _():
                    pltpu.make_async_copy(
                        tiles_ref.at[at - low], held_ref.at[slot, k], held_sem.at[slot]
                    ).start()

    for chunk in range(SLOTS - 1):

        @pl.when(chunk < chunks)
        def _():
            fetch(jnp.int32(chunk))

    done = 0
    for piece in flux:
        flux_ref[done : done + piece.shape[0]] = piece[...]
        done += piece.shape[0]
    if has_base:
        sum_ref[...] = base_ref[...]
    else:
        sum_ref[...] = jnp.zeros_like(sum_ref)

    @pl.loop(0, chunks)
    def _(chunk):
        slot = lax.rem(chunk, SLOTS)
        pltpu.make_async_copy(
            own_ref.at[pl.ds(0, CHUNK)], held_ref.at[slot], held_sem.at[slot]
        ).wait()

        @pl.when(chunk + SLOTS - 1 < chunks)
        def _():
            fetch(chunk + SLOTS - 1)

        products, rows = [], []
        for k in range(CHUNK):
            at = start + chunk * CHUNK + k
            valid = jnp.where(at < stop, 1.0, 0.0)
            at = jnp.minimum(at, stop - 1)
            values = flux_ref[places_ref[SPANS + 2 * total + at]] * valid
            high = values.astype(jnp.bfloat16)
            low = (values - high.astype(jnp.float32)).astype(jnp.bfloat16)
            left = jnp.concatenate([high, low], axis=0)
            tile = held_ref[slot, k]
            high = tile.astype(jnp.bfloat16)
            low = (tile - high.astype(jnp.float32)).astype(jnp.bfloat16)
            both = lax.dot_general(
                jnp.concatenate([left, left], axis=1),
                jnp.concatenate([high, low], axis=1),
                (((1,), (1,)), ((), ())),
                preferred_element_type=jnp.float32,
            )
            temps = values.shape[0]
            products.append(both[:temps] + both[temps:])
            rows.append(places_ref[SPANS + total + at] - skip)
        for row, product in zip(rows, products):
            sum_ref[row] += product

    done = 0
    for out in outs:
        out[...] = sum_ref[done : done + out.shape[0]]
        done += out.shape[0]


def apply_tiles(span, skip, places, tiles, flux, sizes, share, base=None):
    length, size, _ = tiles[0].shape
    temps = flux[0].shape[1]
    rows = sum(sizes)
    inside = pl.BlockSpec(memory_space=pltpu.VMEM)
    given = [*flux] + ([] if base is None else [base])
    return pl.pallas_call(
        functools.partial(apply_kernel, span, skip, len(flux), base is not None),
        out_shape=[jax.ShapeDtypeStruct((n, temps, size), jnp.float32) for n in sizes],
        grid_spec=pltpu.PrefetchScalarGridSpec(
            num_scalar_prefetch=1,
            grid=(),
            in_specs=[pl.BlockSpec(memory_space=pltpu.HBM)] * 2 + [inside] * len(given),
            out_specs=[inside] * len(sizes),
            scratch_shapes=[
                pltpu.VMEM((sum(piece.shape[0] for piece in flux), temps, size), jnp.float32),
                pltpu.VMEM((rows, temps, size), jnp.float32),
                pltpu.VMEM((SLOTS, CHUNK, size, size), jnp.float32),
                pltpu.SemaphoreType.DMA((SLOTS,)),
            ],
        ),
        compiler_params=pltpu.CompilerParams(vmem_limit_bytes=VMEM),
        cost_estimate=pl.CostEstimate(
            flops=int(share * 2 * length * size * size * temps * 8),
            bytes_accessed=int(share * 2 * length * size * size * 4) + 8 * rows * temps * size,
            transcendentals=0,
        ),
    )(places, *tiles, *given)


def shards(
    tile_values, tile_owner, tile_row, tile_col, tile_count, relaxation, driving, heat_weight
):
    n_cols = lax.axis_size("x") * CORES
    chips = lax.axis_size(CHIPS)
    length, size, _ = tile_values.shape
    modes, columns = driving.shape
    per = modes // size
    chip_tiles = CORES * per
    num = chips * chip_tiles
    half = columns // CORES
    core = lax.axis_index("core")
    cores = ("core", 1)

    edges = [chip_tiles * k // len(NEAR) for k in range(len(NEAR) + 1)]

    def place(tile):
        chip, inside = tile // chip_tiles, tile % chip_tiles
        away, width = {}, 1
        for axis in reversed(CHIPS):
            n = lax.axis_size(axis)
            away[axis] = ((chip // width) % n) ^ lax.axis_index(axis)
            width *= n
        side, out = jnp.zeros_like(tile), jnp.zeros_like(tile)
        for part in range(len(NEAR)):
            low, high = edges[part], edges[part + 1]
            (first, _), *steps = near_steps(part)
            slot = jnp.zeros_like(tile)
            for axis, distance in steps + far_steps():
                slot = 2 * slot + (away[axis] // distance) % 2
            slot = chips // 2 * low + slot * (high - low) + inside - low
            out = jnp.where(inside >= low, slot, out)
            side = jnp.where(inside >= low, away[first] % 2, side)
        return side, out

    owners = tile_owner[:, 0]
    row_side, row = place((owners // n_cols) * (n_cols * per) + tile_row)
    col_side, col = place(((tile_col // per) * n_cols + owners % n_cols) * per + tile_col % per)
    used = jnp.arange(length, dtype=jnp.int32) < tile_count[0]
    kind = jnp.where(used, jnp.where(col_side == 0, 0, 2 - row_side), 3)
    row = jnp.where(row_side == 1, row, row + num // 2)
    code = (kind * num + row) * num + col
    other_code = swap(code, cores)
    code = jnp.concatenate([code, other_code])
    kind = code // (num * num)
    slots = jnp.arange(CORES * length, dtype=jnp.int32)
    key = kind * (CORES * length) + slots
    rank = jnp.sum((key[None, :] < key[:, None]).astype(jnp.int32), axis=1)
    ends = jnp.sum((kind[None, :] < jnp.arange(SPANS, dtype=jnp.int32)[:, None]).astype(jnp.int32), axis=1)
    sorts = rank[None, :] == slots[:, None]
    order = jnp.sum(jnp.where(sorts, slots[None, :], 0), axis=1)
    code = jnp.sum(jnp.where(sorts, code[None, :] % (num * num), 0), axis=1)
    places = jnp.concatenate([ends, order, code // num, code % num])

    def by_core(own, other):
        return jnp.concatenate(
            [jnp.where(core == 0, own, other), jnp.where(core == 0, other, own)], axis=0
        )

    drive = jnp.transpose(driving.reshape(per, size, columns), (0, 2, 1))
    relax = relaxation.reshape(per, 1, size)
    heat = heat_weight.reshape(per, 1, size)
    drive = jnp.concatenate(gather_far(drive), axis=0)
    small = jnp.concatenate(gather_far(jnp.concatenate([relax, relax * heat], axis=1)), axis=0)
    low, high = drive[:, :half], drive[:, half:]
    mine = jnp.where(core == 0, low, high)
    theirs = jnp.where(core == 0, high, low)
    packed = [theirs] + [jnp.broadcast_to(small[:, k : k + 1], (len(small), 8, size)) for k in range(2)]
    got = swap(jnp.concatenate(packed, axis=1), cores)
    far = 1 << len(far_steps())
    drives, relaxes, heats = [
        [by_core(o, t) for o, t in zip(jnp.split(own, far), jnp.split(other, far))]
        for own, other in (
            (mine, got[:, :half]),
            (small[:, :1], got[:, half : half + 1]),
            (small[:, 1:], got[:, half + 8 : half + 9]),
        )
    ]
    other_values = swap(tile_values, cores)
    drives[-1], other_values = lax.optimization_barrier((drives[-1], other_values))
    fluxes = [r * d for r, d in zip(relaxes, drives)]
    tiles = (tile_values, other_values)
    sizes = [chips // 2 * (high - low) for low, high in zip(edges[:-1], edges[1:])]
    for sweep in range(ITERS):
        pieces = gather_near(fluxes, edges)
        near, far = [p for p, _ in pieces], [p for _, p in pieces]
        base = apply_tiles(0, 0, places, tiles, near, [num // 2, num // 2], 0.5)
        sends = apply_tiles(1, 0, places, tiles, far, sizes, 0.25, base[0])
        keeps = apply_tiles(2, num // 2, places, tiles, far, sizes, 0.25, base[1])
        blocks = reduce_near(keeps, sends)
        if sweep < ITERS - 1:
            fluxes = [r * (d + s) for r, d, s in zip(relaxes, drives, sum_far(blocks))]
    weighted = sum(
        [jnp.sum(w * b, axis=(0, 2)) for w, b in zip(heats, blocks)],
        jnp.sum(heats[0] * drives[0], axis=(0, 2)),
    )
    totals = jnp.pad(jnp.stack([weighted, jnp.full((half,), jnp.sum(heat))]), ((0, 0), (0, size - half)))
    both = by_core(totals[None], swap(totals[None], cores))
    both = jnp.broadcast_to(both.reshape(1, 2 * CORES, size), (chips, 2 * CORES, size))
    both = lax.all_to_all(both, CHIPS, split_axis=0, concat_axis=0, tiled=True)
    both = jnp.sum(both, axis=0).reshape(CORES, 2, size)[:, :, :half]
    conductivity = both[:, 0].reshape(columns) / jnp.sum(both[:, 1, 0])
    flux = relaxes[0] * (drives[0] + after(reduce_far(blocks), conductivity))
    first, second = flux[:per], flux[per:]
    mine = jnp.where(core == 0, first, second)
    got = swap(jnp.where(core == 0, second, first), cores)
    both = jnp.concatenate(
        [jnp.where(core == 0, mine, got), jnp.where(core == 0, got, mine)], axis=1
    )
    mode_flux = jnp.transpose(both, (0, 2, 1)).reshape(modes, columns)
    return (mode_flux, conductivity)


def solution(mesh):
    n_rows, n_cols = mesh.shape["row"], mesh.shape["col"]
    planes = depth_of(n_rows)
    chips = Mesh(mesh.devices.reshape(planes, n_rows // planes, n_cols // CORES, CORES), ALL)
    placed = (
        P(ALL, None, None),
        P(ALL, None),
        P(ALL),
        P(ALL),
        P(ALL),
        P(ALL),
        P(ALL, None),
        P(ALL),
    )
    return jax.shard_map(
        shards,
        mesh=chips,
        in_specs=placed,
        out_specs=(P(ALL, None), P()),
        check_vma=False,
    )
```

```python
import functools

import jax
import jax.numpy as jnp
from jax import lax
from jax.experimental import pallas as pl
from jax.experimental.pallas import tpu as pltpu
from jax.sharding import Mesh
from jax.sharding import PartitionSpec as P

ITERS = 3
CORES = 2
CHUNK = 8
SLOTS = 8
SPANS = 4
VMEM = 48 * 1024 * 1024
CHIPS = ("z", "y", "x")
ALL = ("z", "y", "x", "core")
NEAR = ("x", "y", "z")


def depth_of(n_rows):
    return min(n for n in range(1, n_rows + 1) if n_rows % n == 0 and n * n >= n_rows)


def far_steps():
    return [(a, 1 << k) for a in NEAR for k in range(1, lax.axis_size(a).bit_length() - 1)]


def near_steps(part):
    turn = part % len(NEAR)
    return [(a, 1) for a in NEAR[turn:] + NEAR[:turn]]


def swap(array, step):
    axis, distance = step
    return lax.ppermute(array, axis, [(i, i ^ distance) for i in range(lax.axis_size(axis))])


def after(value, *others):
    return lax.optimization_barrier((value,) + others)[0]


def halves(array):
    middle = array.shape[0] // 2
    return array[:middle], array[middle:]


def gather_far(block):
    blocks = [block]
    for step in reversed(far_steps()):
        got = swap(blocks[0] if len(blocks) == 1 else jnp.concatenate(blocks, axis=0), step)
        blocks = blocks + jnp.split(got, len(blocks))
    return blocks


def gather_near(blocks, edges):
    starts = [
        jnp.concatenate([b[low:high] for b in blocks], axis=0) for low, high in zip(edges[:-1], edges[1:])
    ]
    pieces = []
    for part, block in enumerate(lax.optimization_barrier(starts)):
        steps = near_steps(part)
        for step in reversed(steps[1:]):
            block = jnp.concatenate([block, swap(block, step)], axis=0)
        pieces.append((block, swap(block, steps[0])))
    return pieces


def reduce_near(keeps, sends):
    far = 1 << len(far_steps())
    parts = []
    for part, (keep, send) in enumerate(zip(keeps, sends)):
        steps = near_steps(part)
        got = swap(send, steps[0])
        terms = [keep]
        for step in steps[1:]:
            terms.append(got)
            got = swap(sum([halves(t)[1] for t in terms[1:]], halves(terms[0])[1]), step)
            *terms, got = lax.optimization_barrier((*terms, got))
            terms = [halves(t)[0] for t in terms]
        terms = [jnp.split(t, far) for t in (*terms, got)]
        parts.append([sum(t[1:], t[0]) for t in zip(*terms)])
    return [jnp.concatenate(group, axis=0) for group in zip(*parts)]


def reduce_far(blocks):
    for step in far_steps():
        middle = len(blocks) // 2
        send = blocks[middle:]
        got = swap(jnp.concatenate(send, axis=0) if middle > 1 else send[0], step)
        blocks = [b + g for b, g in zip(blocks[:middle], jnp.split(got, middle))]
    return blocks[0]


def sum_far(blocks):
    count = len(blocks)
    for place, step in enumerate(far_steps()):
        bit = count >> (place + 1)
        got = jnp.split(swap(jnp.concatenate(blocks, axis=0), step), count)
        blocks = [b + got[k ^ bit] for k, b in enumerate(blocks)]
    return blocks


def apply_kernel(span, skip, pieces, has_base, places_ref, own_ref, other_ref, *refs):
    flux, refs = refs[:pieces], refs[pieces:]
    base_ref, refs = (refs[0], refs[1:]) if has_base else (None, refs)
    *outs, flux_ref, sum_ref, held_ref, held_sem = refs
    length = own_ref.shape[0]
    total = 2 * length
    start, stop = places_ref[span], places_ref[span + 1]
    chunks = (stop - start + CHUNK - 1) // CHUNK

    def fetch(chunk):
        slot = lax.rem(chunk, SLOTS)
        for k in range(CHUNK):
            at = places_ref[SPANS + jnp.minimum(start + chunk * CHUNK + k, total - 1)]
            for tiles_ref, low in ((own_ref, 0), (other_ref, length)):

                @pl.when((at >= low) & (at < low + length))
                def _():
                    pltpu.make_async_copy(
                        tiles_ref.at[at - low], held_ref.at[slot, k], held_sem.at[slot]
                    ).start()

    for chunk in range(SLOTS - 1):

        @pl.when(chunk < chunks)
        def _():
            fetch(jnp.int32(chunk))

    done = 0
    for piece in flux:
        flux_ref[done : done + piece.shape[0]] = piece[...]
        done += piece.shape[0]
    if has_base:
        sum_ref[...] = base_ref[...]
    else:
        sum_ref[...] = jnp.zeros_like(sum_ref)

    @pl.loop(0, chunks)
    def _(chunk):
        slot = lax.rem(chunk, SLOTS)
        pltpu.make_async_copy(
            own_ref.at[pl.ds(0, CHUNK)], held_ref.at[slot], held_sem.at[slot]
        ).wait()

        @pl.when(chunk + SLOTS - 1 < chunks)
        def _():
            fetch(chunk + SLOTS - 1)

        products, rows = [], []
        for k in range(CHUNK):
            at = start + chunk * CHUNK + k
            valid = jnp.where(at < stop, 1.0, 0.0)
            at = jnp.minimum(at, stop - 1)
            values = flux_ref[places_ref[SPANS + 2 * total + at]] * valid
            high = values.astype(jnp.bfloat16)
            low = (values - high.astype(jnp.float32)).astype(jnp.bfloat16)
            left = jnp.concatenate([high, low], axis=0)
            tile = held_ref[slot, k]
            high = tile.astype(jnp.bfloat16)
            low = (tile - high.astype(jnp.float32)).astype(jnp.bfloat16)
            both = lax.dot_general(
                jnp.concatenate([left, left], axis=1),
                jnp.concatenate([high, low], axis=1),
                (((1,), (1,)), ((), ())),
                preferred_element_type=jnp.float32,
            )
            temps = values.shape[0]
            products.append(both[:temps] + both[temps:])
            rows.append(places_ref[SPANS + total + at] - skip)
        for row, product in zip(rows, products):
            sum_ref[row] += product

    done = 0
    for out in outs:
        out[...] = sum_ref[done : done + out.shape[0]]
        done += out.shape[0]


def apply_tiles(span, skip, places, tiles, flux, sizes, share, base=None):
    length, size, _ = tiles[0].shape
    temps = flux[0].shape[1]
    rows = sum(sizes)
    inside = pl.BlockSpec(memory_space=pltpu.VMEM)
    given = [*flux] + ([] if base is None else [base])
    return pl.pallas_call(
        functools.partial(apply_kernel, span, skip, len(flux), base is not None),
        out_shape=[jax.ShapeDtypeStruct((n, temps, size), jnp.float32) for n in sizes],
        grid_spec=pltpu.PrefetchScalarGridSpec(
            num_scalar_prefetch=1,
            grid=(),
            in_specs=[pl.BlockSpec(memory_space=pltpu.HBM)] * 2 + [inside] * len(given),
            out_specs=[inside] * len(sizes),
            scratch_shapes=[
                pltpu.VMEM((sum(piece.shape[0] for piece in flux), temps, size), jnp.float32),
                pltpu.VMEM((rows, temps, size), jnp.float32),
                pltpu.VMEM((SLOTS, CHUNK, size, size), jnp.float32),
                pltpu.SemaphoreType.DMA((SLOTS,)),
            ],
        ),
        compiler_params=pltpu.CompilerParams(vmem_limit_bytes=VMEM),
        cost_estimate=pl.CostEstimate(
            flops=int(share * 2 * length * size * size * temps * 8),
            bytes_accessed=int(share * 2 * length * size * size * 4) + 8 * rows * temps * size,
            transcendentals=0,
        ),
    )(places, *tiles, *given)


def shards(
    tile_values, tile_owner, tile_row, tile_col, tile_count, relaxation, driving, heat_weight
):
    n_cols = lax.axis_size("x") * CORES
    chips = lax.axis_size(CHIPS)
    length, size, _ = tile_values.shape
    modes, columns = driving.shape
    per = modes // size
    chip_tiles = CORES * per
    num = chips * chip_tiles
    half = columns // CORES
    core = lax.axis_index("core")
    cores = ("core", 1)

    edges = [chip_tiles * k // len(NEAR) for k in range(len(NEAR) + 1)]

    def place(tile):
        chip, inside = tile // chip_tiles, tile % chip_tiles
        away, width = {}, 1
        for axis in reversed(CHIPS):
            n = lax.axis_size(axis)
            away[axis] = ((chip // width) % n) ^ lax.axis_index(axis)
            width *= n
        side, out = jnp.zeros_like(tile), jnp.zeros_like(tile)
        for part in range(len(NEAR)):
            low, high = edges[part], edges[part + 1]
            (first, _), *steps = near_steps(part)
            slot = jnp.zeros_like(tile)
            for axis, distance in steps + far_steps():
                slot = 2 * slot + (away[axis] // distance) % 2
            slot = chips // 2 * low + slot * (high - low) + inside - low
            out = jnp.where(inside >= low, slot, out)
            side = jnp.where(inside >= low, away[first] % 2, side)
        return side, out

    owners = tile_owner[:, 0]
    row_side, row = place((owners // n_cols) * (n_cols * per) + tile_row)
    col_side, col = place(((tile_col // per) * n_cols + owners % n_cols) * per + tile_col % per)
    used = jnp.arange(length, dtype=jnp.int32) < tile_count[0]
    kind = jnp.where(used, jnp.where(col_side == 0, 0, 2 - row_side), 3)
    row = jnp.where(row_side == 1, row, row + num // 2)
    code = (kind * num + row) * num + col
    other_code = swap(code, cores)
    code = jnp.concatenate([code, other_code])
    kind = code // (num * num)
    slots = jnp.arange(CORES * length, dtype=jnp.int32)
    key = kind * (CORES * length) + slots
    rank = jnp.sum((key[None, :] < key[:, None]).astype(jnp.int32), axis=1)
    ends = jnp.sum((kind[None, :] < jnp.arange(SPANS, dtype=jnp.int32)[:, None]).astype(jnp.int32), axis=1)
    sorts = rank[None, :] == slots[:, None]
    order = jnp.sum(jnp.where(sorts, slots[None, :], 0), axis=1)
    code = jnp.sum(jnp.where(sorts, code[None, :] % (num * num), 0), axis=1)
    places = jnp.concatenate([ends, order, code // num, code % num])

    def by_core(own, other):
        return jnp.concatenate(
            [jnp.where(core == 0, own, other), jnp.where(core == 0, other, own)], axis=0
        )

    drive = jnp.transpose(driving.reshape(per, size, columns), (0, 2, 1))
    relax = relaxation.reshape(per, 1, size)
    heat = heat_weight.reshape(per, 1, size)
    drive = jnp.concatenate(gather_far(drive), axis=0)
    small = jnp.concatenate(gather_far(jnp.concatenate([relax, relax * heat], axis=1)), axis=0)
    low, high = drive[:, :half], drive[:, half:]
    mine = jnp.where(core == 0, low, high)
    theirs = jnp.where(core == 0, high, low)
    packed = [theirs] + [jnp.broadcast_to(small[:, k : k + 1], (len(small), 8, size)) for k in range(2)]
    got = swap(jnp.concatenate(packed, axis=1), cores)
    far = 1 << len(far_steps())
    drives, relaxes, heats = [
        [by_core(o, t) for o, t in zip(jnp.split(own, far), jnp.split(other, far))]
        for own, other in (
            (mine, got[:, :half]),
            (small[:, :1], got[:, half : half + 1]),
            (small[:, 1:], got[:, half + 8 : half + 9]),
        )
    ]
    other_values = swap(tile_values, cores)
    drives[-1], other_values = lax.optimization_barrier((drives[-1], other_values))
    fluxes = [r * d for r, d in zip(relaxes, drives)]
    tiles = (tile_values, other_values)
    sizes = [chips // 2 * (high - low) for low, high in zip(edges[:-1], edges[1:])]
    for sweep in range(ITERS):
        pieces = gather_near(fluxes, edges)
        near, far = [p for p, _ in pieces], [p for _, p in pieces]
        base = apply_tiles(0, 0, places, tiles, near, [num // 2, num // 2], 0.5)
        sends = apply_tiles(1, 0, places, tiles, far, sizes, 0.25, base[0])
        keeps = apply_tiles(2, num // 2, places, tiles, far, sizes, 0.25, base[1])
        blocks = reduce_near(keeps, sends)
        if sweep < ITERS - 1:
            fluxes = [r * (d + s) for r, d, s in zip(relaxes, drives, sum_far(blocks))]
    weighted = sum(
        [jnp.sum(w * b, axis=(0, 2)) for w, b in zip(heats, lax.optimization_barrier(blocks))],
        jnp.sum(heats[0] * drives[0], axis=(0, 2)),
    )
    totals = jnp.pad(jnp.stack([weighted, jnp.full((half,), jnp.sum(heat))]), ((0, 0), (0, size - half)))
    both = by_core(totals[None], swap(totals[None], cores))
    both = jnp.broadcast_to(both.reshape(1, 2 * CORES, size), (chips, 2 * CORES, size))
    both = lax.all_to_all(both, CHIPS, split_axis=0, concat_axis=0, tiled=True)
    both = jnp.sum(both, axis=0).reshape(CORES, 2, size)[:, :, :half]
    conductivity = both[:, 0].reshape(columns) / jnp.sum(both[:, 1, 0])
    flux = relaxes[0] * (drives[0] + after(reduce_far(blocks), conductivity))
    first, second = flux[:per], flux[per:]
    mine = jnp.where(core == 0, first, second)
    got = swap(jnp.where(core == 0, second, first), cores)
    both = jnp.concatenate(
        [jnp.where(core == 0, mine, got), jnp.where(core == 0, got, mine)], axis=1
    )
    mode_flux = jnp.transpose(both, (0, 2, 1)).reshape(modes, columns)
    return (mode_flux, conductivity)


def solution(mesh):
    n_rows, n_cols = mesh.shape["row"], mesh.shape["col"]
    planes = depth_of(n_rows)
    chips = Mesh(mesh.devices.reshape(planes, n_rows // planes, n_cols // CORES, CORES), ALL)
    placed = (
        P(ALL, None, None),
        P(ALL, None),
        P(ALL),
        P(ALL),
        P(ALL),
        P(ALL),
        P(ALL, None),
        P(ALL),
    )
    return jax.shard_map(
        shards,
        mesh=chips,
        in_specs=placed,
        out_specs=(P(ALL, None), P()),
        check_vma=False,
    )
```

```python
import functools

import jax
import jax.numpy as jnp
from jax import lax
from jax.experimental import pallas as pl
from jax.experimental.pallas import tpu as pltpu
from jax.sharding import Mesh
from jax.sharding import PartitionSpec as P

ITERS = 3
CORES = 2
CHUNK = 8
SLOTS = 8
SPANS = 4
VMEM = 48 * 1024 * 1024
CHIPS = ("z", "y", "x")
ALL = ("z", "y", "x", "core")
NEAR = ("x", "y", "z")


def depth_of(n_rows):
    return min(n for n in range(1, n_rows + 1) if n_rows % n == 0 and n * n >= n_rows)


def far_steps():
    return [(a, 1 << k) for a in NEAR for k in range(1, lax.axis_size(a).bit_length() - 1)]


def near_steps(part):
    turn = part % len(NEAR)
    return [(a, 1) for a in NEAR[turn:] + NEAR[:turn]]


def swap(array, step):
    axis, distance = step
    return lax.ppermute(array, axis, [(i, i ^ distance) for i in range(lax.axis_size(axis))])


def after(value, *others):
    return lax.optimization_barrier((value,) + others)[0]


def halves(array):
    middle = array.shape[0] // 2
    return array[:middle], array[middle:]


def gather_far(block):
    blocks = [block]
    for step in reversed(far_steps()):
        got = swap(blocks[0] if len(blocks) == 1 else jnp.concatenate(blocks, axis=0), step)
        blocks = blocks + jnp.split(got, len(blocks))
    return blocks


def gather_near(blocks, edges):
    starts = [
        jnp.concatenate([b[low:high] for b in blocks], axis=0) for low, high in zip(edges[:-1], edges[1:])
    ]
    pieces = []
    for part, block in enumerate(lax.optimization_barrier(starts)):
        steps = near_steps(part)
        for step in reversed(steps[1:]):
            block = jnp.concatenate([block, swap(block, step)], axis=0)
        pieces.append((block, swap(block, steps[0])))
    return pieces


def reduce_near(keeps, sends):
    far = 1 << len(far_steps())
    parts = []
    for part, (keep, send) in enumerate(zip(keeps, sends)):
        steps = near_steps(part)
        got = swap(send, steps[0])
        terms = [keep]
        for step in steps[1:]:
            terms.append(got)
            got = swap(sum([halves(t)[1] for t in terms[1:]], halves(terms[0])[1]), step)
            *terms, got = lax.optimization_barrier((*terms, got))
            terms = [halves(t)[0] for t in terms]
        terms = [jnp.split(t, far) for t in (*terms, got)]
        parts.append([sum(t[1:], t[0]) for t in zip(*terms)])
    return [jnp.concatenate(group, axis=0) for group in zip(*parts)]


def reduce_far(blocks):
    for step in far_steps():
        middle = len(blocks) // 2
        send = blocks[middle:]
        got = swap(jnp.concatenate(send, axis=0) if middle > 1 else send[0], step)
        blocks = [b + g for b, g in zip(blocks[:middle], jnp.split(got, middle))]
    return blocks[0]


def sum_far(blocks):
    count = len(blocks)
    for place, step in enumerate(far_steps()):
        bit = count >> (place + 1)
        got = jnp.split(swap(jnp.concatenate(blocks, axis=0), step), count)
        blocks = [b + got[k ^ bit] for k, b in enumerate(blocks)]
    return blocks


def apply_kernel(span, skip, pieces, has_base, places_ref, own_ref, other_ref, *refs):
    flux, refs = refs[:pieces], refs[pieces:]
    base_ref, refs = (refs[0], refs[1:]) if has_base else (None, refs)
    *outs, flux_ref, sum_ref, held_ref, held_sem = refs
    length = own_ref.shape[0]
    total = 2 * length
    start, stop = places_ref[span], places_ref[span + 1]
    chunks = (stop - start + CHUNK - 1) // CHUNK

    def fetch(chunk):
        slot = lax.rem(chunk, SLOTS)
        for k in range(CHUNK):
            at = places_ref[SPANS + jnp.minimum(start + chunk * CHUNK + k, total - 1)]
            for tiles_ref, low in ((own_ref, 0), (other_ref, length)):

                @pl.when((at >= low) & (at < low + length))
                def _():
                    pltpu.make_async_copy(
                        tiles_ref.at[at - low], held_ref.at[slot, k], held_sem.at[slot]
                    ).start()

    for chunk in range(SLOTS - 1):

        @pl.when(chunk < chunks)
        def _():
            fetch(jnp.int32(chunk))

    done = 0
    for piece in flux:
        flux_ref[done : done + piece.shape[0]] = piece[...]
        done += piece.shape[0]
    if has_base:
        sum_ref[...] = base_ref[...]
    else:
        sum_ref[...] = jnp.zeros_like(sum_ref)

    @pl.loop(0, chunks)
    def _(chunk):
        slot = lax.rem(chunk, SLOTS)
        pltpu.make_async_copy(
            own_ref.at[pl.ds(0, CHUNK)], held_ref.at[slot], held_sem.at[slot]
        ).wait()

        @pl.when(chunk + SLOTS - 1 < chunks)
        def _():
            fetch(chunk + SLOTS - 1)

        products, rows = [], []
        for k in range(CHUNK):
            at = start + chunk * CHUNK + k
            valid = jnp.where(at < stop, 1.0, 0.0)
            at = jnp.minimum(at, stop - 1)
            values = flux_ref[places_ref[SPANS + 2 * total + at]] * valid
            high = values.astype(jnp.bfloat16)
            low = (values - high.astype(jnp.float32)).astype(jnp.bfloat16)
            left = jnp.concatenate([high, low], axis=0)
            tile = held_ref[slot, k]
            high = tile.astype(jnp.bfloat16)
            low = (tile - high.astype(jnp.float32)).astype(jnp.bfloat16)
            both = lax.dot_general(
                jnp.concatenate([left, left], axis=1),
                jnp.concatenate([high, low], axis=1),
                (((1,), (1,)), ((), ())),
                preferred_element_type=jnp.float32,
            )
            temps = values.shape[0]
            products.append(both[:temps] + both[temps:])
            rows.append(places_ref[SPANS + total + at] - skip)
        for row, product in zip(rows, products):
            sum_ref[row] += product

    done = 0
    for out in outs:
        out[...] = sum_ref[done : done + out.shape[0]]
        done += out.shape[0]


def apply_tiles(span, skip, places, tiles, flux, sizes, share, base=None):
    length, size, _ = tiles[0].shape
    temps = flux[0].shape[1]
    rows = sum(sizes)
    inside = pl.BlockSpec(memory_space=pltpu.VMEM)
    given = [*flux] + ([] if base is None else [base])
    return pl.pallas_call(
        functools.partial(apply_kernel, span, skip, len(flux), base is not None),
        out_shape=[jax.ShapeDtypeStruct((n, temps, size), jnp.float32) for n in sizes],
        grid_spec=pltpu.PrefetchScalarGridSpec(
            num_scalar_prefetch=1,
            grid=(),
            in_specs=[pl.BlockSpec(memory_space=pltpu.HBM)] * 2 + [inside] * len(given),
            out_specs=[inside] * len(sizes),
            scratch_shapes=[
                pltpu.VMEM((sum(piece.shape[0] for piece in flux), temps, size), jnp.float32),
                pltpu.VMEM((rows, temps, size), jnp.float32),
                pltpu.VMEM((SLOTS, CHUNK, size, size), jnp.float32),
                pltpu.SemaphoreType.DMA((SLOTS,)),
            ],
        ),
        compiler_params=pltpu.CompilerParams(vmem_limit_bytes=VMEM),
        cost_estimate=pl.CostEstimate(
            flops=int(share * 2 * length * size * size * temps * 8),
            bytes_accessed=int(share * 2 * length * size * size * 4) + 8 * rows * temps * size,
            transcendentals=0,
        ),
    )(places, *tiles, *given)


def shards(
    tile_values, tile_owner, tile_row, tile_col, tile_count, relaxation, driving, heat_weight
):
    n_cols = lax.axis_size("x") * CORES
    chips = lax.axis_size(CHIPS)
    length, size, _ = tile_values.shape
    modes, columns = driving.shape
    per = modes // size
    chip_tiles = CORES * per
    num = chips * chip_tiles
    half = columns // CORES
    core = lax.axis_index("core")
    cores = ("core", 1)

    edges = [chip_tiles * k // len(NEAR) for k in range(len(NEAR) + 1)]

    def place(tile):
        chip, inside = tile // chip_tiles, tile % chip_tiles
        away, width = {}, 1
        for axis in reversed(CHIPS):
            n = lax.axis_size(axis)
            away[axis] = ((chip // width) % n) ^ lax.axis_index(axis)
            width *= n
        side, out = jnp.zeros_like(tile), jnp.zeros_like(tile)
        for part in range(len(NEAR)):
            low, high = edges[part], edges[part + 1]
            (first, _), *steps = near_steps(part)
            slot = jnp.zeros_like(tile)
            for axis, distance in steps + far_steps():
                slot = 2 * slot + (away[axis] // distance) % 2
            slot = chips // 2 * low + slot * (high - low) + inside - low
            out = jnp.where(inside >= low, slot, out)
            side = jnp.where(inside >= low, away[first] % 2, side)
        return side, out

    owners = tile_owner[:, 0]
    row_side, row = place((owners // n_cols) * (n_cols * per) + tile_row)
    col_side, col = place(((tile_col // per) * n_cols + owners % n_cols) * per + tile_col % per)
    used = jnp.arange(length, dtype=jnp.int32) < tile_count[0]
    kind = jnp.where(used, jnp.where(col_side == 0, 0, 2 - row_side), 3)
    row = jnp.where(row_side == 1, row, row + num // 2)
    code = (kind * num + row) * num + col
    other_code = swap(code, cores)
    code = jnp.concatenate([code, other_code])
    kind = code // (num * num)
    slots = jnp.arange(CORES * length, dtype=jnp.int32)
    key = kind * (CORES * length) + slots
    rank = jnp.sum((key[None, :] < key[:, None]).astype(jnp.int32), axis=1)
    ends = jnp.sum((kind[None, :] < jnp.arange(SPANS, dtype=jnp.int32)[:, None]).astype(jnp.int32), axis=1)
    sorts = rank[None, :] == slots[:, None]
    order = jnp.sum(jnp.where(sorts, slots[None, :], 0), axis=1)
    code = jnp.sum(jnp.where(sorts, code[None, :] % (num * num), 0), axis=1)
    places = jnp.concatenate([ends, order, code // num, code % num])

    def by_core(own, other):
        return jnp.concatenate(
            [jnp.where(core == 0, own, other), jnp.where(core == 0, other, own)], axis=0
        )

    drive = jnp.transpose(driving.reshape(per, size, columns), (0, 2, 1))
    relax = relaxation.reshape(per, 1, size)
    heat = heat_weight.reshape(per, 1, size)
    drive = jnp.concatenate(gather_far(drive), axis=0)
    small = jnp.concatenate(gather_far(jnp.concatenate([relax, relax * heat], axis=1)), axis=0)
    low, high = drive[:, :half], drive[:, half:]
    mine = jnp.where(core == 0, low, high)
    theirs = jnp.where(core == 0, high, low)
    packed = [theirs] + [jnp.broadcast_to(small[:, k : k + 1], (len(small), 8, size)) for k in range(2)]
    got = swap(jnp.concatenate(packed, axis=1), cores)
    far = 1 << len(far_steps())
    drives, relaxes, heats = [
        [by_core(o, t) for o, t in zip(jnp.split(own, far), jnp.split(other, far))]
        for own, other in (
            (mine, got[:, :half]),
            (small[:, :1], got[:, half : half + 1]),
            (small[:, 1:], got[:, half + 8 : half + 9]),
        )
    ]
    other_values = swap(tile_values, cores)
    drives[-1], other_values = lax.optimization_barrier((drives[-1], other_values))
    fluxes = [r * d for r, d in zip(relaxes, drives)]
    tiles = (tile_values, other_values)
    sizes = [chips // 2 * (high - low) for low, high in zip(edges[:-1], edges[1:])]
    for sweep in range(ITERS):
        pieces = gather_near(fluxes, edges)
        near, far = [p for p, _ in pieces], [p for _, p in pieces]
        base = apply_tiles(0, 0, places, tiles, near, [num // 2, num // 2], 0.5)
        sends = apply_tiles(1, 0, places, tiles, far, sizes, 0.25, base[0])
        keeps = apply_tiles(2, num // 2, places, tiles, far, sizes, 0.25, base[1])
        blocks = reduce_near(keeps, sends)
        if sweep < ITERS - 1:
            fluxes = [r * (d + s) for r, d, s in zip(relaxes, drives, sum_far(blocks))]
    weighted = sum(
        [jnp.sum(w * b, axis=(0, 2)) for w, b in zip(heats, blocks)],
        jnp.sum(heats[0] * drives[0], axis=(0, 2)),
    )
    totals = jnp.concatenate([weighted, jnp.sum(heat).reshape(1)])
    totals = jnp.pad(totals[None], ((0, 0), (0, size - half - 1)))
    *blocks, totals = lax.optimization_barrier((*blocks, totals))
    totals = lax.all_to_all(
        jnp.broadcast_to(totals, (chips, size)), CHIPS, split_axis=0, concat_axis=0, tiled=True
    )
    totals = jnp.sum(totals, axis=0, keepdims=True)
    totals = by_core(totals, swap(totals, cores))
    conductivity = totals[:, :half].reshape(columns) / jnp.sum(totals[:, half])
    flux = relaxes[0] * (drives[0] + after(reduce_far(blocks), conductivity))
    first, second = flux[:per], flux[per:]
    mine = jnp.where(core == 0, first, second)
    got = swap(jnp.where(core == 0, second, first), cores)
    both = jnp.concatenate(
        [jnp.where(core == 0, mine, got), jnp.where(core == 0, got, mine)], axis=1
    )
    mode_flux = jnp.transpose(both, (0, 2, 1)).reshape(modes, columns)
    return (mode_flux, conductivity)


def solution(mesh):
    n_rows, n_cols = mesh.shape["row"], mesh.shape["col"]
    planes = depth_of(n_rows)
    chips = Mesh(mesh.devices.reshape(planes, n_rows // planes, n_cols // CORES, CORES), ALL)
    placed = (
        P(ALL, None, None),
        P(ALL, None),
        P(ALL),
        P(ALL),
        P(ALL),
        P(ALL),
        P(ALL, None),
        P(ALL),
    )
    return jax.shard_map(
        shards,
        mesh=chips,
        in_specs=placed,
        out_specs=(P(ALL, None), P()),
        check_vma=False,
    )
```

```python
import functools

import jax
import jax.numpy as jnp
from jax import lax
from jax.experimental import pallas as pl
from jax.experimental.pallas import tpu as pltpu
from jax.sharding import Mesh
from jax.sharding import PartitionSpec as P

ITERS = 3
CORES = 2
CHUNK = 8
SLOTS = 8
SPANS = 4
VMEM = 48 * 1024 * 1024
CHIPS = ("z", "y", "x")
ALL = ("z", "y", "x", "core")
NEAR = ("x", "y", "z")


def depth_of(n_rows):
    return min(n for n in range(1, n_rows + 1) if n_rows % n == 0 and n * n >= n_rows)


def far_steps():
    return [(a, 1 << k) for a in NEAR for k in range(1, lax.axis_size(a).bit_length() - 1)]


def near_steps(part):
    turn = part % len(NEAR)
    return [(a, 1) for a in NEAR[turn:] + NEAR[:turn]]


def swap(array, step):
    axis, distance = step
    return lax.ppermute(array, axis, [(i, i ^ distance) for i in range(lax.axis_size(axis))])


def after(value, *others):
    return lax.optimization_barrier((value,) + others)[0]


def halves(array):
    middle = array.shape[0] // 2
    return array[:middle], array[middle:]


def gather_far(block):
    blocks = [block]
    for step in reversed(far_steps()):
        got = swap(blocks[0] if len(blocks) == 1 else jnp.concatenate(blocks, axis=0), step)
        blocks = blocks + jnp.split(got, len(blocks))
    return blocks


def gather_near(blocks, edges):
    starts = [
        jnp.concatenate([b[low:high] for b in blocks], axis=0) for low, high in zip(edges[:-1], edges[1:])
    ]
    pieces = []
    for part, block in enumerate(lax.optimization_barrier(starts)):
        steps = near_steps(part)
        for step in reversed(steps[1:]):
            block = jnp.concatenate([block, swap(block, step)], axis=0)
        pieces.append((block, swap(block, steps[0])))
    return pieces


def reduce_near(keeps, sends):
    far = 1 << len(far_steps())
    parts = []
    for part, (keep, send) in enumerate(zip(keeps, sends)):
        steps = near_steps(part)
        got = swap(send, steps[0])
        terms = [keep]
        for step in steps[1:]:
            terms.append(got)
            got = swap(sum([halves(t)[1] for t in terms[1:]], halves(terms[0])[1]), step)
            *terms, got = lax.optimization_barrier((*terms, got))
            terms = [halves(t)[0] for t in terms]
        terms = [jnp.split(t, far) for t in (*terms, got)]
        parts.append([sum(t[1:], t[0]) for t in zip(*terms)])
    return [jnp.concatenate(group, axis=0) for group in zip(*parts)]


def reduce_far(blocks):
    for step in far_steps():
        middle = len(blocks) // 2
        send = blocks[middle:]
        got = swap(jnp.concatenate(send, axis=0) if middle > 1 else send[0], step)
        blocks = [b + g for b, g in zip(blocks[:middle], jnp.split(got, middle))]
    return blocks[0]


def sum_far(blocks):
    count = len(blocks)
    for place, step in enumerate(far_steps()):
        bit = count >> (place + 1)
        got = jnp.split(swap(jnp.concatenate(blocks, axis=0), step), count)
        blocks = [b + got[k ^ bit] for k, b in enumerate(blocks)]
    return blocks


def apply_kernel(span, skip, pieces, has_base, places_ref, own_ref, other_ref, *refs):
    flux, refs = refs[:pieces], refs[pieces:]
    base_ref, refs = (refs[0], refs[1:]) if has_base else (None, refs)
    *outs, flux_ref, sum_ref, held_ref, held_sem = refs
    length = own_ref.shape[0]
    total = 2 * length
    start, stop = places_ref[span], places_ref[span + 1]
    chunks = (stop - start + CHUNK - 1) // CHUNK

    def fetch(chunk):
        slot = lax.rem(chunk, SLOTS)
        for k in range(CHUNK):
            at = places_ref[SPANS + jnp.minimum(start + chunk * CHUNK + k, total - 1)]
            for tiles_ref, low in ((own_ref, 0), (other_ref, length)):

                @pl.when((at >= low) & (at < low + length))
                def _():
                    pltpu.make_async_copy(
                        tiles_ref.at[at - low], held_ref.at[slot, k], held_sem.at[slot]
                    ).start()

    for chunk in range(SLOTS - 1):

        @pl.when(chunk < chunks)
        def _():
            fetch(jnp.int32(chunk))

    done = 0
    for piece in flux:
        flux_ref[done : done + piece.shape[0]] = piece[...]
        done += piece.shape[0]
    if has_base:
        sum_ref[...] = base_ref[...]
    else:
        sum_ref[...] = jnp.zeros_like(sum_ref)

    @pl.loop(0, chunks)
    def _(chunk):
        slot = lax.rem(chunk, SLOTS)
        pltpu.make_async_copy(
            own_ref.at[pl.ds(0, CHUNK)], held_ref.at[slot], held_sem.at[slot]
        ).wait()

        @pl.when(chunk + SLOTS - 1 < chunks)
        def _():
            fetch(chunk + SLOTS - 1)

        products, rows = [], []
        for k in range(CHUNK):
            at = start + chunk * CHUNK + k
            valid = jnp.where(at < stop, 1.0, 0.0)
            at = jnp.minimum(at, stop - 1)
            values = flux_ref[places_ref[SPANS + 2 * total + at]] * valid
            high = values.astype(jnp.bfloat16)
            low = (values - high.astype(jnp.float32)).astype(jnp.bfloat16)
            left = jnp.concatenate([high, low], axis=0)
            tile = held_ref[slot, k]
            high = tile.astype(jnp.bfloat16)
            low = (tile - high.astype(jnp.float32)).astype(jnp.bfloat16)
            both = lax.dot_general(
                jnp.concatenate([left, left], axis=1),
                jnp.concatenate([high, low], axis=1),
                (((1,), (1,)), ((), ())),
                preferred_element_type=jnp.float32,
            )
            temps = values.shape[0]
            products.append(both[:temps] + both[temps:])
            rows.append(places_ref[SPANS + total + at] - skip)
        for row, product in zip(rows, products):
            sum_ref[row] += product

    done = 0
    for out in outs:
        out[...] = sum_ref[done : done + out.shape[0]]
        done += out.shape[0]


def apply_tiles(span, skip, places, tiles, flux, sizes, share, base=None):
    length, size, _ = tiles[0].shape
    temps = flux[0].shape[1]
    rows = sum(sizes)
    inside = pl.BlockSpec(memory_space=pltpu.VMEM)
    given = [*flux] + ([] if base is None else [base])
    return pl.pallas_call(
        functools.partial(apply_kernel, span, skip, len(flux), base is not None),
        out_shape=[jax.ShapeDtypeStruct((n, temps, size), jnp.float32) for n in sizes],
        grid_spec=pltpu.PrefetchScalarGridSpec(
            num_scalar_prefetch=1,
            grid=(),
            in_specs=[pl.BlockSpec(memory_space=pltpu.HBM)] * 2 + [inside] * len(given),
            out_specs=[inside] * len(sizes),
            scratch_shapes=[
                pltpu.VMEM((sum(piece.shape[0] for piece in flux), temps, size), jnp.float32),
                pltpu.VMEM((rows, temps, size), jnp.float32),
                pltpu.VMEM((SLOTS, CHUNK, size, size), jnp.float32),
                pltpu.SemaphoreType.DMA((SLOTS,)),
            ],
        ),
        compiler_params=pltpu.CompilerParams(vmem_limit_bytes=VMEM),
        cost_estimate=pl.CostEstimate(
            flops=int(share * 2 * length * size * size * temps * 8),
            bytes_accessed=int(share * 2 * length * size * size * 4) + 8 * rows * temps * size,
            transcendentals=0,
        ),
    )(places, *tiles, *given)


def shards(
    tile_values, tile_owner, tile_row, tile_col, tile_count, relaxation, driving, heat_weight
):
    n_cols = lax.axis_size("x") * CORES
    chips = lax.axis_size(CHIPS)
    length, size, _ = tile_values.shape
    modes, columns = driving.shape
    per = modes // size
    chip_tiles = CORES * per
    num = chips * chip_tiles
    half = columns // CORES
    core = lax.axis_index("core")
    cores = ("core", 1)

    edges = [chip_tiles * k // len(NEAR) for k in range(len(NEAR) + 1)]

    def place(tile):
        chip, inside = tile // chip_tiles, tile % chip_tiles
        away, width = {}, 1
        for axis in reversed(CHIPS):
            n = lax.axis_size(axis)
            away[axis] = ((chip // width) % n) ^ lax.axis_index(axis)
            width *= n
        side, out = jnp.zeros_like(tile), jnp.zeros_like(tile)
        for part in range(len(NEAR)):
            low, high = edges[part], edges[part + 1]
            (first, _), *steps = near_steps(part)
            slot = jnp.zeros_like(tile)
            for axis, distance in steps + far_steps():
                slot = 2 * slot + (away[axis] // distance) % 2
            slot = chips // 2 * low + slot * (high - low) + inside - low
            out = jnp.where(inside >= low, slot, out)
            side = jnp.where(inside >= low, away[first] % 2, side)
        return side, out

    owners = tile_owner[:, 0]
    row_side, row = place((owners // n_cols) * (n_cols * per) + tile_row)
    col_side, col = place(((tile_col // per) * n_cols + owners % n_cols) * per + tile_col % per)
    used = jnp.arange(length, dtype=jnp.int32) < tile_count[0]
    kind = jnp.where(used, jnp.where(col_side == 0, 0, 2 - row_side), 3)
    row = jnp.where(row_side == 1, row, row + num // 2)
    code = (kind * num + row) * num + col
    other_code = swap(code, cores)
    code = jnp.concatenate([code, other_code])
    kind = code // (num * num)
    slots = jnp.arange(CORES * length, dtype=jnp.int32)
    key = kind * (CORES * length) + slots
    rank = jnp.sum((key[None, :] < key[:, None]).astype(jnp.int32), axis=1)
    ends = jnp.sum((kind[None, :] < jnp.arange(SPANS, dtype=jnp.int32)[:, None]).astype(jnp.int32), axis=1)
    sorts = rank[None, :] == slots[:, None]
    order = jnp.sum(jnp.where(sorts, slots[None, :], 0), axis=1)
    code = jnp.sum(jnp.where(sorts, code[None, :] % (num * num), 0), axis=1)
    places = jnp.concatenate([ends, order, code // num, code % num])

    def by_core(own, other):
        return jnp.concatenate(
            [jnp.where(core == 0, own, other), jnp.where(core == 0, other, own)], axis=0
        )

    drive = jnp.transpose(driving.reshape(per, size, columns), (0, 2, 1))
    relax = relaxation.reshape(per, 1, size)
    heat = heat_weight.reshape(per, 1, size)
    low, high = drive[:, :half], drive[:, half:]
    mine = jnp.where(core == 0, low, high)
    theirs = jnp.where(core == 0, high, low)
    packed = [theirs, jnp.broadcast_to(relax, (per, 8, size)), jnp.broadcast_to(heat, (per, 8, size))]
    got = swap(jnp.concatenate(packed, axis=1), cores)
    tile_values = after(tile_values, got, other_code)
    other_values = swap(tile_values, cores)
    drive_half = by_core(mine, got[:, :half])
    relax_both = by_core(relax, got[:, half : half + 1])
    heat_both = by_core(heat, got[:, half + 8 : half + 9])

    drives = gather_far(drive_half)
    small = gather_far(jnp.concatenate([relax_both, heat_both * relax_both], axis=1))
    relaxes, heats = [s[:, :1] for s in small], [s[:, 1:] for s in small]
    drives[-1], other_values = lax.optimization_barrier((drives[-1], other_values))
    fluxes = [r * d for r, d in zip(relaxes, drives)]
    tiles = (tile_values, other_values)
    sizes = [chips // 2 * (high - low) for low, high in zip(edges[:-1], edges[1:])]
    for sweep in range(ITERS):
        pieces = gather_near(fluxes, edges)
        near, far = [p for p, _ in pieces], [p for _, p in pieces]
        base = apply_tiles(0, 0, places, tiles, near, [num // 2, num // 2], 0.5)
        sends = apply_tiles(1, 0, places, tiles, far, sizes, 0.25, base[0])
        keeps = apply_tiles(2, num // 2, places, tiles, far, sizes, 0.25, base[1])
        blocks = reduce_near(keeps, sends)
        if sweep < ITERS - 1:
            fluxes = [r * (d + s) for r, d, s in zip(relaxes, drives, sum_far(blocks))]
    weighted = sum(
        [jnp.sum(w * b, axis=(0, 2)) for w, b in zip(heats, blocks)],
        jnp.sum(heats[0] * drive_half, axis=(0, 2)),
    )
    totals = jnp.concatenate([weighted, jnp.sum(heat).reshape(1)])
    totals = jnp.pad(totals[None], ((0, 0), (0, size - half - 1)))
    *blocks, totals = lax.optimization_barrier((*blocks, totals))
    totals = lax.all_to_all(
        jnp.broadcast_to(totals, (chips * CORES, size)), ALL, split_axis=0, concat_axis=0, tiled=True
    )
    totals = jnp.sum(totals.reshape(chips, CORES, size), axis=0)
    conductivity = totals[:, :half].reshape(columns) / jnp.sum(totals[:, half])
    flux = relax_both * (drive_half + reduce_far(blocks))
    first, second = flux[:per], flux[per:]
    mine = jnp.where(core == 0, first, second)
    got = swap(jnp.where(core == 0, second, first), cores)
    both = jnp.concatenate(
        [jnp.where(core == 0, mine, got), jnp.where(core == 0, got, mine)], axis=1
    )
    mode_flux = jnp.transpose(both, (0, 2, 1)).reshape(modes, columns)
    return (mode_flux, conductivity)


def solution(mesh):
    n_rows, n_cols = mesh.shape["row"], mesh.shape["col"]
    planes = depth_of(n_rows)
    chips = Mesh(mesh.devices.reshape(planes, n_rows // planes, n_cols // CORES, CORES), ALL)
    placed = (
        P(ALL, None, None),
        P(ALL, None),
        P(ALL),
        P(ALL),
        P(ALL),
        P(ALL),
        P(ALL, None),
        P(ALL),
    )
    return jax.shard_map(
        shards,
        mesh=chips,
        in_specs=placed,
        out_specs=(P(ALL, None), P()),
        check_vma=False,
    )
```

```python
import functools

import jax
import jax.numpy as jnp
from jax import lax
from jax.experimental import pallas as pl
from jax.experimental.pallas import tpu as pltpu
from jax.sharding import Mesh
from jax.sharding import PartitionSpec as P

ITERS = 3
CORES = 2
CHUNK = 8
SLOTS = 8
SPANS = 4
VMEM = 48 * 1024 * 1024
CHIPS = ("z", "y", "x")
ALL = ("z", "y", "x", "core")
NEAR = ("z", "x", "y")


def depth_of(n_rows):
    return min(n for n in range(1, n_rows + 1) if n_rows % n == 0 and n * n >= n_rows)


def far_steps():
    return [(a, 1 << k) for a in NEAR for k in range(1, lax.axis_size(a).bit_length() - 1)]


def near_steps(part):
    turn = part % len(NEAR)
    return [(a, 1) for a in NEAR[turn:] + NEAR[:turn]]


def swap(array, step):
    axis, distance = step
    return lax.ppermute(array, axis, [(i, i ^ distance) for i in range(lax.axis_size(axis))])


def after(value, *others):
    return lax.optimization_barrier((value,) + others)[0]


def halves(array):
    middle = array.shape[0] // 2
    return array[:middle], array[middle:]


def gather_far(block):
    blocks = [block]
    for step in reversed(far_steps()):
        got = swap(blocks[0] if len(blocks) == 1 else jnp.concatenate(blocks, axis=0), step)
        blocks = blocks + jnp.split(got, len(blocks))
    return blocks


def gather_near(blocks, edges):
    starts = [
        jnp.concatenate([b[low:high] for b in blocks], axis=0) for low, high in zip(edges[:-1], edges[1:])
    ]
    pieces = []
    for part, block in enumerate(lax.optimization_barrier(starts)):
        steps = near_steps(part)
        for step in reversed(steps[1:]):
            block = jnp.concatenate([block, swap(block, step)], axis=0)
        pieces.append((block, swap(block, steps[0])))
    return pieces


def reduce_near(keeps, sends):
    far = 1 << len(far_steps())
    parts = []
    for part, (keep, send) in enumerate(zip(keeps, sends)):
        steps = near_steps(part)
        got = swap(send, steps[0])
        terms = [keep]
        for step in steps[1:]:
            terms.append(got)
            got = swap(sum([halves(t)[1] for t in terms[1:]], halves(terms[0])[1]), step)
            *terms, got = lax.optimization_barrier((*terms, got))
            terms = [halves(t)[0] for t in terms]
        terms = [jnp.split(t, far) for t in (*terms, got)]
        parts.append([sum(t[1:], t[0]) for t in zip(*terms)])
    return [jnp.concatenate(group, axis=0) for group in zip(*parts)]


def reduce_far(blocks):
    for step in far_steps():
        middle = len(blocks) // 2
        send = blocks[middle:]
        got = swap(jnp.concatenate(send, axis=0) if middle > 1 else send[0], step)
        blocks = [b + g for b, g in zip(blocks[:middle], jnp.split(got, middle))]
    return blocks[0]


def sum_far(blocks):
    count = len(blocks)
    for place, step in enumerate(far_steps()):
        bit = count >> (place + 1)
        got = jnp.split(swap(jnp.concatenate(blocks, axis=0), step), count)
        blocks = [b + got[k ^ bit] for k, b in enumerate(blocks)]
    return blocks


def apply_kernel(span, skip, pieces, has_base, places_ref, own_ref, other_ref, *refs):
    flux, refs = refs[:pieces], refs[pieces:]
    base_ref, refs = (refs[0], refs[1:]) if has_base else (None, refs)
    *outs, flux_ref, sum_ref, held_ref, held_sem = refs
    length = own_ref.shape[0]
    total = 2 * length
    start, stop = places_ref[span], places_ref[span + 1]
    chunks = (stop - start + CHUNK - 1) // CHUNK

    def fetch(chunk):
        slot = lax.rem(chunk, SLOTS)
        for k in range(CHUNK):
            at = places_ref[SPANS + jnp.minimum(start + chunk * CHUNK + k, total - 1)]
            for tiles_ref, low in ((own_ref, 0), (other_ref, length)):

                @pl.when((at >= low) & (at < low + length))
                def _():
                    pltpu.make_async_copy(
                        tiles_ref.at[at - low], held_ref.at[slot, k], held_sem.at[slot]
                    ).start()

    for chunk in range(SLOTS - 1):

        @pl.when(chunk < chunks)
        def _():
            fetch(jnp.int32(chunk))

    done = 0
    for piece in flux:
        flux_ref[done : done + piece.shape[0]] = piece[...]
        done += piece.shape[0]
    if has_base:
        sum_ref[...] = base_ref[...]
    else:
        sum_ref[...] = jnp.zeros_like(sum_ref)

    @pl.loop(0, chunks)
    def _(chunk):
        slot = lax.rem(chunk, SLOTS)
        pltpu.make_async_copy(
            own_ref.at[pl.ds(0, CHUNK)], held_ref.at[slot], held_sem.at[slot]
        ).wait()

        @pl.when(chunk + SLOTS - 1 < chunks)
        def _():
            fetch(chunk + SLOTS - 1)

        products, rows = [], []
        for k in range(CHUNK):
            at = start + chunk * CHUNK + k
            valid = jnp.where(at < stop, 1.0, 0.0)
            at = jnp.minimum(at, stop - 1)
            values = flux_ref[places_ref[SPANS + 2 * total + at]] * valid
            high = values.astype(jnp.bfloat16)
            low = (values - high.astype(jnp.float32)).astype(jnp.bfloat16)
            left = jnp.concatenate([high, low], axis=0)
            tile = held_ref[slot, k]
            high = tile.astype(jnp.bfloat16)
            low = (tile - high.astype(jnp.float32)).astype(jnp.bfloat16)
            both = lax.dot_general(
                jnp.concatenate([left, left], axis=1),
                jnp.concatenate([high, low], axis=1),
                (((1,), (1,)), ((), ())),
                preferred_element_type=jnp.float32,
            )
            temps = values.shape[0]
            products.append(both[:temps] + both[temps:])
            rows.append(places_ref[SPANS + total + at] - skip)
        for row, product in zip(rows, products):
            sum_ref[row] += product

    done = 0
    for out in outs:
        out[...] = sum_ref[done : done + out.shape[0]]
        done += out.shape[0]


def apply_tiles(span, skip, places, tiles, flux, sizes, share, base=None):
    length, size, _ = tiles[0].shape
    temps = flux[0].shape[1]
    rows = sum(sizes)
    inside = pl.BlockSpec(memory_space=pltpu.VMEM)
    given = [*flux] + ([] if base is None else [base])
    return pl.pallas_call(
        functools.partial(apply_kernel, span, skip, len(flux), base is not None),
        out_shape=[jax.ShapeDtypeStruct((n, temps, size), jnp.float32) for n in sizes],
        grid_spec=pltpu.PrefetchScalarGridSpec(
            num_scalar_prefetch=1,
            grid=(),
            in_specs=[pl.BlockSpec(memory_space=pltpu.HBM)] * 2 + [inside] * len(given),
            out_specs=[inside] * len(sizes),
            scratch_shapes=[
                pltpu.VMEM((sum(piece.shape[0] for piece in flux), temps, size), jnp.float32),
                pltpu.VMEM((rows, temps, size), jnp.float32),
                pltpu.VMEM((SLOTS, CHUNK, size, size), jnp.float32),
                pltpu.SemaphoreType.DMA((SLOTS,)),
            ],
        ),
        compiler_params=pltpu.CompilerParams(vmem_limit_bytes=VMEM),
        cost_estimate=pl.CostEstimate(
            flops=int(share * 2 * length * size * size * temps * 8),
            bytes_accessed=int(share * 2 * length * size * size * 4) + 8 * rows * temps * size,
            transcendentals=0,
        ),
    )(places, *tiles, *given)


def shards(
    tile_values, tile_owner, tile_row, tile_col, tile_count, relaxation, driving, heat_weight
):
    n_cols = lax.axis_size("x") * CORES
    chips = lax.axis_size(CHIPS)
    length, size, _ = tile_values.shape
    modes, columns = driving.shape
    per = modes // size
    chip_tiles = CORES * per
    num = chips * chip_tiles
    half = columns // CORES
    core = lax.axis_index("core")
    cores = ("core", 1)

    edges = [chip_tiles * k // len(NEAR) for k in range(len(NEAR) + 1)]

    def place(tile):
        chip, inside = tile // chip_tiles, tile % chip_tiles
        away, width = {}, 1
        for axis in reversed(CHIPS):
            n = lax.axis_size(axis)
            away[axis] = ((chip // width) % n) ^ lax.axis_index(axis)
            width *= n
        side, out = jnp.zeros_like(tile), jnp.zeros_like(tile)
        for part in range(len(NEAR)):
            low, high = edges[part], edges[part + 1]
            (first, _), *steps = near_steps(part)
            slot = jnp.zeros_like(tile)
            for axis, distance in steps + far_steps():
                slot = 2 * slot + (away[axis] // distance) % 2
            slot = chips // 2 * low + slot * (high - low) + inside - low
            out = jnp.where(inside >= low, slot, out)
            side = jnp.where(inside >= low, away[first] % 2, side)
        return side, out

    owners = tile_owner[:, 0]
    row_side, row = place((owners // n_cols) * (n_cols * per) + tile_row)
    col_side, col = place(((tile_col // per) * n_cols + owners % n_cols) * per + tile_col % per)
    used = jnp.arange(length, dtype=jnp.int32) < tile_count[0]
    kind = jnp.where(used, jnp.where(col_side == 0, 0, 2 - row_side), 3)
    row = jnp.where(row_side == 1, row, row + num // 2)
    code = (kind * num + row) * num + col
    other_code = swap(code, cores)
    code = jnp.concatenate([code, other_code])
    kind = code // (num * num)
    slots = jnp.arange(CORES * length, dtype=jnp.int32)
    key = kind * (CORES * length) + slots
    rank = jnp.sum((key[None, :] < key[:, None]).astype(jnp.int32), axis=1)
    ends = jnp.sum((kind[None, :] < jnp.arange(SPANS, dtype=jnp.int32)[:, None]).astype(jnp.int32), axis=1)
    sorts = rank[None, :] == slots[:, None]
    order = jnp.sum(jnp.where(sorts, slots[None, :], 0), axis=1)
    code = jnp.sum(jnp.where(sorts, code[None, :] % (num * num), 0), axis=1)
    places = jnp.concatenate([ends, order, code // num, code % num])

    def by_core(own, other):
        return jnp.concatenate(
            [jnp.where(core == 0, own, other), jnp.where(core == 0, other, own)], axis=0
        )

    drive = jnp.transpose(driving.reshape(per, size, columns), (0, 2, 1))
    relax = relaxation.reshape(per, 1, size)
    heat = heat_weight.reshape(per, 1, size)
    low, high = drive[:, :half], drive[:, half:]
    mine = jnp.where(core == 0, low, high)
    theirs = jnp.where(core == 0, high, low)
    packed = [theirs, jnp.broadcast_to(relax, (per, 8, size)), jnp.broadcast_to(heat, (per, 8, size))]
    got = swap(jnp.concatenate(packed, axis=1), cores)
    tile_values = after(tile_values, got, other_code)
    other_values = swap(tile_values, cores)
    drive_half = by_core(mine, got[:, :half])
    relax_both = by_core(relax, got[:, half : half + 1])
    heat_both = by_core(heat, got[:, half + 8 : half + 9])

    drives = gather_far(drive_half)
    small = gather_far(jnp.concatenate([relax_both, heat_both * relax_both], axis=1))
    relaxes, heats = [s[:, :1] for s in small], [s[:, 1:] for s in small]
    drives[-1], other_values = lax.optimization_barrier((drives[-1], other_values))
    fluxes = [r * d for r, d in zip(relaxes, drives)]
    tiles = (tile_values, other_values)
    sizes = [chips // 2 * (high - low) for low, high in zip(edges[:-1], edges[1:])]
    for sweep in range(ITERS):
        pieces = gather_near(fluxes, edges)
        near, far = [p for p, _ in pieces], [p for _, p in pieces]
        base = apply_tiles(0, 0, places, tiles, near, [num // 2, num // 2], 0.5)
        sends = apply_tiles(1, 0, places, tiles, far, sizes, 0.25, base[0])
        keeps = apply_tiles(2, num // 2, places, tiles, far, sizes, 0.25, base[1])
        blocks = reduce_near(keeps, sends)
        if sweep < ITERS - 1:
            fluxes = [r * (d + s) for r, d, s in zip(relaxes, drives, sum_far(blocks))]
    weighted = sum(
        [jnp.sum(w * b, axis=(0, 2)) for w, b in zip(heats, blocks)],
        jnp.sum(heats[0] * drive_half, axis=(0, 2)),
    )
    totals = jnp.concatenate([weighted, jnp.sum(heat).reshape(1)])
    totals = jnp.pad(totals[None], ((0, 0), (0, size - half - 1)))
    *blocks, totals = lax.optimization_barrier((*blocks, totals))
    totals = lax.all_to_all(
        jnp.broadcast_to(totals, (chips * CORES, size)), ALL, split_axis=0, concat_axis=0, tiled=True
    )
    totals = jnp.sum(totals.reshape(chips, CORES, size), axis=0)
    conductivity = totals[:, :half].reshape(columns) / jnp.sum(totals[:, half])
    flux = relax_both * (drive_half + reduce_far(blocks))
    first, second = flux[:per], flux[per:]
    mine = jnp.where(core == 0, first, second)
    got = swap(jnp.where(core == 0, second, first), cores)
    both = jnp.concatenate(
        [jnp.where(core == 0, mine, got), jnp.where(core == 0, got, mine)], axis=1
    )
    mode_flux = jnp.transpose(both, (0, 2, 1)).reshape(modes, columns)
    return (mode_flux, conductivity)


def solution(mesh):
    n_rows, n_cols = mesh.shape["row"], mesh.shape["col"]
    planes = depth_of(n_rows)
    chips = Mesh(mesh.devices.reshape(planes, n_rows // planes, n_cols // CORES, CORES), ALL)
    placed = (
        P(ALL, None, None),
        P(ALL, None),
        P(ALL),
        P(ALL),
        P(ALL),
        P(ALL),
        P(ALL, None),
        P(ALL),
    )
    return jax.shard_map(
        shards,
        mesh=chips,
        in_specs=placed,
        out_specs=(P(ALL, None), P()),
        check_vma=False,
    )
```
